128 devices in a mesh: group: 8 (over y, x_lo), tp: 16 (over x_hi, z, core).
Axes of the slice: x: 4 (x_hi: 2, x_lo: 2; x = x_hi * 2 + x_lo), y: 4, z: 4, core: 2. Of those that a mesh axis runs over, the one named last changes fastest.
Arguments:
- tokens: bfloat16 [8192, 8192], P('group', 'tp'), may hold values from -6 to 6
- norm_gain: bfloat16 [1, 8192], P(None, 'tp'), may hold values from 0.5 to 1.5
- query_weight: bfloat16 [8192, 8192], P(None, 'tp'), may hold values from -0.0625 to 0.0625
- kv_weight: bfloat16 [8192, 2048], P(None, 'tp'), may hold values from -0.0625 to 0.0625
- out_weight: bfloat16 [8192, 8192], P('tp'), may hold values from -0.0625 to 0.0625
- prefix_cache: bfloat16 [8192, 2048], P('group', 'tp'), may hold values from -456 to 456
- prompt_len: int32 [8], P('group'), may hold values from 512 to 1024, as said below
- page_owner: int32 [2048, 1], P('group'), may hold values from 0 to 127; in each aligned block of 256 rows (0 to 255, 256 to 511, ...) at most 3 rows name the same one
- page_seq: int32 [2048], P('group'), may hold values from 0 to 7
- dec_queries: bfloat16 [64, 8192], P('group'), may hold values from -6 to 6
- dec_cache: bfloat16 [64, 2048, 2048], P('group', 'tp'), may hold values from -456 to 456
- dec_len: int32 [64], P('group'), may hold values from 1 to 2048, as said below
Outputs:
- hidden_out: bfloat16 [8192, 8192], P('group', 'tp')
- dec_out: bfloat16 [64, 8192], P('group')
The draws below stay inside these ranges and needn't reach their ends.
Inputs may be any that keep to these rules, and one draw needn't show every extreme that they name: `page_owner`: in the 256 rows of one group no owner is named more than 3 times. `prompt_len`: some group's block is fully live. `dec_len`: some decode sequence uses every position.
All inputs are finite; a program needn't handle non-finite values.
Results may differ from the reference program's by a relative error of at most 0.011.
Values may be sent and summed in bfloat16 or wider, within the bound.
A program may use at most 192 MiB of HBM per device.

```python
import math
import jax
import jax.numpy as jnp
import numpy as np
from jax import lax

D = 8192
HEADS = 64
KVH = 8
HD = 128
SPAN = 1024
PRE = 1024
PAGE = 4
DSEQ = 8
CTX_DEV = 128
PAGES = 256
CAP = 3
TOKENS = 8192
PREFIX_ROWS = 8192
PAGE_ROWS = 2048
DROWS = 64
CTX_ALL = 2048
N_GROUP = 8
N_TP = 16
DEVICES = 128


def draw_prefix_cache(key, part):
    key = jax.random.fold_in(key, 31)
    rows = jnp.clip(jax.random.normal(key, (PREFIX_ROWS, KVH, 2, HD), jnp.float32), -6.0, 6.0)
    return rows.reshape(PREFIX_ROWS, 2 * KVH * HD).astype(jnp.bfloat16)


def draw_dec_cache(key, part):
    key = jax.random.fold_in(key, 37)
    rows = jnp.clip(jax.random.normal(key, (DROWS * CTX_ALL, KVH, 2, HD), jnp.float32), -6.0, 6.0)
    return rows.reshape(DROWS, CTX_ALL, 2 * KVH * HD).astype(jnp.bfloat16)


def draw_prompt_len(key, part):
    key = jax.random.fold_in(key, 11)
    lengths = jax.random.randint(key, (N_GROUP,), SPAN // 2, SPAN + 1)
    chosen = jax.random.randint(jax.random.fold_in(key, 1), (), 0, N_GROUP)
    lengths = lengths.at[chosen].set(SPAN)
    lengths = lengths.at[(chosen + 1) % N_GROUP].set(SPAN // 2)
    return lengths.astype(jnp.int32)


def draw_dec_len(key, part):
    key = jax.random.fold_in(key, 23)
    lengths = jax.random.randint(key, (DROWS,), 1, CTX_ALL + 1)
    chosen = jax.random.randint(jax.random.fold_in(key, 1), (), 0, DROWS)
    return lengths.at[chosen].set(CTX_ALL).astype(jnp.int32)


def plant(array, own_key, low, high):
    index_at = [jax.random.randint(jax.random.fold_in(own_key, axis), (), 0, length) for axis, length in enumerate(array.shape)]
    longest = array.shape.index(max(array.shape))
    next_to = index_at[:longest] + [(index_at[longest] + 1) % array.shape[longest]] + index_at[longest + 1:]
    return array.at[tuple(index_at)].set(low).at[tuple(next_to)].set(high)


def levels(stream_key, extent, split, least, high):
    def one(dim, parts):
        steps = jax.random.uniform(jax.random.fold_in(jax.random.fold_in(stream_key, 6), dim), (parts,), jnp.float32, least / len(split), high / len(split))
        return jnp.repeat(jnp.exp(steps), extent[dim] // parts).reshape((-1,) + (1,) * (len(extent) - dim - 1))

    level = one(*split[0])
    for cut in split[1:]:
        level = level * one(*cut)
    return level


def routed_block(rng, own, number, rows, count, top, most, lean):
    ranking = jax.random.permutation(rng, count)
    heavy_load, ordinary = shares(count, rows * top, most, lean, True), shares(count, rows * top, most, lean, False)
    places = jnp.arange(count)

    def named(tallies, rotation):
        used = int((tallies > 0).sum())
        fixed = max(1, used // 4)
        moved = fixed + (places - fixed + rotation * (used - fixed)) % max(1, count - fixed)
        return jnp.zeros((count,), jnp.int32).at[ranking[jnp.where(places < fixed, places, moved)]].set(jnp.asarray(tallies, jnp.int32))

    tallies = jnp.where(number % 4 == 0, named(heavy_load, number // 4), named(ordinary, number - number // 4 - 1))
    mixed = jax.random.permutation(jax.random.fold_in(own, 3), count)
    donor, taker = mixed[0:count // 2 * 2:2], mixed[1:count // 2 * 2:2]
    room = jnp.minimum(tallies[donor] - 1, most - tallies[taker]) // 2
    room = jnp.where((donor == ranking[0]) | (taker == ranking[0]) | (tallies[taker] == 0), 0, jnp.maximum(room, 0))
    moved = jax.random.randint(jax.random.fold_in(own, 4), (count // 2,), 0, 1 << 20) % (room + 1)
    tallies = tallies.at[donor].add(-moved).at[taker].add(moved)
    members = jnp.searchsorted(jnp.cumsum(tallies), jnp.arange(rows * top), side="right").astype(jnp.int32)
    table = members.reshape(top, rows).T
    table = table[jax.random.permutation(jax.random.fold_in(own, 1), rows)]
    rotation = jax.random.randint(jax.random.fold_in(own, 2), (rows, 1), 0, top)
    return jnp.take_along_axis(table, (jnp.arange(top)[None, :] + rotation) % top, axis=1)


def shares(number_of, total, bound, slope, full):
    loads = [(1 << 20) // math.isqrt(standing ** slope) + 1 for standing in range(1, number_of + 1)]
    largest = bound if full else min(bound, max(-(-total // number_of), total * loads[0] // sum(loads)))
    least = 1 if total - largest >= number_of - 1 else 0
    given, rest = [largest] + [least] * (number_of - 1), total - largest - least * (number_of - 1)
    while rest > 0:
        free = [i for i in range(1, number_of) if given[i] < largest] or [i for i in range(1, number_of) if given[i] < bound]
        mass, remaining = sum([loads[i] for i in free]), rest
        for i in free:
            addition = min(bound - given[i], max(1, remaining * loads[i] // mass), rest)
            given[i] = given[i] + addition
            rest = rest - addition
    return np.array(given)


def scatter_about(rng, shape, scale, bound, shards=(), kind=jnp.bfloat16):
    factor_of = levels(rng, shape, shards, -0.22, 0.18) if shards else 1.0
    array = jax.random.normal(rng, shape, jnp.float32) * scale * factor_of
    return jnp.minimum(jnp.maximum(array, -bound), bound).astype(kind)


def setup_inputs(seed: int = 0) -> dict:
    key_of = jax.random.split(jax.random.key(seed), 13)
    tokens = scatter_about(key_of[0], (TOKENS, D), 1.0, 6.0, ((0, 8), (1, 16)))
    norm_gain = jnp.clip(1.0 + 0.1 * jax.random.normal(key_of[1], (1, D), jnp.float32), 0.5, 1.5).astype(jnp.bfloat16)
    query_weight = scatter_about(key_of[2], (D, HEADS * HD), D ** -0.5, 0.0625, ((1, 16),))
    kv_weight = scatter_about(key_of[3], (D, 2 * KVH * HD), D ** -0.5, 0.0625, ((1, 16),))
    out_weight = scatter_about(key_of[4], (HEADS * HD, D), (HEADS * HD) ** -0.5, 0.0625, ((0, 16),))
    prefix_cache = draw_prefix_cache(jax.random.fold_in(key_of[12], 71), 0)
    prompt_len = draw_prompt_len(jax.random.fold_in(key_of[12], 71), 0)
    page_owner_keys = jax.random.split(jax.random.fold_in(key_of[7], 1), PAGE_ROWS // PAGES)
    page_owner_turns = jax.random.permutation(jax.random.fold_in(key_of[7], 3), PAGE_ROWS // PAGES)
    page_owner = jax.vmap(lambda own, number: routed_block(jax.random.fold_in(key_of[7], 2), own, number, PAGES, DEVICES, 1, CAP, 2))(page_owner_keys, page_owner_turns).reshape((PAGE_ROWS, 1))
    page_seq = plant(jax.random.randint(key_of[8], (PAGE_ROWS,), 0, DSEQ), jax.random.fold_in(key_of[8], 1), 0, DSEQ - 1).astype(jnp.int32)
    dec_queries = scatter_about(key_of[9], (DROWS, HEADS * HD), 1.0, 6.0, ((0, 8),))
    dec_cache = draw_dec_cache(jax.random.fold_in(key_of[12], 71), 0)
    dec_len = draw_dec_len(jax.random.fold_in(key_of[12], 71), 0)
    return dict(tokens=tokens, norm_gain=norm_gain, query_weight=query_weight, kv_weight=kv_weight, out_weight=out_weight, prefix_cache=prefix_cache, prompt_len=prompt_len, page_owner=page_owner, page_seq=page_seq, dec_queries=dec_queries, dec_cache=dec_cache, dec_len=dec_len)


EPSILON = 1e-05
NEG_BIG = -1e+30

def rounded(value):
    return lax.optimization_barrier(value.astype(jnp.bfloat16)).astype(jnp.float32)

def normalize(rows, gain):
    wide = rows.astype(jnp.float32)
    power = lax.optimization_barrier(jnp.sum(wide * wide, axis=-1, keepdims=True)) / wide.shape[-1]
    return (wide * lax.rsqrt(power + EPSILON) * gain.astype(jnp.float32)).astype(jnp.bfloat16)

def block_attention(queries, key_rows, value_rows):
    count = queries.shape[0]
    total = key_rows.shape[0]
    factor = 1.0 / math.sqrt(queries.shape[-1])
    scores = jnp.einsum('cgd,jd->gcj', queries.astype(jnp.float32), key_rows.astype(jnp.float32)) * factor
    row_index = lax.broadcasted_iota(jnp.int32, (count, total), 0)
    column_index = lax.broadcasted_iota(jnp.int32, (count, total), 1)
    allowed = column_index <= row_index + (total - count)
    scores = jnp.where(allowed[None], scores, NEG_BIG)
    top_score = lax.optimization_barrier(jnp.max(scores, axis=-1, keepdims=True))
    expo = jnp.exp(scores - top_score)
    weights = rounded(expo / lax.optimization_barrier(jnp.sum(expo, axis=-1, keepdims=True)))
    return jnp.einsum('gcj,jd->cgd', weights, value_rows.astype(jnp.float32)).astype(jnp.bfloat16)

def shard_partial(queries, old_rows, old_valid, new_rows, new_valid):
    seqs = queries.shape[0]
    head_dim = queries.shape[-1] // HEADS
    factor = 1.0 / math.sqrt(head_dim)
    grouped = queries.reshape(seqs, KVH, HEADS // KVH, head_dim).astype(jnp.float32)
    old_split = old_rows.reshape(seqs, old_rows.shape[1], KVH, 2, head_dim).astype(jnp.float32)
    new_split = new_rows.reshape(new_rows.shape[0], KVH, 2, head_dim).astype(jnp.float32)
    old_scores = jnp.einsum('skgd,sjkd->skgj', grouped, old_split[:, :, :, 0]) * factor
    new_scores = jnp.einsum('skgd,jkd->skgj', grouped, new_split[:, :, 0]) * factor
    old_mask = old_valid[:, None, None, :]
    new_mask = new_valid[:, None, None, :]
    old_scores = jnp.where(old_mask, old_scores, NEG_BIG)
    new_scores = jnp.where(new_mask, new_scores, NEG_BIG)
    top_score = jnp.maximum(lax.optimization_barrier(jnp.max(old_scores, axis=-1)), lax.optimization_barrier(jnp.max(new_scores, axis=-1)))
    old_expo = jnp.where(old_mask, jnp.exp(old_scores - top_score[..., None]), 0.0)
    new_expo = jnp.where(new_mask, jnp.exp(new_scores - top_score[..., None]), 0.0)
    total = lax.optimization_barrier(jnp.sum(old_expo, axis=-1)) + lax.optimization_barrier(jnp.sum(new_expo, axis=-1))
    accum = jnp.einsum('skgj,sjkd->skgd', rounded(old_expo), old_split[:, :, :, 1])
    accum = accum + jnp.einsum('skgj,jkd->skgd', rounded(new_expo), new_split[:, :, 1])
    return (top_score, total, accum)

def reference(tokens, norm_gain, query_weight, kv_weight, out_weight, prefix_cache, prompt_len, page_owner, page_seq, dec_queries, dec_cache, dec_len):
    width_kv = 2 * KVH * HD
    share = HEADS * HD // N_TP
    out_wide = out_weight.astype(jnp.float32).reshape(N_TP, share, D)

    def prefill_group(inputs):
        rows, prefix = inputs
        normed = normalize(rows, norm_gain[0])
        queries = jnp.dot(normed, query_weight, preferred_element_type=jnp.float32).astype(jnp.bfloat16)
        kv_new = jnp.dot(normed, kv_weight, preferred_element_type=jnp.float32).astype(jnp.bfloat16)
        kv_rows = jnp.concatenate([prefix, kv_new], 0).reshape(-1, KVH, 2, HD)
        grouped = queries.reshape(SPAN, KVH, HEADS // KVH, HD)
        attended = jax.vmap(block_attention, in_axes=(1, 1, 1), out_axes=1)(grouped, kv_rows[:, :, 0], kv_rows[:, :, 1])
        attended = attended.reshape(SPAN, N_TP, share).astype(jnp.float32)
        terms = jnp.einsum('ctw,twd->tcd', attended, out_wide)
        projected = lax.optimization_barrier(jnp.sum(rounded(terms), axis=0))
        hidden = (rows.astype(jnp.float32) + projected).astype(jnp.bfloat16)
        return (hidden, kv_new)
    hidden_all, kv_all = lax.map(prefill_group, (tokens.reshape(N_GROUP, SPAN, D), prefix_cache.reshape(N_GROUP, PRE, width_kv)))
    hidden_out = hidden_all.reshape(N_GROUP * SPAN, D)
    devices = N_GROUP * N_TP
    pages = SPAN // PAGE
    owner = page_owner.reshape(N_GROUP, pages)
    onehot = (owner[:, :, None] == jnp.arange(devices, dtype=jnp.int32)[None, None, :]).astype(jnp.int32)
    slot = lax.optimization_barrier(jnp.sum((jnp.cumsum(onehot, axis=1) - onehot) * onehot, axis=-1)).astype(jnp.int32)
    starts = jnp.arange(pages, dtype=jnp.int32) * PAGE
    live = starts[None, :] < prompt_len[:, None]
    target = jnp.where(live, owner, devices).astype(jnp.int32)
    source = jnp.broadcast_to(jnp.arange(N_GROUP, dtype=jnp.int32)[:, None], (N_GROUP, pages))
    region = jnp.zeros((devices, N_GROUP, CAP, PAGE, width_kv), jnp.bfloat16)
    region = region.at[target, source, slot].set(kv_all.reshape(N_GROUP, pages, PAGE, width_kv), mode='drop')
    seq_table = jnp.full((devices, N_GROUP, CAP), -1, jnp.int32).at[target, source, slot].set(page_seq.reshape(N_GROUP, pages), mode='drop')
    count_table = jnp.zeros((devices, N_GROUP, CAP), jnp.int32).at[target, source, slot].set(jnp.minimum(PAGE, prompt_len[:, None] - starts[None, :]).astype(jnp.int32), mode='drop')
    fresh = N_GROUP * CAP * PAGE
    position = jnp.arange(PAGE, dtype=jnp.int32)
    new_seq = jnp.broadcast_to(seq_table[..., None], (devices, N_GROUP, CAP, PAGE)).reshape(N_GROUP, N_TP, fresh)
    new_live = (position[None, None, None, :] < count_table[..., None]).reshape(N_GROUP, N_TP, fresh)
    region = region.reshape(N_GROUP, N_TP, fresh, width_kv)
    cache = dec_cache.reshape(N_GROUP, DSEQ, N_TP, CTX_DEV, width_kv).transpose(0, 2, 1, 3, 4)
    lengths = dec_len.reshape(N_GROUP, DSEQ)
    seq_ids = jnp.arange(DSEQ, dtype=jnp.int32)

    def decode_group(inputs):
        queries, cache_group, length_group, region_group, seq_group, live_group = inputs

        def one_shard(shard, old_rows, new_rows, new_seqs, new_lives):
            old_pos = shard * CTX_DEV + jnp.arange(CTX_DEV, dtype=jnp.int32)
            old_valid = old_pos[None, :] < length_group[:, None]
            new_valid = (new_seqs[None, :] == seq_ids[:, None]) & new_lives[None, :]
            return shard_partial(queries, old_rows, old_valid, new_rows, new_valid)
        tops, totals, accums = jax.vmap(one_shard)(jnp.arange(N_TP, dtype=jnp.int32), cache_group, region_group, seq_group, live_group)
        best = lax.optimization_barrier(jnp.max(tops, axis=0))
        factor = jnp.exp(tops - best[None])
        total = lax.optimization_barrier(jnp.sum(factor * totals, axis=0))
        accum = lax.optimization_barrier(jnp.sum(factor[..., None] * accums, axis=0))
        return (accum / total[..., None]).reshape(DSEQ, HEADS * HD).astype(jnp.bfloat16)
    dec_all = lax.map(decode_group, (dec_queries.reshape(N_GROUP, DSEQ, HEADS * HD), cache, lengths, region, new_seq, new_live))
    dec_out = dec_all.reshape(N_GROUP * DSEQ, HEADS * HD)
    return (hidden_out, dec_out)
```

```python
import math

import jax
import jax.numpy as jnp
from jax import lax
from jax.experimental import pallas as pl
from jax.experimental.pallas import tpu as pltpu
from jax.sharding import PartitionSpec as P

HEADS = 64
KVH = 8
HD = 128
PAGE = 4


EPSILON = 1e-05
NEG_BIG = -1e30


MESH = pl.DeviceIdType.MESH
BF = jnp.bfloat16
F32 = jnp.float32
MIB = 1024 * 1024
SIDES = 2
RING = 4


def here():
    t = lax.axis_index("tp")
    return t // (RING * 2), lax.rem(t // 2, RING), lax.rem(t, 2)


def shard_at(side, ring, core, far, step, other):
    s = lax.rem(side + far, SIDES)
    r = lax.rem(ring + step, RING)
    c = lax.rem(core + other, 2)
    return (s * RING + r) * 2 + c


def push(src, dst, send_sem, recv_sem, to):
    copy = pltpu.make_async_remote_copy(
        src_ref=src,
        dst_ref=dst,
        send_sem=send_sem,
        recv_sem=recv_sem,
        device_id={"tp": to},
        device_id_type=MESH,
    )
    copy.start()
    return copy


def landed(ref, recv_sem, to):
    pltpu.make_async_remote_copy(
        src_ref=ref,
        dst_ref=ref,
        send_sem=recv_sem,
        recv_sem=recv_sem,
        device_id={"tp": to},
        device_id_type=MESH,
    ).wait_recv()


def greet(peers):
    barrier = pltpu.get_barrier_semaphore()
    for peer in peers:
        pl.semaphore_signal(barrier, inc=1, device_id={"tp": peer}, device_id_type=MESH)
    pl.semaphore_wait(barrier, len(peers))


GATHER_CHUNKS = 4
GAIN_ROWS = 16


def gather_kernel(
    tok,
    gain,
    prefix,
    qw_hbm,
    kw_hbm,
    q_out,
    kv_out,
    xall,
    qw,
    kw,
    acc_q,
    acc_k,
    power,
    w_sem,
    recv_sem,
    sib_sem,
    x_send,
    up_send,
    down_send,
    sib_send,
    kv_send,
    kv_recv,
):
    side, ring, core = here()
    rows_all, width = tok.shape
    chunk = rows_all // GATHER_CHUNKS

    def at(far, step, other=0):
        return shard_at(side, ring, core, far, step, other)

    me, across, sib = at(0, 0), at(1, 0), at(0, 0, 1)
    up, down = at(0, 1), at(0, 3)

    load_q = pltpu.make_async_copy(qw_hbm, qw, w_sem.at[0])
    load_k = pltpu.make_async_copy(kw_hbm, kw, w_sem.at[1])
    load_q.start()
    load_k.start()
    xall[me, pl.ds(0, GAIN_ROWS), :] = jnp.broadcast_to(gain[...], (GAIN_ROWS, width))
    xall[me, pl.ds(GAIN_ROWS, rows_all), :] = tok[...]
    prefix_rows = prefix.shape[0]
    kv_out[core, pl.ds(0, prefix_rows), :] = prefix[...]
    acc_q[...] = jnp.zeros_like(acc_q)
    acc_k[...] = jnp.zeros_like(acc_k)
    power[...] = jnp.zeros_like(power)
    greet((across, up, down, sib))

    sends = []

    def span(i, half=None):
        low = 0 if i == 0 else GAIN_ROWS + i * chunk
        high = GAIN_ROWS + (i + 1) * chunk
        middle = high - chunk // 2
        if half == 0:
            high = middle
        if half == 1:
            low = middle
        return pl.ds(low, high - low)

    def send(slot, rows, send_sem, there_sem, to):
        ref = xall.at[slot, rows, :]
        sends.append(push(ref, ref, send_sem, there_sem, to))

    def to_sibling(far, step, i):
        kind = far * 4 + step
        send(at(far, step), span(i), sib_send.at[kind, i], sib_sem.at[kind, i], sib)

    def multiply(slot, i):
        rows = pl.ds(i * chunk, chunk)
        wide = xall[slot, pl.ds(GAIN_ROWS + i * chunk, chunk), :].astype(F32)
        weight = xall[slot, pl.ds(0, 1), :].astype(F32)
        square = wide * wide
        part = square[:, 0:HD]
        for k in range(1, width // HD):
            part = part + square[:, k * HD : (k + 1) * HD]
        power[rows, :] += part
        scaled = (wide * weight).astype(BF)
        depth = pl.ds(pl.multiple_of(slot * width, width), width)
        acc_q[rows, :] += jnp.dot(scaled, qw[depth, :], preferred_element_type=F32)
        acc_k[rows, :] += jnp.dot(scaled, kw[depth, :], preferred_element_type=F32)

    def from_sibling(far, step, i):
        kind = far * 4 + step
        slot = at(far, step, 1)
        landed(xall.at[slot, span(i), :], sib_sem.at[kind, i], sib)
        multiply(slot, i)

    def got(far, step, i):
        kind = far * 4 + step
        slot = at(far, step)
        if step == 2:
            landed(xall.at[slot, span(i, 0), :], recv_sem.at[kind, i], down)
            landed(xall.at[slot, span(i, 1), :], recv_sem.at[8 + far, i], up)
        else:
            landed(xall.at[slot, span(i), :], recv_sem.at[kind, i], up)

    for i in range(GATHER_CHUNKS):
        send(me, span(i), x_send.at[i], recv_sem.at[4, i], across)
        send(me, span(i), up_send.at[0, i], recv_sem.at[3, i], up)
        send(me, span(i), down_send.at[0, i], recv_sem.at[1, i], down)
        to_sibling(0, 0, i)
    early = kv_out.at[core, pl.ds(0, prefix_rows), :]
    sends.append(push(early, early, kv_send.at[0], kv_recv.at[0], sib))
    load_q.wait()
    load_k.wait()

    def event(name, i):
        if name == "O":
            multiply(me, i)
            return [(0, 0, i)]
        if name == "X":
            got(1, 0, i)
            send(across, span(i), up_send.at[1, i], recv_sem.at[7, i], up)
            send(across, span(i), down_send.at[1, i], recv_sem.at[5, i], down)
            to_sibling(1, 0, i)
            multiply(across, i)
            return [(1, 0, i)]
        far = 0 if name in ("Z", "F") else 1
        if name in ("Z", "P"):
            got(far, 3, i)
            send(at(far, 3), span(i, 0), up_send.at[2 + far, i], recv_sem.at[4 * far + 2, i], up)
            got(far, 1, i)
            send(at(far, 1), span(i, 1), down_send.at[2 + far, i], recv_sem.at[8 + far, i], down)
            to_sibling(far, 3, i)
            to_sibling(far, 1, i)
            multiply(at(far, 3), i)
            multiply(at(far, 1), i)
            return [(far, 3, i), (far, 1, i)]
        got(far, 2, i)
        to_sibling(far, 2, i)
        multiply(at(far, 2), i)
        return [(far, 2, i)]

    order = (
        ("O", 0), ("O", 1), ("O", 2), ("O", 3), ("Z", 0), ("Z", 1), ("X", 0), ("Z", 2),
        ("Z", 3), ("X", 1), ("F", 0), ("F", 1), ("P", 0), ("X", 2), ("F", 2), ("F", 3),
        ("P", 1), ("X", 3), ("P", 2), ("G", 0), ("P", 3), ("G", 1), ("G", 2), ("G", 3),
    )
    late = []
    for name, i in order:
        fresh = event(name, i)
        for item in late:
            from_sibling(*item)
        late = fresh
    for item in late:
        from_sibling(*item)

    for i in range(GATHER_CHUNKS):
        rows = pl.ds(i * chunk, chunk)
        total = jnp.sum(power[rows, :], axis=-1, keepdims=True) / (width * 2 * RING * SIDES)
        factor = lax.rsqrt(total + EPSILON)
        new = pl.ds(prefix_rows + i * chunk, chunk)
        kv_out[core, new, :] = (acc_k[rows, :] * factor).astype(BF)
        ref = kv_out.at[core, new, :]
        sends.append(push(ref, ref, kv_send.at[1 + i], kv_recv.at[1 + i], sib))
        q_out[rows, :] = (acc_q[rows, :] * factor).astype(BF)
    landed(kv_out.at[1 - core, pl.ds(0, prefix_rows), :], kv_recv.at[0], sib)
    for i in range(GATHER_CHUNKS):
        new = pl.ds(prefix_rows + i * chunk, chunk)
        landed(kv_out.at[1 - core, new, :], kv_recv.at[1 + i], sib)
    for copy in sends:
        copy.wait_send()


def gather_multiply(tokens, gain, prefix, query_weight, kv_weight):
    rows, width = tokens.shape
    shards = 2 * RING * SIDES
    kv_rows = prefix.shape[0] + rows
    vmem = pl.BlockSpec(memory_space=pltpu.VMEM)
    dma = pltpu.SemaphoreType.DMA
    n = GATHER_CHUNKS
    return pl.pallas_call(
        gather_kernel,
        out_shape=(
            jax.ShapeDtypeStruct((rows, query_weight.shape[1]), BF),
            jax.ShapeDtypeStruct((2, kv_rows, HD), BF),
        ),
        in_specs=[vmem, vmem, vmem, pl.BlockSpec(memory_space=pl.ANY), pl.BlockSpec(memory_space=pl.ANY)],
        out_specs=(vmem, vmem),
        scratch_shapes=[
            pltpu.VMEM((shards, rows + GAIN_ROWS, width), BF),
            pltpu.VMEM(query_weight.shape, BF),
            pltpu.VMEM(kv_weight.shape, BF),
            pltpu.VMEM((rows, query_weight.shape[1]), F32),
            pltpu.VMEM((rows, HD), F32),
            pltpu.VMEM((rows, HD), F32),
            dma((2,)),
            dma((10, n)),
            dma((8, n)),
            dma((n,)),
            dma((4, n)),
            dma((4, n)),
            dma((8, n)),
            dma((n + 1,)),
            dma((n + 1,)),
        ],
        compiler_params=pltpu.CompilerParams(
            collective_id=1, has_side_effects=True, vmem_limit_bytes=48 * MIB
        ),
        cost_estimate=pl.CostEstimate(
            flops=2 * rows * width * shards * (query_weight.shape[1] + HD),
            bytes_accessed=16 * MIB,
            transcendentals=0,
        ),
        name="gather_multiply",
    )(tokens, gain, prefix, query_weight, kv_weight)


SCATTER_CHUNKS = 8


def attend_kernel(
    tok,
    q,
    kv,
    pages,
    dec_q,
    dec_len,
    wo_hbm,
    cache_hbm,
    out,
    dec_out,
    wo,
    att,
    mine,
    lend,
    borrowed,
    mid,
    near,
    last,
    cache,
    first_stop,
    fresh,
    scores,
    partial,
    shares,
    w_sem,
    lend_send,
    lend_recv,
    mid_send,
    mid_recv,
    near_send,
    near_recv,
    last_send,
    last_recv,
    first_send,
    first_recv,
    fresh_send,
    fresh_recv,
    share_send,
    share_recv,
    done_send,
    done_recv,
):
    side, ring, core = here()
    rows_all, width = tok.shape
    chunk = rows_all // SCATTER_CHUNKS
    half = chunk // 2
    old = kv.shape[1] - rows_all
    n = SCATTER_CHUNKS

    def at(far, step, other=0):
        return shard_at(side, ring, core, far, step, other)

    across, sib, up, down = at(1, 0), at(0, 0, 1), at(0, 1), at(0, 3)
    load = pltpu.make_async_copy(wo_hbm, wo, w_sem.at[0])
    load.start()
    load_cache = pltpu.make_async_copy(cache_hbm, cache, w_sem.at[1])
    load_cache.start()
    shard = lax.axis_index("tp")
    group = lax.axis_index("group")
    shards = 2 * RING * SIDES
    groups = lax.axis_size("group")
    dec_seqs = cache.shape[0]
    barrier = pltpu.get_barrier_semaphore()

    def greet_shard(d, carry):
        pl.semaphore_signal(
            barrier, inc=1, device_id={"tp": lax.rem(shard + d, shards)}, device_id_type=MESH
        )
        return carry

    def greet_group(d, carry):
        pl.semaphore_signal(
            barrier, inc=1, device_id={"group": lax.rem(group + d, groups)}, device_id_type=MESH
        )
        return carry

    lax.fori_loop(1, shards, greet_shard, 0)
    lax.fori_loop(1, groups, greet_group, 0)
    pl.semaphore_wait(barrier, shards + groups - 2)

    def copy_to(src, dst, send_sem, recv_sem, to):
        return pltpu.make_async_remote_copy(
            src_ref=src,
            dst_ref=dst,
            send_sem=send_sem,
            recv_sem=recv_sem,
            device_id=to,
            device_id_type=MESH,
        )

    def first_copy(d):
        to = lax.rem(shard + d, shards)
        return copy_to(
            pages.at[to], first_stop.at[shard], first_send.at[d], first_recv.at[d], {"tp": to}
        )

    def fresh_copy(d):
        to = lax.rem(group + d, groups)
        return copy_to(
            first_stop.at[:, to], fresh.at[group], fresh_send.at[d], fresh_recv.at[d], {"group": to}
        )

    def share_of(shard_to):
        return partial.at[
            pl.ds(lax.rem(shard_to, 2) * 4, 5), pl.ds(pl.multiple_of(shard_to // 2 * 8, 8), 8), :
        ]

    def share_copy(d):
        to = lax.rem(shard + d, shards)
        return copy_to(
            share_of(to), shares.at[shard], share_send.at[d], share_recv.at[d], {"tp": to}
        )

    def result_of(of):
        return dec_out.at[of // 2, pl.ds(pl.multiple_of(lax.rem(of, 2) * 32, 32), 32), :]

    def done_copy(d):
        to = lax.rem(shard + d, shards)
        return copy_to(
            result_of(shard), result_of(shard), done_send.at[d], done_recv.at[d], {"tp": to}
        )

    def each(count, act):
        def body(d, carry):
            act(d)
            return carry

        lax.fori_loop(1, count, body, 0)

    def source(d, count, of):
        return lax.rem(of + count - d, count)

    def dec_begin():
        first_stop[shard] = pages[shard]
        each(shards, lambda d: first_copy(d).start())

    def dec_forward():
        def take(d):
            frm = source(d, shards, shard)
            ref = first_stop.at[frm]
            copy_to(ref, ref, first_send.at[d], first_recv.at[d], {"tp": frm}).wait_recv()

        each(shards, take)
        fresh[group] = first_stop[:, pl.ds(group, 1)].reshape(shards, 16, HD)
        each(groups, lambda d: fresh_copy(d).start())

    def dec_arrive():
        def take(d):
            frm = source(d, groups, group)
            ref = fresh.at[frm]
            copy_to(ref, ref, fresh_send.at[d], fresh_recv.at[d], {"group": frm}).wait_recv()

        each(groups, take)

    scale = math.log2(math.e) / math.sqrt(HD)
    contract = (((1,), (1,)), ((), ()))

    def head_cols(k, part):
        return pl.ds(pl.multiple_of(k * 2 * HD + part * HD, HD), HD)

    def dec_scores(k):
        ctx = cache.shape[1]
        position = lax.broadcasted_iota(jnp.int32, (8, ctx), 1) + shard * ctx
        for seq in range(dec_seqs):
            rows = pl.ds(seq * 8, 8)
            query = dec_q[k, rows, :].astype(BF)
            score = lax.dot_general(
                query, cache[seq, :, head_cols(k, 0)], contract, preferred_element_type=F32
            )
            scores[k, rows, :] = jnp.where(position < dec_len[seq], score * scale, NEG_BIG)

    def dec_settle(k):
        count = dec_seqs * 8
        spots = fresh.shape[0] * 16
        mark = fresh[0, 0].astype(F32)
        for g in range(1, fresh.shape[0]):
            mark = mark + fresh[g, 0].astype(F32)
        mark = mark[12:13, :]
        seq_of = lax.broadcasted_iota(jnp.int32, (count, spots), 0) // 8 + 1
        held = mark == seq_of.astype(F32)
        key = fresh[:, pl.ds(2 * k, 1)].reshape(spots, HD)
        value = fresh[:, pl.ds(2 * k + 1, 1)].reshape(spots, HD)
        new = lax.dot_general(dec_q[k].astype(BF), key, contract, preferred_element_type=F32)
        new = jnp.where(held, new * scale, NEG_BIG)
        old = scores[k]
        top = jnp.maximum(
            jnp.max(new, axis=-1, keepdims=True), jnp.max(old, axis=-1, keepdims=True)
        )
        new = jnp.where(held, jnp.exp2(new - top), 0.0)
        old = jnp.where(old > 0.5 * NEG_BIG, jnp.exp2(old - top), 0.0)
        total = jnp.sum(new, axis=-1, keepdims=True) + jnp.sum(old, axis=-1, keepdims=True)
        accum = jnp.dot(new.astype(BF), value, preferred_element_type=F32)
        place = k + k // 4
        for seq in range(dec_seqs):
            rows = slice(seq * 8, seq * 8 + 8)
            partial[place, pl.ds(seq * 8, 8), :] = accum[rows] + jnp.dot(
                old[rows].astype(BF), cache[seq, :, head_cols(k, 1)], preferred_element_type=F32
            )
        lane = lax.broadcasted_iota(jnp.int32, (count, HD), 1)
        stat = jnp.where(lax.rem(lane, 16) < 8, top, total)
        partial[4] = jnp.where(lane // 16 == k, stat, partial[4])

    def dec_share():
        shares[shard] = partial[
            pl.ds(core * 4, 5), pl.ds(pl.multiple_of(shard // 2 * 8, 8), 8), :
        ]
        each(shards, lambda d: share_copy(d).start())

    def dec_combine():
        def take(d):
            frm = source(d, shards, shard)
            ref = shares.at[frm]
            copy_to(ref, ref, share_send.at[d], share_recv.at[d], {"tp": frm}).wait_recv()

        each(shards, take)
        stat = shares[:, pl.ds(4 - 4 * core, 1)].reshape(shards, 8, HD)
        lane = lax.broadcasted_iota(jnp.int32, (shards, 8, HD), 2)
        parts = []
        for h in range(4):
            here_lane = lane // 16 == core * 4 + h
            low = lax.rem(lane, 16) < 8
            top = jnp.max(jnp.where(here_lane & low, stat, NEG_BIG), axis=-1, keepdims=True)
            total = jnp.max(
                jnp.where(here_lane & jnp.logical_not(low), stat, 0.0), axis=-1, keepdims=True
            )
            factor = jnp.exp2(top - jnp.max(top, axis=0, keepdims=True))
            whole = jnp.sum(factor * total, axis=0)
            accum = jnp.sum(
                factor * shares[:, pl.ds(core + h, 1)].reshape(shards, 8, HD), axis=0
            )
            parts.append(accum / whole)
        for pair in range(2):
            rows = pl.ds(pl.multiple_of(core * 32 + pair * 16, 16), 16)
            both = jnp.concatenate([parts[2 * pair], parts[2 * pair + 1]], axis=0)
            dec_out[shard // 2, rows, :] = both.astype(BF)
        each(shards, lambda d: done_copy(d).start())

    def dec_end():
        def take(d):
            frm = source(d, shards, shard)
            ref = result_of(frm)
            copy_to(ref, ref, done_send.at[d], done_recv.at[d], {"tp": frm}).wait_recv()

        each(shards, take)
        for copy in (first_copy, share_copy, done_copy):
            each(shards, lambda d, copy=copy: copy(d).wait_send())
        each(groups, lambda d: fresh_copy(d).wait_send())

    dec_begin()
    partial[4] = jnp.zeros_like(partial[4])
    load.wait()
    load_cache.wait()

    def rows_of(j):
        return pl.ds(pl.multiple_of(j * chunk, chunk), chunk)

    def half_of(j, k):
        return pl.ds(pl.multiple_of(j * chunk + k * half, half), half)

    def attention(j):
        rows = rows_of(j)
        row = lax.broadcasted_iota(jnp.int32, (chunk, rows_all), 0) + j * chunk
        column = lax.broadcasted_iota(jnp.int32, (chunk, rows_all), 1)
        seen = column <= row
        for h in range(width // HD):
            cols = pl.ds(h * HD, HD)
            query = q[rows, cols]
            first = lax.dot_general(
                query, kv[0, pl.ds(0, old), :], contract, preferred_element_type=F32
            )
            second = lax.dot_general(
                query, kv[0, pl.ds(old, rows_all), :], contract, preferred_element_type=F32
            )
            first = first * scale
            second = jnp.where(seen, second * scale, NEG_BIG)
            top = jnp.maximum(
                jnp.max(first, axis=-1, keepdims=True), jnp.max(second, axis=-1, keepdims=True)
            )
            first = jnp.exp2(first - top)
            second = jnp.exp2(second - top)
            total = jnp.sum(first, axis=-1, keepdims=True) + jnp.sum(second, axis=-1, keepdims=True)
            value = jnp.dot(
                first.astype(BF), kv[1, pl.ds(0, old), :], preferred_element_type=F32
            ) + jnp.dot(
                second.astype(BF), kv[1, pl.ds(old, rows_all), :], preferred_element_type=F32
            )
            att[:, cols] = (value / total).astype(BF)

    def term(far, step, other):
        slot = at(far, step, other)
        cols = pl.ds(pl.multiple_of(slot * width, width), width)
        return jnp.dot(att[...], wo[:, cols], preferred_element_type=F32).astype(BF)

    def add_into(dst, src):
        dst[...] = (dst[...].astype(F32) + src[...].astype(F32)).astype(BF)

    def lend_copy(kind, j):
        rows = rows_of(j)
        return pltpu.make_async_remote_copy(
            src_ref=lend.at[kind, rows, :],
            dst_ref=borrowed.at[kind, rows, :],
            send_sem=lend_send.at[kind, j],
            recv_sem=lend_recv.at[kind, j],
            device_id={"tp": sib},
            device_id_type=MESH,
        )

    def mid_copy(far, way, j):
        rows = half_of(j, way)
        return pltpu.make_async_remote_copy(
            src_ref=mine.at[far * 4 + 2, rows, :],
            dst_ref=mid.at[far, rows, :],
            send_sem=mid_send.at[far * 2 + way, j],
            recv_sem=mid_recv.at[far * 2 + way, j],
            device_id={"tp": down if way else up},
            device_id_type=MESH,
        )

    def near_copy(far, way, k, j):
        rows = half_of(j, k)
        return pltpu.make_async_remote_copy(
            src_ref=mine.at[far * 4 + (3 if way else 1), rows, :],
            dst_ref=near.at[far * 2 + way, rows, :],
            send_sem=near_send.at[far * 4 + way * 2 + k, j],
            recv_sem=near_recv.at[far * 4 + way * 2 + k, j],
            device_id={"tp": down if way else up},
            device_id_type=MESH,
        )

    def last_copy(j):
        rows = rows_of(j)
        return pltpu.make_async_remote_copy(
            src_ref=mine.at[4, rows, :],
            dst_ref=last.at[rows, :],
            send_sem=last_send.at[j],
            recv_sem=last_recv.at[j],
            device_id={"tp": across},
            device_id_type=MESH,
        )

    kinds = ((1, 2), (0, 2), (1, 1), (1, 3), (0, 1), (0, 3), (1, 0), (0, 0))
    lag = 2

    def produce(j):
        attention(j)
        rows = rows_of(j)
        for k in range(len(kinds) + lag):
            if k < len(kinds):
                far, step = kinds[k]
                kind = far * 4 + step
                lend[kind, rows, :] = term(far, step, 1)
                lend_copy(kind, j).start()
                mine[kind, rows, :] = term(far, step, 0)
            if k >= lag:
                far, step = kinds[k - lag]
                kind = far * 4 + step
                lend_copy(kind, j).wait_recv()
                add_into(mine.at[kind, rows, :], borrowed.at[kind, rows, :])
                if step == 2:
                    mid_copy(far, 0, j).start()
                    mid_copy(far, 1, j).start()
                if step == 1:
                    near_copy(far, 0, 1, j).start()
                if step == 3:
                    near_copy(far, 1, 0, j).start()

    def relay(j):
        for far in (1, 0):
            for way in (0, 1):
                mid_copy(far, way, j).wait_recv()
                rows = half_of(j, way)
                add_into(mine.at[far * 4 + (3 if way else 1), rows, :], mid.at[far, rows, :])
                near_copy(far, way, way, j).start()

    def near_wait(far, j):
        for way in (0, 1):
            for k in (0, 1):
                near_copy(far, way, k, j).wait_recv()

    def cross(j):
        near_wait(1, j)
        rows = rows_of(j)
        mine[4, rows, :] = (
            mine[4, rows, :].astype(F32) + near[2, rows, :].astype(F32) + near[3, rows, :].astype(F32)
        ).astype(BF)
        last_copy(j).start()

    def finish(j):
        near_wait(0, j)
        last_copy(j).wait_recv()
        rows = rows_of(j)
        out[rows, :] = (
            tok[rows, :].astype(F32)
            + (
                mine[0, rows, :].astype(F32)
                + near[0, rows, :].astype(F32)
                + near[1, rows, :].astype(F32)
                + last[rows, :].astype(F32)
            )
        ).astype(BF)

    def turn(j, carry):
        @pl.when(j < n)
        def _():
            produce(j)

        @pl.when((j >= 1) & (j < n + 1))
        def _():
            relay(j - 1)

        @pl.when((j >= 2) & (j < n + 2))
        def _():
            cross(j - 2)

        @pl.when(j >= 3)
        def _():
            finish(j - 3)

        @pl.when(j == 1)
        def _():
            dec_forward()

        @pl.when(j < 4)
        def _():
            dec_scores(2 * j)
            dec_scores(2 * j + 1)

        @pl.when(j == 4)
        def _():
            dec_arrive()

        @pl.when((j >= 4) & (j < 8))
        def _():
            dec_settle(2 * j - 8)
            dec_settle(2 * j - 7)

        @pl.when(j == 7)
        def _():
            dec_share()

        @pl.when(j == 8)
        def _():
            dec_combine()

        return carry

    lax.fori_loop(0, n + 3, turn, 0)

    def drain(j, carry):
        for kind in range(8):
            lend_copy(kind, j).wait_send()
        for far in (0, 1):
            for way in (0, 1):
                mid_copy(far, way, j).wait_send()
                for k in (0, 1):
                    near_copy(far, way, k, j).wait_send()
        last_copy(j).wait_send()
        return carry

    lax.fori_loop(0, n, drain, 0)
    dec_end()


def attend_scatter(tokens, queries, kv, pages, dec_q, dec_len, out_weight, cache):
    rows, width = tokens.shape
    vmem = pl.BlockSpec(memory_space=pltpu.VMEM)
    dma = pltpu.SemaphoreType.DMA
    n = SCATTER_CHUNKS
    seqs = cache.shape[0]
    shards = 2 * RING * SIDES
    groups = pages.shape[1]
    return pl.pallas_call(
        attend_kernel,
        out_shape=(
            jax.ShapeDtypeStruct((rows, width), BF),
            jax.ShapeDtypeStruct((seqs, HEADS, HD), BF),
        ),
        in_specs=[
            vmem,
            vmem,
            vmem,
            vmem,
            vmem,
            pl.BlockSpec(memory_space=pltpu.SMEM),
            pl.BlockSpec(memory_space=pl.ANY),
            pl.BlockSpec(memory_space=pl.ANY),
        ],
        out_specs=(vmem, vmem),
        scratch_shapes=[
            pltpu.VMEM(out_weight.shape, BF),
            pltpu.VMEM((rows // n, width), BF),
            pltpu.VMEM((8, rows, width), BF),
            pltpu.VMEM((8, rows, width), BF),
            pltpu.VMEM((8, rows, width), BF),
            pltpu.VMEM((2, rows, width), BF),
            pltpu.VMEM((4, rows, width), BF),
            pltpu.VMEM((rows, width), BF),
            pltpu.VMEM(cache.shape, BF),
            pltpu.VMEM(pages.shape, BF),
            pltpu.VMEM((groups, shards, 16, HD), BF),
            pltpu.VMEM((KVH, seqs * 8, HD), F32),
            pltpu.VMEM((KVH + 1, seqs * 8, HD), F32),
            pltpu.VMEM((shards, 5, 8, HD), F32),
            dma((2,)),
            dma((8, n)),
            dma((8, n)),
            dma((4, n)),
            dma((4, n)),
            dma((8, n)),
            dma((8, n)),
            dma((n,)),
            dma((n,)),
            dma((shards,)),
            dma((shards,)),
            dma((groups,)),
            dma((groups,)),
            dma((shards,)),
            dma((shards,)),
            dma((shards,)),
            dma((shards,)),
        ],
        compiler_params=pltpu.CompilerParams(
            collective_id=2, has_side_effects=True, vmem_limit_bytes=60 * MIB
        ),
        cost_estimate=pl.CostEstimate(
            flops=2 * rows * width * out_weight.shape[1] * 2,
            bytes_accessed=12 * MIB,
            transcendentals=4 * rows * kv.shape[1],
        ),
        name="attend_scatter",
    )(tokens, queries, kv, pages, dec_q, dec_len, out_weight, cache)


def per_device(
    tokens,
    norm_gain,
    query_weight,
    kv_weight,
    out_weight,
    prefix_cache,
    prompt_len,
    page_owner,
    page_seq,
    dec_queries,
    dec_cache,
    dec_len,
):
    group_count = lax.axis_size("group")
    shard_count = lax.axis_size("tp")
    device_count = group_count * shard_count
    shard_index = lax.axis_index("tp")
    span_rows = tokens.shape[0]
    kv_width = kv_weight.shape[1]
    page_count = span_rows // PAGE
    capacity = max(2, 3 * page_count // (2 * device_count))
    queries, kv_both = gather_multiply(tokens, norm_gain, prefix_cache, query_weight, kv_weight)
    kv_own = lax.dynamic_index_in_dim(kv_both, shard_index % 2, 0, keepdims=False)[-span_rows:]
    owner = page_owner[:, 0]
    index = jnp.arange(page_count, dtype=jnp.int32)
    earlier = (owner[:, None] == owner[None, :]) & (index[None, :] < index[:, None])
    slot = jnp.sum(earlier.astype(jnp.int32), axis=1)
    starts = index * PAGE
    live = starts < prompt_len[0]
    place = owner % shard_count * group_count + owner // shard_count
    target = jnp.where(live, place * capacity + slot, device_count * capacity)
    spots = jnp.arange(device_count * capacity, dtype=jnp.int32)
    choose = (target[None, :] == spots[:, None]).astype(jnp.bfloat16)
    sent = jnp.dot(
        choose, kv_own.reshape(page_count, PAGE * kv_width), preferred_element_type=jnp.float32
    ).astype(jnp.bfloat16)
    sent = sent.reshape(device_count, capacity * PAGE, kv_width)
    lane = jnp.arange(kv_width, dtype=jnp.int32)[None, :]
    count = jnp.minimum(PAGE, prompt_len[0] - starts)
    first = lax.axis_index("group") * 16 + slot[:, None] * PAGE
    held = (lane >= first) & (lane < first + count[:, None])
    marks = jnp.where(held, page_seq[:, None] + 1, 0).astype(jnp.bfloat16)
    devices = jnp.arange(device_count, dtype=jnp.int32)
    mine = ((place[None, :] == devices[:, None]) & live[None, :]).astype(jnp.bfloat16)
    mark_rows = jnp.dot(mine, marks, preferred_element_type=jnp.float32).astype(jnp.bfloat16)
    mark_rows = jnp.pad(mark_rows[:, None, :], ((0, 0), (0, 16 - capacity * PAGE - 1), (0, 0)))
    pages = jnp.concatenate([sent, mark_rows], 1)
    pages = pages.reshape(shard_count, group_count, 16, kv_width)
    dec_seqs = dec_queries.shape[0]
    dec_q = dec_queries.reshape(dec_seqs, KVH, HEADS // KVH, HD).transpose(1, 0, 2, 3)
    dec_q = dec_q.reshape(KVH, dec_seqs * (HEADS // KVH), HD).astype(jnp.float32)
    hidden_out, dec_out = attend_scatter(
        tokens, queries, kv_both, pages, dec_q, dec_len, out_weight, dec_cache
    )
    dec_out = dec_out.reshape(dec_seqs, HEADS * HD)
    return (hidden_out, dec_out)


def solution(mesh):
    return jax.shard_map(
        per_device,
        mesh=mesh,
        in_specs=(
            P("group", "tp"),
            P(None, "tp"),
            P(None, "tp"),
            P(None, "tp"),
            P("tp", None),
            P("group", "tp"),
            P("group"),
            P("group", None),
            P("group"),
            P("group", None),
            P("group", "tp", None),
            P("group"),
        ),
        out_specs=(P("group", "tp"), P("group", None)),
        check_vma=False,
    )
```

```python
import math

import jax
import jax.numpy as jnp
from jax import lax
from jax.experimental import pallas as pl
from jax.experimental.pallas import tpu as pltpu
from jax.sharding import PartitionSpec as P

HEADS = 64
KVH = 8
HD = 128
PAGE = 4


EPSILON = 1e-05
NEG_BIG = -1e30


MESH = pl.DeviceIdType.MESH
BF = jnp.bfloat16
F32 = jnp.float32
MIB = 1024 * 1024
SIDES = 2
RING = 4


def here():
    t = lax.axis_index("tp")
    return t // (RING * 2), lax.rem(t // 2, RING), lax.rem(t, 2)


def shard_at(side, ring, core, far, step, other):
    s = lax.rem(side + far, SIDES)
    r = lax.rem(ring + step, RING)
    c = lax.rem(core + other, 2)
    return (s * RING + r) * 2 + c


def push(src, dst, send_sem, recv_sem, to):
    copy = pltpu.make_async_remote_copy(
        src_ref=src,
        dst_ref=dst,
        send_sem=send_sem,
        recv_sem=recv_sem,
        device_id={"tp": to},
        device_id_type=MESH,
    )
    copy.start()
    return copy


def landed(ref, recv_sem, to):
    pltpu.make_async_remote_copy(
        src_ref=ref,
        dst_ref=ref,
        send_sem=recv_sem,
        recv_sem=recv_sem,
        device_id={"tp": to},
        device_id_type=MESH,
    ).wait_recv()


def greet(peers):
    barrier = pltpu.get_barrier_semaphore()
    for peer in peers:
        pl.semaphore_signal(barrier, inc=1, device_id={"tp": peer}, device_id_type=MESH)
    pl.semaphore_wait(barrier, len(peers))


GATHER_CHUNKS = 4
GAIN_ROWS = 16


def gather_kernel(
    gain,
    tok,
    prefix,
    qw_hbm,
    kw_hbm,
    q_out,
    kv_out,
    xall,
    qw,
    kw,
    acc_q,
    acc_k,
    power,
    w_sem,
    recv_sem,
    sib_sem,
    x_send,
    up_send,
    down_send,
    sib_send,
    kv_send,
    kv_recv,
):
    side, ring, core = here()
    rows_all, width = tok.shape
    chunk = rows_all // GATHER_CHUNKS

    def at(far, step, other=0):
        return shard_at(side, ring, core, far, step, other)

    me, across, sib = at(0, 0), at(1, 0), at(0, 0, 1)
    up, down = at(0, 1), at(0, 3)

    load_q = pltpu.make_async_copy(qw_hbm, qw, w_sem.at[0])
    load_k = pltpu.make_async_copy(kw_hbm, kw, w_sem.at[1])
    prefix_rows = prefix.shape[0]
    load_x = pltpu.make_async_copy(tok, xall.at[me, pl.ds(GAIN_ROWS, rows_all), :], w_sem.at[2])
    load_x.start()
    load_p = pltpu.make_async_copy(prefix, kv_out.at[core, pl.ds(0, prefix_rows), :], w_sem.at[3])
    load_p.start()
    load_q.start()
    load_k.start()
    xall[me, pl.ds(0, GAIN_ROWS), :] = jnp.broadcast_to(gain[...], (GAIN_ROWS, width))
    acc_q[...] = jnp.zeros_like(acc_q)
    acc_k[...] = jnp.zeros_like(acc_k)
    power[...] = jnp.zeros_like(power)
    greet((across, up, down, sib))
    load_x.wait()

    sends = []

    def span(i, half=None):
        low = 0 if i == 0 else GAIN_ROWS + i * chunk
        high = GAIN_ROWS + (i + 1) * chunk
        middle = high - chunk // 2
        if half == 0:
            high = middle
        if half == 1:
            low = middle
        return pl.ds(low, high - low)

    def send(slot, rows, send_sem, there_sem, to):
        ref = xall.at[slot, rows, :]
        sends.append(push(ref, ref, send_sem, there_sem, to))

    def to_sibling(far, step, i):
        kind = far * 4 + step
        send(at(far, step), span(i), sib_send.at[kind, i], sib_sem.at[kind, i], sib)

    def multiply(slot, i):
        rows = pl.ds(i * chunk, chunk)
        wide = xall[slot, pl.ds(GAIN_ROWS + i * chunk, chunk), :].astype(F32)
        weight = xall[slot, pl.ds(0, 1), :].astype(F32)
        square = wide * wide
        part = square[:, 0:HD]
        for k in range(1, width // HD):
            part = part + square[:, k * HD : (k + 1) * HD]
        power[rows, :] += part
        scaled = (wide * weight).astype(BF)
        depth = pl.ds(pl.multiple_of(slot * width, width), width)
        acc_q[rows, :] += jnp.dot(scaled, qw[depth, :], preferred_element_type=F32)
        acc_k[rows, :] += jnp.dot(scaled, kw[depth, :], preferred_element_type=F32)

    def from_sibling(far, step, i):
        kind = far * 4 + step
        slot = at(far, step, 1)
        landed(xall.at[slot, span(i), :], sib_sem.at[kind, i], sib)
        multiply(slot, i)

    def got(far, step, i):
        kind = far * 4 + step
        slot = at(far, step)
        if step == 2 and far == 0:
            landed(xall.at[slot, span(i, 0), :], recv_sem.at[kind, i], down)
            landed(xall.at[slot, span(i, 1), :], recv_sem.at[8, i], up)
        else:
            landed(xall.at[slot, span(i), :], recv_sem.at[kind, i], up)

    for i in range(GATHER_CHUNKS):
        send(me, span(i), x_send.at[i], recv_sem.at[4, i], across)
        send(me, span(i), up_send.at[0, i], recv_sem.at[3, i], up)
        send(me, span(i), down_send.at[0, i], recv_sem.at[1, i], down)
        to_sibling(0, 0, i)
    load_p.wait()
    early = kv_out.at[core, pl.ds(0, prefix_rows), :]
    sends.append(push(early, early, kv_send.at[0], kv_recv.at[0], sib))
    load_q.wait()
    load_k.wait()

    def event(name, i):
        if name == "O":
            multiply(me, i)
            return [(0, 0, i)]
        if name == "X":
            got(1, 0, i)
            send(across, span(i), up_send.at[1, i], recv_sem.at[7, i], up)
            send(across, span(i), down_send.at[1, i], recv_sem.at[5, i], down)
            to_sibling(1, 0, i)
            multiply(across, i)
            return [(1, 0, i)]
        far = 0 if name in ("Z", "F") else 1
        if name in ("Z", "P"):
            got(far, 3, i)
            if far == 0:
                send(at(0, 3), span(i, 0), up_send.at[2, i], recv_sem.at[2, i], up)
            got(far, 1, i)
            if far == 0:
                send(at(0, 1), span(i, 1), down_send.at[2, i], recv_sem.at[8, i], down)
            to_sibling(far, 3, i)
            to_sibling(far, 1, i)
            multiply(at(far, 3), i)
            multiply(at(far, 1), i)
            return [(far, 3, i), (far, 1, i)]
        got(far, 2, i)
        if far == 0:
            send(at(0, 2), span(i), x_send.at[GATHER_CHUNKS + i], recv_sem.at[6, i], across)
        to_sibling(far, 2, i)
        multiply(at(far, 2), i)
        return [(far, 2, i)]

    order = (
        ("O", 0), ("O", 1), ("O", 2), ("O", 3), ("Z", 0), ("Z", 1), ("Z", 2), ("Z", 3),
        ("X", 0), ("X", 1), ("X", 2), ("X", 3), ("F", 0), ("F", 1), ("F", 2), ("F", 3),
        ("P", 0), ("P", 1), ("G", 0), ("P", 2), ("G", 1), ("G", 2), ("P", 3), ("G", 3),
    )
    late = []
    for name, i in order:
        fresh = event(name, i)
        for item in late:
            from_sibling(*item)
        late = fresh
    for item in late:
        from_sibling(*item)

    for i in range(GATHER_CHUNKS):
        rows = pl.ds(i * chunk, chunk)
        total = jnp.sum(power[rows, :], axis=-1, keepdims=True) / (width * 2 * RING * SIDES)
        factor = lax.rsqrt(total + EPSILON)
        new = pl.ds(prefix_rows + i * chunk, chunk)
        kv_out[core, new, :] = (acc_k[rows, :] * factor).astype(BF)
        ref = kv_out.at[core, new, :]
        sends.append(push(ref, ref, kv_send.at[1 + i], kv_recv.at[1 + i], sib))
        q_out[rows, :] = (acc_q[rows, :] * factor).astype(BF)
    landed(kv_out.at[1 - core, pl.ds(0, prefix_rows), :], kv_recv.at[0], sib)
    for i in range(GATHER_CHUNKS):
        new = pl.ds(prefix_rows + i * chunk, chunk)
        landed(kv_out.at[1 - core, new, :], kv_recv.at[1 + i], sib)
    for copy in sends:
        copy.wait_send()


def gather_multiply(tokens, gain, prefix, query_weight, kv_weight):
    rows, width = tokens.shape
    shards = 2 * RING * SIDES
    kv_rows = prefix.shape[0] + rows
    vmem = pl.BlockSpec(memory_space=pltpu.VMEM)
    dma = pltpu.SemaphoreType.DMA
    n = GATHER_CHUNKS
    return pl.pallas_call(
        gather_kernel,
        out_shape=(
            jax.ShapeDtypeStruct((rows, query_weight.shape[1]), BF),
            jax.ShapeDtypeStruct((2, kv_rows, HD), BF),
        ),
        in_specs=[vmem] + [pl.BlockSpec(memory_space=pl.ANY)] * 4,
        out_specs=(vmem, vmem),
        scratch_shapes=[
            pltpu.VMEM((shards, rows + GAIN_ROWS, width), BF),
            pltpu.VMEM(query_weight.shape, BF),
            pltpu.VMEM(kv_weight.shape, BF),
            pltpu.VMEM((rows, query_weight.shape[1]), F32),
            pltpu.VMEM((rows, HD), F32),
            pltpu.VMEM((rows, HD), F32),
            dma((4,)),
            dma((9, n)),
            dma((8, n)),
            dma((2 * n,)),
            dma((3, n)),
            dma((3, n)),
            dma((8, n)),
            dma((n + 1,)),
            dma((n + 1,)),
        ],
        compiler_params=pltpu.CompilerParams(
            collective_id=1, has_side_effects=True, vmem_limit_bytes=48 * MIB
        ),
        cost_estimate=pl.CostEstimate(
            flops=2 * rows * width * shards * (query_weight.shape[1] + HD),
            bytes_accessed=16 * MIB,
            transcendentals=0,
        ),
        name="gather_multiply",
    )(gain, tokens, prefix, query_weight, kv_weight)


SCATTER_CHUNKS = 8


def attend_kernel(
    q,
    kv,
    owner,
    page_rows,
    dec_q,
    dec_len,
    live_len,
    tok_hbm,
    wo_hbm,
    cache_hbm,
    out,
    dec_out,
    wo,
    att,
    mine,
    lend,
    borrowed,
    mid,
    near,
    last,
    far_in,
    tok,
    cache,
    pages,
    first_stop,
    fresh,
    heads,
    scores,
    partial,
    shares,
    results,
    w_sem,
    lend_send,
    lend_recv,
    mid_send,
    mid_recv,
    near_send,
    near_recv,
    last_send,
    last_recv,
    far_send,
    far_recv,
    first_send,
    first_recv,
    fresh_send,
    fresh_recv,
    share_send,
    share_recv,
    done_send,
    done_recv,
):
    side, ring, core = here()
    rows_all, width = out.shape
    chunk = rows_all // SCATTER_CHUNKS
    half = chunk // 2
    old = kv.shape[1] - rows_all
    n = SCATTER_CHUNKS

    def at(far, step, other=0):
        return shard_at(side, ring, core, far, step, other)

    across, sib, up, down = at(1, 0), at(0, 0, 1), at(0, 1), at(0, 3)
    load = pltpu.make_async_copy(wo_hbm, wo, w_sem.at[0])
    load.start()
    load_cache = pltpu.make_async_copy(cache_hbm, cache, w_sem.at[1])
    load_cache.start()
    load_tok = pltpu.make_async_copy(tok_hbm, tok, w_sem.at[2])
    load_tok.start()
    shard = lax.axis_index("tp")
    group = lax.axis_index("group")
    shards = 2 * RING * SIDES
    groups = lax.axis_size("group")
    dec_seqs = cache.shape[0]
    barrier = pltpu.get_barrier_semaphore()

    def greet_shard(d, carry):
        pl.semaphore_signal(
            barrier, inc=1, device_id={"tp": lax.rem(shard + d, shards)}, device_id_type=MESH
        )
        return carry

    def greet_group(d, carry):
        pl.semaphore_signal(
            barrier, inc=1, device_id={"group": lax.rem(group + d, groups)}, device_id_type=MESH
        )
        return carry

    lax.fori_loop(1, shards, greet_shard, 0)
    lax.fori_loop(1, groups, greet_group, 0)
    pl.semaphore_wait(barrier, shards + groups - 2)

    def copy_to(src, dst, send_sem, recv_sem, to):
        return pltpu.make_async_remote_copy(
            src_ref=src,
            dst_ref=dst,
            send_sem=send_sem,
            recv_sem=recv_sem,
            device_id=to,
            device_id_type=MESH,
        )

    def first_copy(d):
        to = lax.rem(shard + d, shards)
        return copy_to(
            pages.at[to], first_stop.at[shard], first_send.at[d], first_recv.at[d], {"tp": to}
        )

    def fresh_copy(d):
        to = lax.rem(group + d, groups)
        return copy_to(
            first_stop.at[:, to], fresh.at[group], fresh_send.at[d], fresh_recv.at[d], {"group": to}
        )

    def share_copy(d):
        to = lax.rem(shard + d, shards)
        return copy_to(
            partial.at[to], shares.at[shard], share_send.at[d], share_recv.at[d], {"tp": to}
        )

    def result_of(of):
        return results.at[:, pl.ds(pl.multiple_of(of * width, width), width)]

    def done_copy(d):
        to = lax.rem(shard + d, shards)
        return copy_to(
            result_of(shard), result_of(shard), done_send.at[d], done_recv.at[d], {"tp": to}
        )

    def each(count, act):
        def body(d, carry):
            act(d)
            return carry

        lax.fori_loop(1, count, body, 0)

    def source(d, count, of):
        return lax.rem(of + count - d, count)

    def dec_begin():
        old_rows = kv.shape[1] - rows_all
        turn_of = lax.broadcasted_iota(jnp.int32, (1, rows_all), 1)
        names, seqs = page_rows[0:1, :], page_rows[1:2, :]
        count = owner.shape[0]
        page = lax.broadcasted_iota(jnp.int32, (count, rows_all), 0)
        before = page < lax.broadcasted_iota(jnp.int32, (count, rows_all), 1) // PAGE
        slot = jnp.sum(
            jnp.where((owner[...] == names) & before, 1, 0), axis=0, keepdims=True
        )
        place = (lax.rem(names, shards) * groups + names // shards) * 16
        spot = slot * PAGE + lax.rem(turn_of, PAGE)
        live = turn_of // PAGE * PAGE < live_len[0]
        target = jnp.where(live, place + spot, -1)
        tag = jnp.where(live, place + 12, -1)
        lane = lax.broadcasted_iota(jnp.int32, (HD, rows_all), 0)
        mark = jnp.where(
            (lane == group * 16 + spot) & (turn_of < live_len[0]), seqs + 1, 0
        )
        mark = mark.astype(F32).astype(BF)
        block = 16 * groups

        def fill(b, carry):
            row = lax.broadcasted_iota(jnp.int32, (block, rows_all), 0) + b * block
            chosen = jnp.where(row == target, 1.0, 0.0).astype(BF)
            tagged = jnp.where(row == tag, 1.0, 0.0).astype(BF)
            made = jnp.dot(
                chosen, kv[core, pl.ds(old_rows, rows_all), :], preferred_element_type=F32
            ) + lax.dot_general(tagged, mark, contract, preferred_element_type=F32)
            pages[b] = made.astype(BF).reshape(groups, 16, HD)
            return carry

        lax.fori_loop(0, shards, fill, 0)
        first_stop[shard] = pages[shard]
        each(shards, lambda d: first_copy(d).start())

    def dec_forward():
        def take(d):
            frm = source(d, shards, shard)
            ref = first_stop.at[frm]
            copy_to(ref, ref, first_send.at[d], first_recv.at[d], {"tp": frm}).wait_recv()

        each(shards, take)
        fresh[group] = first_stop[:, pl.ds(group, 1)].reshape(shards, 16, HD)
        each(groups, lambda d: fresh_copy(d).start())

    def dec_arrive():
        def take(d):
            frm = source(d, groups, group)
            ref = fresh.at[frm]
            copy_to(ref, ref, fresh_send.at[d], fresh_recv.at[d], {"group": frm}).wait_recv()

        each(groups, take)

    scale = math.log2(math.e) / math.sqrt(HD)
    contract = (((1,), (1,)), ((), ()))

    def head_cols(k, part):
        return pl.ds(pl.multiple_of(k * 2 * HD + part * HD, HD), HD)

    count = dec_seqs * 8
    seq_row = lax.rem(lax.broadcasted_iota(jnp.int32, (count, HD), 0), 8)

    def dec_scores(k):
        ctx = cache.shape[1]
        position = lax.broadcasted_iota(jnp.int32, (count, ctx), 1) + shard * ctx
        parts = []
        for h in range(8):
            cols = pl.ds(pl.multiple_of(k * 8 * HD + h * HD, HD), HD)
            parts.append(dec_q[:, cols].astype(F32))
        query = jnp.concatenate(parts, axis=0).astype(BF)
        heads[k] = query
        found = jnp.full((count, ctx), NEG_BIG, F32)
        for seq in range(dec_seqs):
            score = lax.dot_general(
                query, cache[seq, :, head_cols(k, 0)], contract, preferred_element_type=F32
            )
            valid = (position < dec_len[seq]) & (seq_row == seq)
            found = jnp.where(valid, score * scale, found)
        scores[k] = found

    def dec_settle(k):
        spots = fresh.shape[0] * 16
        mark = fresh[0, 0].astype(F32)
        for g in range(1, fresh.shape[0]):
            mark = mark + fresh[g, 0].astype(F32)
        mark = mark[12:13, :]
        held = mark == (seq_row + 1).astype(F32)
        key = fresh[:, pl.ds(2 * k, 1)].reshape(spots, HD)
        value = fresh[:, pl.ds(2 * k + 1, 1)].reshape(spots, HD)
        new = lax.dot_general(heads[k], key, contract, preferred_element_type=F32)
        new = jnp.where(held, new * scale, NEG_BIG)
        old = scores[k]
        top = jnp.maximum(
            jnp.max(new, axis=-1, keepdims=True), jnp.max(old, axis=-1, keepdims=True)
        )
        new = jnp.where(held, jnp.exp2(new - top), 0.0)
        old = jnp.where(old > 0.5 * NEG_BIG, jnp.exp2(old - top), 0.0)
        total = jnp.sum(new, axis=-1, keepdims=True) + jnp.sum(old, axis=-1, keepdims=True)
        accum = jnp.dot(new.astype(BF), value, preferred_element_type=F32)
        for seq in range(dec_seqs):
            own = jnp.where(seq_row == seq, old, 0.0).astype(BF)
            accum = accum + jnp.dot(
                own, cache[seq, :, head_cols(k, 1)], preferred_element_type=F32
            )
        lane = lax.broadcasted_iota(jnp.int32, (8, HD), 1) // 16
        for half_of_heads in range(2):
            low = half_of_heads * 32
            stat = jnp.zeros((8, HD), F32)
            for h in range(4):
                rows = slice(low + h * 8, low + h * 8 + 8)
                stat = jnp.where(lane == h, top[rows], stat)
                stat = jnp.where(lane == 4 + h, total[rows], stat)
            partial[2 * k + half_of_heads, pl.ds(0, 32), :] = accum[low : low + 32]
            partial[2 * k + half_of_heads, pl.ds(32, 8), :] = stat

    def dec_share():
        shares[shard] = partial[shard]
        each(shards, lambda d: share_copy(d).start())

    def dec_combine():
        def take(d):
            frm = source(d, shards, shard)
            ref = shares.at[frm]
            copy_to(ref, ref, share_send.at[d], share_recv.at[d], {"tp": frm}).wait_recv()

        each(shards, take)
        stat = shares[:, pl.ds(32, 8), :]
        lane = lax.broadcasted_iota(jnp.int32, (shards, 8, HD), 2) // 16
        for h in range(4):
            top = jnp.max(jnp.where(lane == h, stat, NEG_BIG), axis=-1, keepdims=True)
            total = jnp.max(jnp.where(lane == 4 + h, stat, 0.0), axis=-1, keepdims=True)
            factor = jnp.exp2(top - jnp.max(top, axis=0, keepdims=True))
            whole = jnp.sum(factor * total, axis=0)
            accum = jnp.sum(factor * shares[:, pl.ds(h * 8, 8), :], axis=0)
            cols = pl.ds(pl.multiple_of(shard * width + h * HD, HD), HD)
            results[:, cols] = accum / whole
        each(shards, lambda d: done_copy(d).start())

    def dec_end():
        def take(d):
            frm = source(d, shards, shard)
            ref = result_of(frm)
            copy_to(ref, ref, done_send.at[d], done_recv.at[d], {"tp": frm}).wait_recv()

        each(shards, take)
        dec_out[...] = results[...].astype(BF)
        for copy in (first_copy, share_copy, done_copy):
            each(shards, lambda d, copy=copy: copy(d).wait_send())
        each(groups, lambda d: fresh_copy(d).wait_send())

    load.wait()
    load_cache.wait()
    load_tok.wait()

    def rows_of(j):
        return pl.ds(pl.multiple_of(j * chunk, chunk), chunk)

    def half_of(j, k):
        return pl.ds(pl.multiple_of(j * chunk + k * half, half), half)

    def attend(j, new):
        rows = rows_of(j)
        row = lax.broadcasted_iota(jnp.int32, (chunk, new), 0) + j * chunk
        seen = lax.broadcasted_iota(jnp.int32, (chunk, new), 1) <= row
        for h in range(width // HD):
            cols = pl.ds(h * HD, HD)
            query = q[rows, cols]
            first = lax.dot_general(
                query, kv[0, pl.ds(0, old), :], contract, preferred_element_type=F32
            )
            second = lax.dot_general(
                query, kv[0, pl.ds(old, new), :], contract, preferred_element_type=F32
            )
            first = first * scale
            second = jnp.where(seen, second * scale, NEG_BIG)
            top = jnp.maximum(
                jnp.max(first, axis=-1, keepdims=True), jnp.max(second, axis=-1, keepdims=True)
            )
            first = jnp.exp2(first - top)
            second = jnp.exp2(second - top)
            total = jnp.sum(first, axis=-1, keepdims=True) + jnp.sum(second, axis=-1, keepdims=True)
            value = jnp.dot(
                first.astype(BF), kv[1, pl.ds(0, old), :], preferred_element_type=F32
            ) + jnp.dot(
                second.astype(BF), kv[1, pl.ds(old, new), :], preferred_element_type=F32
            )
            att[:, cols] = (value / total).astype(BF)

    def attention(j):
        for low, high in ((0, n // 4), (n // 4, n // 2), (n // 2, n)):

            @pl.when((j >= low) & (j < high))
            def _(high=high):
                attend(j, high * chunk)

    def term(far, step, other):
        slot = at(far, step, other)
        cols = pl.ds(pl.multiple_of(slot * width, width), width)
        return jnp.dot(att[...], wo[:, cols], preferred_element_type=F32).astype(BF)

    def add_into(dst, src):
        dst[...] = (dst[...].astype(F32) + src[...].astype(F32)).astype(BF)

    def lend_copy(kind, j):
        rows = rows_of(j)
        return pltpu.make_async_remote_copy(
            src_ref=lend.at[kind, rows, :],
            dst_ref=borrowed.at[kind, rows, :],
            send_sem=lend_send.at[kind, j],
            recv_sem=lend_recv.at[kind, j],
            device_id={"tp": sib},
            device_id_type=MESH,
        )

    def mid_copy(way, j):
        rows = half_of(j, way)
        return pltpu.make_async_remote_copy(
            src_ref=mine.at[2, rows, :],
            dst_ref=mid.at[rows, :],
            send_sem=mid_send.at[way, j],
            recv_sem=mid_recv.at[way, j],
            device_id={"tp": down if way else up},
            device_id_type=MESH,
        )

    def far_copy(j):
        rows = rows_of(j)
        return pltpu.make_async_remote_copy(
            src_ref=mine.at[6, rows, :],
            dst_ref=far_in.at[rows, :],
            send_sem=far_send.at[j],
            recv_sem=far_recv.at[j],
            device_id={"tp": across},
            device_id_type=MESH,
        )

    def near_copy(far, way, k, j):
        rows = half_of(j, k)
        return pltpu.make_async_remote_copy(
            src_ref=mine.at[far * 4 + (3 if way else 1), rows, :],
            dst_ref=near.at[far * 2 + way, rows, :],
            send_sem=near_send.at[far * 4 + way * 2 + k, j],
            recv_sem=near_recv.at[far * 4 + way * 2 + k, j],
            device_id={"tp": down if way else up},
            device_id_type=MESH,
        )

    def last_copy(j):
        rows = rows_of(j)
        return pltpu.make_async_remote_copy(
            src_ref=mine.at[4, rows, :],
            dst_ref=last.at[rows, :],
            send_sem=last_send.at[j],
            recv_sem=last_recv.at[j],
            device_id={"tp": across},
            device_id_type=MESH,
        )

    kinds = ((1, 2), (0, 2), (1, 1), (1, 3), (0, 1), (0, 3), (1, 0), (0, 0))
    lag = 2

    def produce(j):
        attention(j)
        rows = rows_of(j)
        for k in range(len(kinds) + lag):
            if k < len(kinds):
                far, step = kinds[k]
                kind = far * 4 + step
                lend[kind, rows, :] = term(far, step, 1)
                lend_copy(kind, j).start()
                mine[kind, rows, :] = term(far, step, 0)
            if k >= lag:
                far, step = kinds[k - lag]
                kind = far * 4 + step
                lend_copy(kind, j).wait_recv()
                add_into(mine.at[kind, rows, :], borrowed.at[kind, rows, :])
                if (far, step) == (1, 2):
                    far_copy(j).start()
                if step == 1:
                    near_copy(far, 0, 1, j).start()
                    if far:
                        near_copy(far, 0, 0, j).start()
                if step == 3:
                    near_copy(far, 1, 0, j).start()
                    if far:
                        near_copy(far, 1, 1, j).start()

    def pass_on(j):
        far_copy(j).wait_recv()
        rows = rows_of(j)
        add_into(mine.at[2, rows, :], far_in.at[rows, :])
        mid_copy(0, j).start()
        mid_copy(1, j).start()

    def relay(j):
        for way in (0, 1):
            mid_copy(way, j).wait_recv()
            rows = half_of(j, way)
            add_into(mine.at[3 if way else 1, rows, :], mid.at[rows, :])
            near_copy(0, way, way, j).start()

    def near_wait(far, j):
        for way in (0, 1):
            for k in (0, 1):
                near_copy(far, way, k, j).wait_recv()

    def cross(j):
        near_wait(1, j)
        rows = rows_of(j)
        mine[4, rows, :] = (
            mine[4, rows, :].astype(F32) + near[2, rows, :].astype(F32) + near[3, rows, :].astype(F32)
        ).astype(BF)
        last_copy(j).start()

    def finish(j):
        near_wait(0, j)
        last_copy(j).wait_recv()
        rows = rows_of(j)
        out[rows, :] = (
            tok[rows, :].astype(F32)
            + (
                mine[0, rows, :].astype(F32)
                + near[0, rows, :].astype(F32)
                + near[1, rows, :].astype(F32)
                + last[rows, :].astype(F32)
            )
        ).astype(BF)

    def turn(j, carry):
        @pl.when(j < n)
        def _():
            produce(j)

        @pl.when((j >= 1) & (j < n + 1))
        def _():
            relay(j - 1)

        @pl.when(j < n)
        def _():
            pass_on(j)

        @pl.when((j >= 2) & (j < n + 2))
        def _():
            cross(j - 2)

        @pl.when(j >= 3)
        def _():
            finish(j - 3)

        @pl.when(j == 0)
        def _():
            dec_begin()

        @pl.when(j == 2)
        def _():
            dec_forward()

        @pl.when(j < 4)
        def _():
            dec_scores(2 * j)
            dec_scores(2 * j + 1)

        @pl.when(j == 4)
        def _():
            dec_arrive()

        @pl.when((j >= 4) & (j < 8))
        def _():
            dec_settle(2 * j - 8)
            dec_settle(2 * j - 7)

        @pl.when(j == 7)
        def _():
            dec_share()

        @pl.when(j == 8)
        def _():
            dec_combine()

        return carry

    lax.fori_loop(0, n + 3, turn, 0)

    def drain(j, carry):
        for kind in range(8):
            lend_copy(kind, j).wait_send()
        for far in (0, 1):
            for way in (0, 1):
                for k in (0, 1):
                    near_copy(far, way, k, j).wait_send()
        last_copy(j).wait_send()
        far_copy(j).wait_send()
        mid_copy(0, j).wait_send()
        mid_copy(1, j).wait_send()
        return carry

    lax.fori_loop(0, n, drain, 0)
    dec_end()


def attend_scatter(
    tokens, queries, kv, owner, page_rows, dec_q, dec_len, live_len, out_weight, cache, groups
):
    rows, width = tokens.shape
    vmem = pl.BlockSpec(memory_space=pltpu.VMEM)
    dma = pltpu.SemaphoreType.DMA
    n = SCATTER_CHUNKS
    seqs = cache.shape[0]
    shards = 2 * RING * SIDES
    return pl.pallas_call(
        attend_kernel,
        out_shape=(
            jax.ShapeDtypeStruct((rows, width), BF),
            jax.ShapeDtypeStruct((seqs, HEADS * HD), BF),
        ),
        in_specs=[
            vmem,
            vmem,
            vmem,
            vmem,
            vmem,
            pl.BlockSpec(memory_space=pltpu.SMEM),
            pl.BlockSpec(memory_space=pltpu.SMEM),
            pl.BlockSpec(memory_space=pl.ANY),
            pl.BlockSpec(memory_space=pl.ANY),
            pl.BlockSpec(memory_space=pl.ANY),
        ],
        out_specs=(vmem, vmem),
        scratch_shapes=[
            pltpu.VMEM(out_weight.shape, BF),
            pltpu.VMEM((rows // n, width), BF),
            pltpu.VMEM((8, rows, width), BF),
            pltpu.VMEM((8, rows, width), BF),
            pltpu.VMEM((8, rows, width), BF),
            pltpu.VMEM((rows, width), BF),
            pltpu.VMEM((4, rows, width), BF),
            pltpu.VMEM((rows, width), BF),
            pltpu.VMEM((rows, width), BF),
            pltpu.VMEM((rows, width), BF),
            pltpu.VMEM(cache.shape, BF),
            pltpu.VMEM((shards, groups, 16, HD), BF),
            pltpu.VMEM((shards, groups, 16, HD), BF),
            pltpu.VMEM((groups, shards, 16, HD), BF),
            pltpu.VMEM((KVH, seqs * 8, HD), BF),
            pltpu.VMEM((KVH, seqs * 8, HD), F32),
            pltpu.VMEM((shards, 40, HD), F32),
            pltpu.VMEM((shards, 40, HD), F32),
            pltpu.VMEM((seqs, HEADS * HD), F32),
            dma((3,)),
            dma((8, n)),
            dma((8, n)),
            dma((2, n)),
            dma((2, n)),
            dma((8, n)),
            dma((8, n)),
            dma((n,)),
            dma((n,)),
            dma((n,)),
            dma((n,)),
            dma((shards,)),
            dma((shards,)),
            dma((groups,)),
            dma((groups,)),
            dma((shards,)),
            dma((shards,)),
            dma((shards,)),
            dma((shards,)),
        ],
        compiler_params=pltpu.CompilerParams(
            collective_id=2, has_side_effects=True, vmem_limit_bytes=60 * MIB
        ),
        cost_estimate=pl.CostEstimate(
            flops=2 * rows * width * out_weight.shape[1] * 2,
            bytes_accessed=12 * MIB,
            transcendentals=4 * rows * kv.shape[1],
        ),
        name="attend_scatter",
    )(queries, kv, owner, page_rows, dec_q, dec_len, live_len, tokens, out_weight, cache)


def per_device(
    tokens,
    norm_gain,
    query_weight,
    kv_weight,
    out_weight,
    prefix_cache,
    prompt_len,
    page_owner,
    page_seq,
    dec_queries,
    dec_cache,
    dec_len,
):
    queries, kv_both = gather_multiply(tokens, norm_gain, prefix_cache, query_weight, kv_weight)
    page_rows = jnp.repeat(jnp.stack([page_owner[:, 0], page_seq]), PAGE, axis=1)
    hidden_out, dec_out = attend_scatter(
        tokens,
        queries,
        kv_both,
        page_owner,
        page_rows,
        dec_queries,
        dec_len,
        prompt_len,
        out_weight,
        dec_cache,
        lax.axis_size("group"),
    )
    return (hidden_out, dec_out)


def solution(mesh):
    return jax.shard_map(
        per_device,
        mesh=mesh,
        in_specs=(
            P("group", "tp"),
            P(None, "tp"),
            P(None, "tp"),
            P(None, "tp"),
            P("tp", None),
            P("group", "tp"),
            P("group"),
            P("group", None),
            P("group"),
            P("group", None),
            P("group", "tp", None),
            P("group"),
        ),
        out_specs=(P("group", "tp"), P("group", None)),
        check_vma=False,
    )
```

```python
import math

import jax
import jax.numpy as jnp
from jax import lax
from jax.experimental import pallas as pl
from jax.experimental.pallas import tpu as pltpu
from jax.sharding import PartitionSpec as P

HEADS = 64
KVH = 8
HD = 128
PAGE = 4


EPSILON = 1e-05
NEG_BIG = -1e30


MESH = pl.DeviceIdType.MESH
BF = jnp.bfloat16
F32 = jnp.float32
MIB = 1024 * 1024
SIDES = 2
RING = 4


def here():
    t = lax.axis_index("tp")
    return t // (RING * 2), lax.rem(t // 2, RING), lax.rem(t, 2)


def shard_at(side, ring, core, far, step, other):
    s = lax.rem(side + far, SIDES)
    r = lax.rem(ring + step, RING)
    c = lax.rem(core + other, 2)
    return (s * RING + r) * 2 + c


def push(src, dst, send_sem, recv_sem, to):
    copy = pltpu.make_async_remote_copy(
        src_ref=src,
        dst_ref=dst,
        send_sem=send_sem,
        recv_sem=recv_sem,
        device_id={"tp": to},
        device_id_type=MESH,
    )
    copy.start()
    return copy


def landed(ref, recv_sem, to):
    pltpu.make_async_remote_copy(
        src_ref=ref,
        dst_ref=ref,
        send_sem=recv_sem,
        recv_sem=recv_sem,
        device_id={"tp": to},
        device_id_type=MESH,
    ).wait_recv()


def greet(peers):
    barrier = pltpu.get_barrier_semaphore()
    for peer in peers:
        pl.semaphore_signal(barrier, inc=1, device_id={"tp": peer}, device_id_type=MESH)
    pl.semaphore_wait(barrier, len(peers))


GATHER_CHUNKS = 4
GAIN_ROWS = 16
LOG_SCALE = math.log2(math.e) / math.sqrt(HD)


def gather_kernel(
    gain,
    dec_q,
    dec_len,
    tok,
    prefix,
    qw_hbm,
    kw_hbm,
    cache_hbm,
    q_out,
    kv_out,
    heads,
    old_sum,
    old_stat,
    xall,
    cache,
    qw,
    kw,
    acc_q,
    acc_k,
    power,
    w_sem,
    recv_sem,
    sib_sem,
    x_send,
    up_send,
    down_send,
    sib_send,
    kv_send,
    kv_recv,
):
    side, ring, core = here()
    rows_all, width = tok.shape
    chunk = rows_all // GATHER_CHUNKS

    def at(far, step, other=0):
        return shard_at(side, ring, core, far, step, other)

    me, across, sib = at(0, 0), at(1, 0), at(0, 0, 1)
    up, down = at(0, 1), at(0, 3)

    load_q = pltpu.make_async_copy(qw_hbm, qw, w_sem.at[0])
    load_k = pltpu.make_async_copy(kw_hbm, kw, w_sem.at[1])
    prefix_rows = prefix.shape[0]
    load_x = pltpu.make_async_copy(tok, xall.at[me, pl.ds(GAIN_ROWS, rows_all), :], w_sem.at[2])
    load_x.start()
    load_p = pltpu.make_async_copy(prefix, kv_out.at[core, pl.ds(0, prefix_rows), :], w_sem.at[3])
    load_p.start()
    load_q.start()
    load_k.start()
    load_cache = pltpu.make_async_copy(cache_hbm, cache, w_sem.at[4])
    load_cache.start()
    xall[me, pl.ds(0, GAIN_ROWS), :] = jnp.broadcast_to(gain[...], (GAIN_ROWS, width))
    acc_q[...] = jnp.zeros_like(acc_q)
    acc_k[...] = jnp.zeros_like(acc_k)
    power[...] = jnp.zeros_like(power)
    greet((across, up, down, sib))
    load_x.wait()

    sends = []

    def span(i, half=None):
        low = 0 if i == 0 else GAIN_ROWS + i * chunk
        high = GAIN_ROWS + (i + 1) * chunk
        middle = high - chunk // 2
        if half == 0:
            high = middle
        if half == 1:
            low = middle
        return pl.ds(low, high - low)

    def send(slot, rows, send_sem, there_sem, to):
        ref = xall.at[slot, rows, :]
        sends.append(push(ref, ref, send_sem, there_sem, to))

    def to_sibling(far, step, i):
        kind = far * 4 + step
        send(at(far, step), span(i), sib_send.at[kind, i], sib_sem.at[kind, i], sib)

    def multiply(slot, i):
        rows = pl.ds(i * chunk, chunk)
        wide = xall[slot, pl.ds(GAIN_ROWS + i * chunk, chunk), :].astype(F32)
        weight = xall[slot, pl.ds(0, 1), :].astype(F32)
        square = wide * wide
        part = square[:, 0:HD]
        for k in range(1, width // HD):
            part = part + square[:, k * HD : (k + 1) * HD]
        power[rows, :] += part
        scaled = (wide * weight).astype(BF)
        depth = pl.ds(pl.multiple_of(slot * width, width), width)
        acc_q[rows, :] += jnp.dot(scaled, qw[depth, :], preferred_element_type=F32)
        acc_k[rows, :] += jnp.dot(scaled, kw[depth, :], preferred_element_type=F32)

    def from_sibling(far, step, i):
        kind = far * 4 + step
        slot = at(far, step, 1)
        landed(xall.at[slot, span(i), :], sib_sem.at[kind, i], sib)
        multiply(slot, i)

    def got(far, step, i):
        kind = far * 4 + step
        slot = at(far, step)
        if step == 2 and far == 0:
            landed(xall.at[slot, span(i, 0), :], recv_sem.at[kind, i], down)
            landed(xall.at[slot, span(i, 1), :], recv_sem.at[8, i], up)
        else:
            landed(xall.at[slot, span(i), :], recv_sem.at[kind, i], up)

    for i in range(GATHER_CHUNKS):
        send(me, span(i), x_send.at[i], recv_sem.at[4, i], across)
        send(me, span(i), up_send.at[0, i], recv_sem.at[3, i], up)
        send(me, span(i), down_send.at[0, i], recv_sem.at[1, i], down)
        to_sibling(0, 0, i)
    load_p.wait()
    early = kv_out.at[core, pl.ds(0, prefix_rows), :]
    sends.append(push(early, early, kv_send.at[0], kv_recv.at[0], sib))
    load_q.wait()
    load_k.wait()
    load_cache.wait()
    dec_seqs, ctx = cache.shape[0], cache.shape[1]
    contract = (((1,), (1,)), ((), ()))

    def dec_old(k):
        count = dec_seqs * 8
        seq_row = lax.rem(lax.broadcasted_iota(jnp.int32, (count, ctx), 0), 8)
        position = lax.broadcasted_iota(jnp.int32, (count, ctx), 1) + me * ctx
        parts = [dec_q[:, pl.ds((k * 8 + h) * HD, HD)].astype(F32) for h in range(8)]
        query = jnp.concatenate(parts, axis=0).astype(BF)
        heads[k] = query
        found = jnp.full((count, ctx), NEG_BIG, F32)
        for seq in range(dec_seqs):
            score = lax.dot_general(
                query,
                cache[seq, :, pl.ds(2 * k * HD, HD)],
                contract,
                preferred_element_type=F32,
            )
            valid = (position < dec_len[seq]) & (seq_row == seq)
            found = jnp.where(valid, score * LOG_SCALE, found)
        top = jnp.max(found, axis=-1, keepdims=True)
        expo = jnp.where(found > 0.5 * NEG_BIG, jnp.exp2(found - top), 0.0)
        accum = jnp.zeros((count, HD), F32)
        for seq in range(dec_seqs):
            own = jnp.where(seq_row == seq, expo, 0.0).astype(BF)
            accum = accum + jnp.dot(
                own, cache[seq, :, pl.ds((2 * k + 1) * HD, HD)], preferred_element_type=F32
            )
        old_sum[k] = accum
        lane = lax.broadcasted_iota(jnp.int32, (count, HD), 1)
        total = jnp.sum(expo, axis=-1, keepdims=True)
        old_stat[k] = jnp.where(lane < HD // 2, top, total)

    def event(name, i):
        if name == "O":
            multiply(me, i)
            return [(0, 0, i)]
        if name == "X":
            got(1, 0, i)
            send(across, span(i), up_send.at[1, i], recv_sem.at[7, i], up)
            send(across, span(i), down_send.at[1, i], recv_sem.at[5, i], down)
            to_sibling(1, 0, i)
            multiply(across, i)
            return [(1, 0, i)]
        far = 0 if name in ("Z", "F") else 1
        if name in ("Z", "P"):
            got(far, 3, i)
            if far == 0:
                send(at(0, 3), span(i, 0), up_send.at[2, i], recv_sem.at[2, i], up)
            got(far, 1, i)
            if far == 0:
                send(at(0, 1), span(i, 1), down_send.at[2, i], recv_sem.at[8, i], down)
            to_sibling(far, 3, i)
            to_sibling(far, 1, i)
            multiply(at(far, 3), i)
            multiply(at(far, 1), i)
            return [(far, 3, i), (far, 1, i)]
        got(far, 2, i)
        if far == 0:
            send(at(0, 2), span(i), x_send.at[GATHER_CHUNKS + i], recv_sem.at[6, i], across)
        to_sibling(far, 2, i)
        multiply(at(far, 2), i)
        return [(far, 2, i)]

    order = (
        ("O", 0), ("O", 1), ("O", 2), ("O", 3), ("Z", 0), ("Z", 1), ("Z", 2), ("Z", 3),
        ("X", 0), ("X", 1), ("X", 2), ("X", 3), ("F", 0), ("F", 1), ("F", 2), ("F", 3),
        ("P", 0), ("P", 1), ("G", 0), ("P", 2), ("G", 1), ("G", 2), ("P", 3), ("G", 3),
    )
    late = []
    for name, i in order:
        fresh = event(name, i)
        if name in ("Z", "X"):
            dec_old(i + (4 if name == "X" else 0))
        for item in late:
            from_sibling(*item)
        late = fresh
    for item in late:
        from_sibling(*item)

    for i in range(GATHER_CHUNKS):
        rows = pl.ds(i * chunk, chunk)
        total = jnp.sum(power[rows, :], axis=-1, keepdims=True) / (width * 2 * RING * SIDES)
        factor = lax.rsqrt(total + EPSILON)
        new = pl.ds(prefix_rows + i * chunk, chunk)
        kv_out[core, new, :] = (acc_k[rows, :] * factor).astype(BF)
        ref = kv_out.at[core, new, :]
        sends.append(push(ref, ref, kv_send.at[1 + i], kv_recv.at[1 + i], sib))
        queries = (acc_q[rows, :] * (factor * LOG_SCALE)).astype(BF)
        for h in range(q_out.shape[0]):
            q_out[h, rows, :] = queries[:, h * HD : (h + 1) * HD]
    landed(kv_out.at[1 - core, pl.ds(0, prefix_rows), :], kv_recv.at[0], sib)
    for i in range(GATHER_CHUNKS):
        new = pl.ds(prefix_rows + i * chunk, chunk)
        landed(kv_out.at[1 - core, new, :], kv_recv.at[1 + i], sib)
    for copy in sends:
        copy.wait_send()


def gather_multiply(tokens, gain, prefix, query_weight, kv_weight, dec_q, dec_len, cache):
    rows, width = tokens.shape
    shards = 2 * RING * SIDES
    kv_rows = prefix.shape[0] + rows
    vmem = pl.BlockSpec(memory_space=pltpu.VMEM)
    dma = pltpu.SemaphoreType.DMA
    n = GATHER_CHUNKS
    dec_rows = cache.shape[0] * 8
    return pl.pallas_call(
        gather_kernel,
        out_shape=(
            jax.ShapeDtypeStruct((query_weight.shape[1] // HD, rows, HD), BF),
            jax.ShapeDtypeStruct((2, kv_rows, HD), BF),
            jax.ShapeDtypeStruct((KVH, dec_rows, HD), BF),
            jax.ShapeDtypeStruct((KVH, dec_rows, HD), F32),
            jax.ShapeDtypeStruct((KVH, dec_rows, HD), F32),
        ),
        in_specs=[vmem, vmem, pl.BlockSpec(memory_space=pltpu.SMEM)]
        + [pl.BlockSpec(memory_space=pltpu.HBM)] * 5,
        out_specs=(vmem,) * 5,
        scratch_shapes=[
            pltpu.VMEM((shards, rows + GAIN_ROWS, width), BF),
            pltpu.VMEM(cache.shape, BF),
            pltpu.VMEM(query_weight.shape, BF),
            pltpu.VMEM(kv_weight.shape, BF),
            pltpu.VMEM((rows, query_weight.shape[1]), F32),
            pltpu.VMEM((rows, HD), F32),
            pltpu.VMEM((rows, HD), F32),
            dma((5,)),
            dma((9, n)),
            dma((8, n)),
            dma((2 * n,)),
            dma((3, n)),
            dma((3, n)),
            dma((8, n)),
            dma((n + 1,)),
            dma((n + 1,)),
        ],
        compiler_params=pltpu.CompilerParams(
            collective_id=1, has_side_effects=True, vmem_limit_bytes=62 * MIB
        ),
        cost_estimate=pl.CostEstimate(
            flops=2 * rows * width * shards * (query_weight.shape[1] + HD),
            bytes_accessed=16 * MIB,
            transcendentals=0,
        ),
        name="gather_multiply",
    )(gain, dec_q, dec_len, tokens, prefix, query_weight, kv_weight, cache)


SCATTER_CHUNKS = 8


def attend_kernel(
    q,
    kv,
    heads,
    old_sum,
    old_stat,
    owner,
    seq_of_page,
    live_len,
    tok_hbm,
    wo_hbm,
    out,
    dec_out,
    wo,
    att,
    mine,
    lend,
    borrowed,
    mid,
    near,
    last,
    far_in,
    tok,
    pages,
    first_stop,
    fresh,
    partial,
    shares,
    results,
    w_sem,
    lend_send,
    lend_recv,
    mid_send,
    mid_recv,
    near_send,
    near_recv,
    last_send,
    last_recv,
    far_send,
    far_recv,
    first_send,
    first_recv,
    fresh_send,
    fresh_recv,
    share_send,
    share_recv,
    done_send,
    done_recv,
):
    side, ring, core = here()
    rows_all, width = out.shape
    chunk = rows_all // SCATTER_CHUNKS
    half = chunk // 2
    old = kv.shape[1] - rows_all
    n = SCATTER_CHUNKS

    def at(far, step, other=0):
        return shard_at(side, ring, core, far, step, other)

    across, sib, up, down = at(1, 0), at(0, 0, 1), at(0, 1), at(0, 3)
    load = pltpu.make_async_copy(wo_hbm, wo, w_sem.at[0])
    load.start()
    load_tok = pltpu.make_async_copy(tok_hbm, tok, w_sem.at[1])
    load_tok.start()
    shard = lax.axis_index("tp")
    group = lax.axis_index("group")
    shards = 2 * RING * SIDES
    groups = lax.axis_size("group")
    dec_seqs = dec_out.shape[0]
    barrier = pltpu.get_barrier_semaphore()

    def greet_shard(d, carry):
        pl.semaphore_signal(
            barrier, inc=1, device_id={"tp": lax.rem(shard + d, shards)}, device_id_type=MESH
        )
        return carry

    def greet_group(d, carry):
        pl.semaphore_signal(
            barrier, inc=1, device_id={"group": lax.rem(group + d, groups)}, device_id_type=MESH
        )
        return carry

    lax.fori_loop(1, shards, greet_shard, 0)
    lax.fori_loop(1, groups, greet_group, 0)
    pl.semaphore_wait(barrier, shards + groups - 2)

    def copy_to(src, dst, send_sem, recv_sem, to):
        return pltpu.make_async_remote_copy(
            src_ref=src,
            dst_ref=dst,
            send_sem=send_sem,
            recv_sem=recv_sem,
            device_id=to,
            device_id_type=MESH,
        )

    def first_copy(d):
        to = lax.rem(shard + d, shards)
        return copy_to(
            pages.at[to], first_stop.at[shard], first_send.at[d], first_recv.at[d], {"tp": to}
        )

    def fresh_copy(d):
        to = lax.rem(group + d, groups)
        return copy_to(
            first_stop.at[:, to], fresh.at[group], fresh_send.at[d], fresh_recv.at[d], {"group": to}
        )

    def share_copy(d):
        to = lax.rem(shard + d, shards)
        return copy_to(
            partial.at[to], shares.at[shard], share_send.at[d], share_recv.at[d], {"tp": to}
        )

    def result_of(of):
        return results.at[:, pl.ds(pl.multiple_of(of * width, width), width)]

    def done_copy(d):
        to = lax.rem(shard + d, shards)
        return copy_to(
            result_of(shard), result_of(shard), done_send.at[d], done_recv.at[d], {"tp": to}
        )

    def each(count, act):
        def body(d, carry):
            act(d)
            return carry

        lax.fori_loop(1, count, body, 0)

    def source(d, count, of):
        return lax.rem(of + count - d, count)

    def dec_begin():
        old_rows = kv.shape[1] - rows_all
        turn_of = lax.broadcasted_iota(jnp.int32, (1, rows_all), 1)
        count = owner.shape[1]
        both = jnp.concatenate(
            [
                jnp.broadcast_to(owner[...], (8, count)),
                jnp.broadcast_to(seq_of_page[...], (8, count)),
            ],
            axis=0,
        ).astype(F32)
        page = lax.broadcasted_iota(jnp.int32, (count, rows_all), 0)
        page_of = lax.broadcasted_iota(jnp.int32, (count, rows_all), 1) // PAGE
        spread = jnp.where(page == page_of, 1.0, 0.0).astype(BF)
        by_token = jnp.dot(both.astype(BF), spread, preferred_element_type=F32).astype(jnp.int32)
        names, seqs = by_token[0:1, :], by_token[8:9, :]
        column = jnp.transpose(jnp.broadcast_to(owner[...].astype(F32), (HD, count)))
        column = column[:, 0:1].astype(jnp.int32)
        before = page < page_of
        slot = jnp.sum(
            jnp.where((column == names) & before, 1, 0), axis=0, keepdims=True
        )
        place = (lax.rem(names, shards) * groups + names // shards) * 16
        spot = slot * PAGE + lax.rem(turn_of, PAGE)
        live = turn_of // PAGE * PAGE < live_len[0]
        target = jnp.where(live, place + spot, -1)
        tag = jnp.where(live, place + 12, -1)
        lane = lax.broadcasted_iota(jnp.int32, (HD, rows_all), 0)
        mark = jnp.where(
            (lane == group * 16 + spot) & (turn_of < live_len[0]), seqs + 1, 0
        )
        mark = mark.astype(F32).astype(BF)
        block = 16 * groups

        def fill(b, carry):
            row = lax.broadcasted_iota(jnp.int32, (block, rows_all), 0) + b * block
            chosen = jnp.where(row == target, 1.0, 0.0).astype(BF)
            tagged = jnp.where(row == tag, 1.0, 0.0).astype(BF)
            made = jnp.dot(
                chosen, kv[core, pl.ds(old_rows, rows_all), :], preferred_element_type=F32
            ) + lax.dot_general(tagged, mark, contract, preferred_element_type=F32)
            pages[b] = made.astype(BF).reshape(groups, 16, HD)
            return carry

        lax.fori_loop(0, shards, fill, 0)
        first_stop[shard] = pages[shard]
        each(shards, lambda d: first_copy(d).start())

    def dec_forward():
        def take(d):
            frm = source(d, shards, shard)
            ref = first_stop.at[frm]
            copy_to(ref, ref, first_send.at[d], first_recv.at[d], {"tp": frm}).wait_recv()

        each(shards, take)
        fresh[group] = first_stop[:, pl.ds(group, 1)].reshape(shards, 16, HD)
        each(groups, lambda d: fresh_copy(d).start())

    def dec_arrive():
        def take(d):
            frm = source(d, groups, group)
            ref = fresh.at[frm]
            copy_to(ref, ref, fresh_send.at[d], fresh_recv.at[d], {"group": frm}).wait_recv()

        each(groups, take)

    contract = (((1,), (1,)), ((), ()))

    count = dec_seqs * 8
    seq_row = lax.rem(lax.broadcasted_iota(jnp.int32, (count, HD), 0), 8)

    def dec_settle(k):
        spots = fresh.shape[0] * 16
        mark = fresh[0, 0].astype(F32)
        for g in range(1, fresh.shape[0]):
            mark = mark + fresh[g, 0].astype(F32)
        mark = mark[12:13, :]
        held = mark == (seq_row + 1).astype(F32)
        key = fresh[:, pl.ds(2 * k, 1)].reshape(spots, HD)
        value = fresh[:, pl.ds(2 * k + 1, 1)].reshape(spots, HD)
        new = lax.dot_general(heads[k], key, contract, preferred_element_type=F32)
        new = jnp.where(held, new * LOG_SCALE, NEG_BIG)
        old_top = old_stat[k, :, pl.ds(0, 1)]
        old_total = old_stat[k, :, pl.ds(HD // 2, 1)]
        top = jnp.maximum(jnp.max(new, axis=-1, keepdims=True), old_top)
        new = jnp.where(held, jnp.exp2(new - top), 0.0)
        keep = jnp.exp2(old_top - top)
        total = jnp.sum(new, axis=-1, keepdims=True) + keep * old_total
        accum = jnp.dot(new.astype(BF), value, preferred_element_type=F32) + keep * old_sum[k]
        lane = lax.broadcasted_iota(jnp.int32, (8, HD), 1) // 16
        for half_of_heads in range(2):
            low = half_of_heads * 32
            stat = jnp.zeros((8, HD), F32)
            for h in range(4):
                rows = slice(low + h * 8, low + h * 8 + 8)
                stat = jnp.where(lane == h, top[rows], stat)
                stat = jnp.where(lane == 4 + h, total[rows], stat)
            partial[2 * k + half_of_heads, pl.ds(0, 32), :] = accum[low : low + 32]
            partial[2 * k + half_of_heads, pl.ds(32, 8), :] = stat

    def dec_share():
        shares[shard] = partial[shard]
        each(shards, lambda d: share_copy(d).start())

    def dec_combine():
        def take(d):
            frm = source(d, shards, shard)
            ref = shares.at[frm]
            copy_to(ref, ref, share_send.at[d], share_recv.at[d], {"tp": frm}).wait_recv()

        each(shards, take)
        stat = shares[:, pl.ds(32, 8), :]
        lane = lax.broadcasted_iota(jnp.int32, (shards, 8, HD), 2) // 16
        for h in range(4):
            top = jnp.max(jnp.where(lane == h, stat, NEG_BIG), axis=-1, keepdims=True)
            total = jnp.max(jnp.where(lane == 4 + h, stat, 0.0), axis=-1, keepdims=True)
            factor = jnp.exp2(top - jnp.max(top, axis=0, keepdims=True))
            whole = jnp.sum(factor * total, axis=0)
            accum = jnp.sum(factor * shares[:, pl.ds(h * 8, 8), :], axis=0)
            cols = pl.ds(pl.multiple_of(shard * width + h * HD, HD), HD)
            results[:, cols] = accum / whole
        each(shards, lambda d: done_copy(d).start())

    def dec_end():
        def take(d):
            frm = source(d, shards, shard)
            ref = result_of(frm)
            copy_to(ref, ref, done_send.at[d], done_recv.at[d], {"tp": frm}).wait_recv()

        each(shards, take)
        dec_out[...] = results[...].astype(BF)
        for copy in (first_copy, share_copy, done_copy):
            each(shards, lambda d, copy=copy: copy(d).wait_send())
        each(groups, lambda d: fresh_copy(d).wait_send())


    def rows_of(j):
        return pl.ds(pl.multiple_of(j * chunk, chunk), chunk)

    def half_of(j, k):
        return pl.ds(pl.multiple_of(j * chunk + k * half, half), half)

    def attend(j, plain, edge):
        rows = rows_of(j)
        count = width // HD
        query = q[:, rows, :].reshape(count * chunk, HD)
        row = lax.rem(lax.broadcasted_iota(jnp.int32, (count * chunk, edge), 0), chunk)
        column = lax.broadcasted_iota(jnp.int32, (count * chunk, edge), 1)
        seen = column + plain <= row + old + j * chunk
        first = lax.dot_general(
            query, kv[0, pl.ds(0, plain), :], contract, preferred_element_type=F32
        )
        second = lax.dot_general(
            query, kv[0, pl.ds(plain, edge), :], contract, preferred_element_type=F32
        )
        second = jnp.where(seen, second, NEG_BIG)
        top = jnp.maximum(
            jnp.max(first, axis=-1, keepdims=True), jnp.max(second, axis=-1, keepdims=True)
        )
        first = jnp.exp2(first - top)
        second = jnp.exp2(second - top)
        total = jnp.sum(first, axis=-1, keepdims=True) + jnp.sum(second, axis=-1, keepdims=True)
        value = jnp.dot(
            first.astype(BF), kv[1, pl.ds(0, plain), :], preferred_element_type=F32
        ) + jnp.dot(second.astype(BF), kv[1, pl.ds(plain, edge), :], preferred_element_type=F32)
        value = value / total
        for h in range(count):
            att[:, h * HD : (h + 1) * HD] = value[h * chunk : (h + 1) * chunk].astype(BF)

    def attention(j):
        for pair in range(n // 2):

            @pl.when(j // 2 == pair)
            def _(pair=pair):
                attend(j, old + 2 * pair * chunk, 2 * chunk)

    def term(far, step, other):
        slot = at(far, step, other)
        cols = pl.ds(pl.multiple_of(slot * width, width), width)
        return jnp.dot(att[...], wo[:, cols], preferred_element_type=F32).astype(BF)

    def add_into(dst, src):
        dst[...] = (dst[...].astype(F32) + src[...].astype(F32)).astype(BF)

    def lend_copy(kind, j):
        rows = rows_of(j)
        return pltpu.make_async_remote_copy(
            src_ref=lend.at[kind, rows, :],
            dst_ref=borrowed.at[kind, rows, :],
            send_sem=lend_send.at[kind, j],
            recv_sem=lend_recv.at[kind, j],
            device_id={"tp": sib},
            device_id_type=MESH,
        )

    def mid_copy(way, j):
        rows = half_of(j, way)
        return pltpu.make_async_remote_copy(
            src_ref=mine.at[2, rows, :],
            dst_ref=mid.at[rows, :],
            send_sem=mid_send.at[way, j],
            recv_sem=mid_recv.at[way, j],
            device_id={"tp": down if way else up},
            device_id_type=MESH,
        )

    def far_copy(j):
        rows = rows_of(j)
        return pltpu.make_async_remote_copy(
            src_ref=mine.at[6, rows, :],
            dst_ref=far_in.at[rows, :],
            send_sem=far_send.at[j],
            recv_sem=far_recv.at[j],
            device_id={"tp": across},
            device_id_type=MESH,
        )

    def near_copy(far, way, k, j):
        rows = half_of(j, k)
        return pltpu.make_async_remote_copy(
            src_ref=mine.at[far * 4 + (3 if way else 1), rows, :],
            dst_ref=near.at[far * 2 + way, rows, :],
            send_sem=near_send.at[far * 4 + way * 2 + k, j],
            recv_sem=near_recv.at[far * 4 + way * 2 + k, j],
            device_id={"tp": down if way else up},
            device_id_type=MESH,
        )

    def last_copy(j):
        rows = rows_of(j)
        return pltpu.make_async_remote_copy(
            src_ref=mine.at[4, rows, :],
            dst_ref=last.at[rows, :],
            send_sem=last_send.at[j],
            recv_sem=last_recv.at[j],
            device_id={"tp": across},
            device_id_type=MESH,
        )

    kinds = ((1, 2), (0, 2), (1, 1), (1, 3), (0, 1), (0, 3), (1, 0), (0, 0))
    lag = 2

    def produce(j):
        rows = rows_of(j)
        for k in range(len(kinds) + lag):
            if k < len(kinds):
                far, step = kinds[k]
                kind = far * 4 + step
                lend[kind, rows, :] = term(far, step, 1)
                lend_copy(kind, j).start()
                mine[kind, rows, :] = term(far, step, 0)
            if k >= lag:
                far, step = kinds[k - lag]
                kind = far * 4 + step
                lend_copy(kind, j).wait_recv()
                add_into(mine.at[kind, rows, :], borrowed.at[kind, rows, :])
                if (far, step) == (1, 2):
                    far_copy(j).start()
                if step == 1:
                    near_copy(far, 0, 1, j).start()
                    if far:
                        near_copy(far, 0, 0, j).start()
                if step == 3:
                    near_copy(far, 1, 0, j).start()
                    if far:
                        near_copy(far, 1, 1, j).start()

    def pass_on(j):
        far_copy(j).wait_recv()
        rows = rows_of(j)
        add_into(mine.at[2, rows, :], far_in.at[rows, :])
        mid_copy(0, j).start()
        mid_copy(1, j).start()

    def relay(j):
        for way in (0, 1):
            mid_copy(way, j).wait_recv()
            rows = half_of(j, way)
            add_into(mine.at[3 if way else 1, rows, :], mid.at[rows, :])
            near_copy(0, way, way, j).start()

    def near_wait(far, j):
        for way in (0, 1):
            for k in (0, 1):
                near_copy(far, way, k, j).wait_recv()

    def cross(j):
        near_wait(1, j)
        rows = rows_of(j)
        mine[4, rows, :] = (
            mine[4, rows, :].astype(F32) + near[2, rows, :].astype(F32) + near[3, rows, :].astype(F32)
        ).astype(BF)
        last_copy(j).start()

    def finish(j):
        near_wait(0, j)
        last_copy(j).wait_recv()
        rows = rows_of(j)
        out[rows, :] = (
            tok[rows, :].astype(F32)
            + (
                mine[0, rows, :].astype(F32)
                + near[0, rows, :].astype(F32)
                + near[1, rows, :].astype(F32)
                + last[rows, :].astype(F32)
            )
        ).astype(BF)

    def turn(j, carry):
        @pl.when(j < n)
        def _():
            attention(j)

        @pl.when(j == 0)
        def _():
            load.wait()
            load_tok.wait()

        @pl.when((j >= 1) & (j < n + 1))
        def _():
            pass_on(j - 1)

        @pl.when(j < n)
        def _():
            produce(j)

        @pl.when((j >= 2) & (j < n + 2))
        def _():
            relay(j - 2)

        @pl.when((j >= 3) & (j < n + 3))
        def _():
            cross(j - 3)

        @pl.when(j >= 4)
        def _():
            finish(j - 4)

        @pl.when(j == 1)
        def _():
            dec_begin()

        @pl.when(j == 3)
        def _():
            dec_forward()

        @pl.when(j == 5)
        def _():
            dec_arrive()

        @pl.when((j >= 5) & (j < 7))
        def _():
            def settle(k, carry):
                dec_settle(k)
                return carry

            lax.fori_loop((j - 5) * 4, (j - 4) * 4, settle, 0)

        @pl.when(j == 6)
        def _():
            dec_share()

        @pl.when(j == 8)
        def _():
            dec_combine()

        return carry

    lax.fori_loop(0, n + 4, turn, 0)

    def drain(j, carry):
        for kind in range(8):
            lend_copy(kind, j).wait_send()
        for far in (0, 1):
            for way in (0, 1):
                for k in (0, 1):
                    near_copy(far, way, k, j).wait_send()
        last_copy(j).wait_send()
        far_copy(j).wait_send()
        mid_copy(0, j).wait_send()
        mid_copy(1, j).wait_send()
        return carry

    lax.fori_loop(0, n, drain, 0)
    dec_end()


def attend_scatter(
    tokens, queries, kv, heads, old_sum, old_stat, owner, seq_of_page, live_len, out_weight, groups
):
    rows, width = tokens.shape
    vmem = pl.BlockSpec(memory_space=pltpu.VMEM)
    dma = pltpu.SemaphoreType.DMA
    n = SCATTER_CHUNKS
    seqs = heads.shape[1] // 8
    shards = 2 * RING * SIDES
    return pl.pallas_call(
        attend_kernel,
        out_shape=(
            jax.ShapeDtypeStruct((rows, width), BF),
            jax.ShapeDtypeStruct((seqs, HEADS * HD), BF),
        ),
        in_specs=[
            vmem,
            vmem,
            vmem,
            vmem,
            vmem,
            vmem,
            vmem,
            pl.BlockSpec(memory_space=pltpu.SMEM),
            pl.BlockSpec(memory_space=pltpu.HBM),
            pl.BlockSpec(memory_space=pltpu.HBM),
        ],
        out_specs=(vmem, vmem),
        scratch_shapes=[
            pltpu.VMEM(out_weight.shape, BF),
            pltpu.VMEM((rows // n, width), BF),
            pltpu.VMEM((8, rows, width), BF),
            pltpu.VMEM((8, rows, width), BF),
            pltpu.VMEM((8, rows, width), BF),
            pltpu.VMEM((rows, width), BF),
            pltpu.VMEM((4, rows, width), BF),
            pltpu.VMEM((rows, width), BF),
            pltpu.VMEM((rows, width), BF),
            pltpu.VMEM((rows, width), BF),
            pltpu.VMEM((shards, groups, 16, HD), BF),
            pltpu.VMEM((shards, groups, 16, HD), BF),
            pltpu.VMEM((groups, shards, 16, HD), BF),
            pltpu.VMEM((shards, 40, HD), F32),
            pltpu.VMEM((shards, 40, HD), F32),
            pltpu.VMEM((seqs, HEADS * HD), F32),
            dma((2,)),
            dma((8, n)),
            dma((8, n)),
            dma((2, n)),
            dma((2, n)),
            dma((8, n)),
            dma((8, n)),
            dma((n,)),
            dma((n,)),
            dma((n,)),
            dma((n,)),
            dma((shards,)),
            dma((shards,)),
            dma((groups,)),
            dma((groups,)),
            dma((shards,)),
            dma((shards,)),
            dma((shards,)),
            dma((shards,)),
        ],
        compiler_params=pltpu.CompilerParams(
            collective_id=2, has_side_effects=True, vmem_limit_bytes=62 * MIB
        ),
        cost_estimate=pl.CostEstimate(
            flops=2 * rows * width * out_weight.shape[1] * 2,
            bytes_accessed=12 * MIB,
            transcendentals=4 * rows * kv.shape[1],
        ),
        name="attend_scatter",
    )(queries, kv, heads, old_sum, old_stat, owner, seq_of_page, live_len, tokens, out_weight)


def hand_on_kernel(hidden, dec, hidden_out, dec_out, sem):
    first = pltpu.make_async_copy(hidden, hidden_out, sem.at[0])
    second = pltpu.make_async_copy(dec, dec_out, sem.at[1])
    first.start()
    second.start()
    first.wait()
    second.wait()


def hand_on(hidden, dec):
    vmem = pl.BlockSpec(memory_space=pltpu.VMEM)
    hbm = pl.BlockSpec(memory_space=pltpu.HBM)
    return pl.pallas_call(
        hand_on_kernel,
        out_shape=(
            jax.ShapeDtypeStruct(hidden.shape, hidden.dtype),
            jax.ShapeDtypeStruct(dec.shape, dec.dtype),
        ),
        in_specs=[vmem, vmem],
        out_specs=(hbm, hbm),
        scratch_shapes=[pltpu.SemaphoreType.DMA((2,))],
        name="hand_on",
    )(hidden, dec)


def per_device(
    tokens,
    norm_gain,
    query_weight,
    kv_weight,
    out_weight,
    prefix_cache,
    prompt_len,
    page_owner,
    page_seq,
    dec_queries,
    dec_cache,
    dec_len,
):
    queries, kv_both, heads, old_sum, old_stat = gather_multiply(
        tokens, norm_gain, prefix_cache, query_weight, kv_weight, dec_queries, dec_len, dec_cache
    )
    hidden_out, dec_out = attend_scatter(
        tokens,
        queries,
        kv_both,
        heads,
        old_sum,
        old_stat,
        page_owner.reshape(1, -1),
        page_seq.reshape(1, -1),
        prompt_len,
        out_weight,
        lax.axis_size("group"),
    )
    return hand_on(hidden_out, dec_out)


def solution(mesh):
    return jax.shard_map(
        per_device,
        mesh=mesh,
        in_specs=(
            P("group", "tp"),
            P(None, "tp"),
            P(None, "tp"),
            P(None, "tp"),
            P("tp", None),
            P("group", "tp"),
            P("group"),
            P("group", None),
            P("group"),
            P("group", None),
            P("group", "tp", None),
            P("group"),
        ),
        out_specs=(P("group", "tp"), P("group", None)),
        check_vma=False,
    )
```

```python
import math

import jax
import jax.numpy as jnp
from jax import lax
from jax.experimental import pallas as pl
from jax.experimental.pallas import tpu as pltpu
from jax.sharding import PartitionSpec as P

HEADS = 64
KVH = 8
HD = 128
PAGE = 4


EPSILON = 1e-05
NEG_BIG = -1e30


MESH = pl.DeviceIdType.MESH
BF = jnp.bfloat16
F32 = jnp.float32
MIB = 1024 * 1024
SIDES = 2
RING = 4


def here():
    t = lax.axis_index("tp")
    return t // (RING * 2), lax.rem(t // 2, RING), lax.rem(t, 2)


def shard_at(side, ring, core, far, step, other):
    s = lax.rem(side + far, SIDES)
    r = lax.rem(ring + step, RING)
    c = lax.rem(core + other, 2)
    return (s * RING + r) * 2 + c


def push(src, dst, send_sem, recv_sem, to):
    copy = pltpu.make_async_remote_copy(
        src_ref=src,
        dst_ref=dst,
        send_sem=send_sem,
        recv_sem=recv_sem,
        device_id={"tp": to},
        device_id_type=MESH,
    )
    copy.start()
    return copy


def landed(ref, recv_sem, to):
    pltpu.make_async_remote_copy(
        src_ref=ref,
        dst_ref=ref,
        send_sem=recv_sem,
        recv_sem=recv_sem,
        device_id={"tp": to},
        device_id_type=MESH,
    ).wait_recv()


def greet(peers):
    barrier = pltpu.get_barrier_semaphore()
    for peer in peers:
        pl.semaphore_signal(barrier, inc=1, device_id={"tp": peer}, device_id_type=MESH)
    pl.semaphore_wait(barrier, len(peers))


GATHER_CHUNKS = 4
GAIN_ROWS = 16
PACK_PARTS = 8
LOG_SCALE = math.log2(math.e) / math.sqrt(HD)


def gather_kernel(
    gain,
    dec_q,
    owner,
    seq_of_page,
    dec_len,
    live_len,
    tok,
    prefix,
    qw_hbm,
    kw_hbm,
    cache_hbm,
    q_out,
    kv_out,
    heads,
    old_sum,
    old_stat,
    pages,
    xall,
    cache,
    choice,
    tags,
    qw,
    kw,
    acc_q,
    acc_k,
    power,
    w_sem,
    recv_sem,
    sib_sem,
    x_send,
    up_send,
    down_send,
    sib_send,
    kv_send,
    kv_recv,
    split_send,
    split_recv,
):
    side, ring, core = here()
    rows_all, width = tok.shape
    chunk = rows_all // GATHER_CHUNKS
    group = lax.axis_index("group")
    groups = lax.axis_size("group")
    shards = 2 * RING * SIDES

    def at(far, step, other=0):
        return shard_at(side, ring, core, far, step, other)

    me, across, sib = at(0, 0), at(1, 0), at(0, 0, 1)
    up, down = at(0, 1), at(0, 3)

    load_q = pltpu.make_async_copy(qw_hbm, qw, w_sem.at[0])
    load_k = pltpu.make_async_copy(kw_hbm, kw, w_sem.at[1])
    prefix_rows = prefix.shape[0]
    load_x = pltpu.make_async_copy(tok, xall.at[me, pl.ds(GAIN_ROWS, rows_all), :], w_sem.at[2])
    load_x.start()
    load_p = pltpu.make_async_copy(prefix, kv_out.at[core, pl.ds(0, prefix_rows), :], w_sem.at[3])
    load_p.start()
    load_q.start()
    load_k.start()
    load_cache = pltpu.make_async_copy(cache_hbm, cache, w_sem.at[4])
    load_cache.start()
    xall[me, pl.ds(0, GAIN_ROWS), :] = jnp.broadcast_to(gain[...], (GAIN_ROWS, width))
    acc_q[...] = jnp.zeros_like(acc_q)
    acc_k[...] = jnp.zeros_like(acc_k)
    power[...] = jnp.zeros_like(power)
    greet((across, up, down, sib))
    load_x.wait()

    sends = []
    split = GATHER_CHUNKS - 1

    def span(i, half=None):
        low = 0 if i == 0 else GAIN_ROWS + i * chunk
        high = GAIN_ROWS + (i + 1) * chunk
        middle = high - chunk // 2
        if half == 0:
            high = middle
        if half == 1:
            low = middle
        return pl.ds(low, high - low)

    def send(slot, rows, send_sem, there_sem, to):
        ref = xall.at[slot, rows, :]
        sends.append(push(ref, ref, send_sem, there_sem, to))

    def to_sibling(far, step, i):
        kind = far * 4 + step
        send(at(far, step), span(i), sib_send.at[kind, i], sib_sem.at[kind, i], sib)

    def multiply(slot, i):
        rows = pl.ds(i * chunk, chunk)
        wide = xall[slot, pl.ds(GAIN_ROWS + i * chunk, chunk), :].astype(F32)
        weight = xall[slot, pl.ds(0, 1), :].astype(F32)
        square = wide * wide
        part = square[:, 0:HD]
        for k in range(1, width // HD):
            part = part + square[:, k * HD : (k + 1) * HD]
        power[rows, :] += part
        scaled = (wide * weight).astype(BF)
        depth = pl.ds(pl.multiple_of(slot * width, width), width)
        acc_q[rows, :] += jnp.dot(scaled, qw[depth, :], preferred_element_type=F32)
        acc_k[rows, :] += jnp.dot(scaled, kw[depth, :], preferred_element_type=F32)

    def from_sibling(far, step, i):
        kind = far * 4 + step
        slot = at(far, step, 1)
        landed(xall.at[slot, span(i), :], sib_sem.at[kind, i], sib)
        multiply(slot, i)

    def got(far, step, i):
        kind = far * 4 + step
        slot = at(far, step)
        if step == 2 and far == 0:
            landed(xall.at[slot, span(i, 0), :], recv_sem.at[kind, i], down)
            landed(xall.at[slot, span(i, 1), :], recv_sem.at[8, i], up)
        elif i == split and far == 1 and step in (1, 3):
            landed(xall.at[slot, span(i, 0), :], recv_sem.at[kind, i], up)
            landed(xall.at[slot, span(i, 1), :], split_recv.at[step // 2], across)
        else:
            landed(xall.at[slot, span(i), :], recv_sem.at[kind, i], up)

    for i in range(GATHER_CHUNKS):
        send(me, span(i), x_send.at[i], recv_sem.at[4, i], across)
        send(me, span(i), up_send.at[0, i], recv_sem.at[3, i], up)
        send(me, span(i), down_send.at[0, i], recv_sem.at[1, i], down)
        to_sibling(0, 0, i)
    load_p.wait()
    early = kv_out.at[core, pl.ds(0, prefix_rows), :]
    sends.append(push(early, early, kv_send.at[0], kv_recv.at[0], sib))
    load_q.wait()
    load_k.wait()
    load_cache.wait()
    dec_seqs, ctx = cache.shape[0], cache.shape[1]
    contract = (((1,), (1,)), ((), ()))

    def dec_old(k):
        count = dec_seqs * 8
        seq_row = lax.rem(lax.broadcasted_iota(jnp.int32, (count, ctx), 0), 8)
        position = lax.broadcasted_iota(jnp.int32, (count, ctx), 1) + me * ctx
        parts = [dec_q[:, pl.ds((k * 8 + h) * HD, HD)].astype(F32) for h in range(8)]
        query = jnp.concatenate(parts, axis=0).astype(BF)
        heads[k] = query
        found = jnp.full((count, ctx), NEG_BIG, F32)
        for seq in range(dec_seqs):
            score = lax.dot_general(
                query,
                cache[seq, :, pl.ds(2 * k * HD, HD)],
                contract,
                preferred_element_type=F32,
            )
            valid = (position < dec_len[seq]) & (seq_row == seq)
            found = jnp.where(valid, score * LOG_SCALE, found)
        top = jnp.max(found, axis=-1, keepdims=True)
        expo = jnp.where(found > 0.5 * NEG_BIG, jnp.exp2(found - top), 0.0)
        accum = jnp.zeros((count, HD), F32)
        for seq in range(dec_seqs):
            own = jnp.where(seq_row == seq, expo, 0.0).astype(BF)
            accum = accum + jnp.dot(
                own, cache[seq, :, pl.ds((2 * k + 1) * HD, HD)], preferred_element_type=F32
            )
        old_sum[k] = accum
        lane = lax.broadcasted_iota(jnp.int32, (count, HD), 1)
        total = jnp.sum(expo, axis=-1, keepdims=True)
        old_stat[k] = jnp.where(lane < HD // 2, top, total)

    turn_of = lax.broadcasted_iota(jnp.int32, (1, rows_all), 1)
    count = owner.shape[1]
    both = jnp.concatenate(
        [
            jnp.broadcast_to(owner[...], (8, count)),
            jnp.broadcast_to(seq_of_page[...], (8, count)),
        ],
        axis=0,
    ).astype(F32)
    page = lax.broadcasted_iota(jnp.int32, (count, rows_all), 0)
    page_of = lax.broadcasted_iota(jnp.int32, (count, rows_all), 1) // PAGE
    spread = jnp.where(page == page_of, 1.0, 0.0).astype(BF)
    by_token = jnp.dot(both.astype(BF), spread, preferred_element_type=F32).astype(jnp.int32)
    names, seqs = by_token[0:1, :], by_token[8:9, :]
    column = jnp.transpose(jnp.broadcast_to(owner[...].astype(F32), (HD, count)))
    column = column[:, 0:1].astype(jnp.int32)
    before = page < page_of
    slot = jnp.sum(
        jnp.where((column == names) & before, 1, 0), axis=0, keepdims=True
    )
    place = (lax.rem(names, shards) * groups + names // shards) * 16
    spot = slot * PAGE + lax.rem(turn_of, PAGE)
    live = turn_of // PAGE * PAGE < live_len[0]
    target = jnp.where(live, place + spot, -1)
    tag = jnp.where(live, place + 12, -1)
    lane = lax.broadcasted_iota(jnp.int32, (HD, rows_all), 0)
    mark = jnp.where(
        (lane == group * 16 + spot) & (turn_of < live_len[0]), seqs + 1, 0
    )
    mark = mark.astype(F32).astype(BF)
    block = tags.shape[0] // PACK_PARTS

    def pack(part):
        row = lax.broadcasted_iota(jnp.int32, (block, rows_all), 0) + part * block
        rows = pl.ds(part * block, block)
        choice[rows, :] = jnp.where(row == target, 1.0, 0.0).astype(BF)
        tagged = jnp.where(row == tag, 1.0, 0.0).astype(BF)
        tags[rows, :] = lax.dot_general(
            tagged, mark, contract, preferred_element_type=F32
        ).astype(BF)

    def event(name, i):
        if name == "O":
            multiply(me, i)
            return [(0, 0, i)]
        if name == "X":
            got(1, 0, i)
            rows = span(i, 0) if i == split else span(i)
            send(across, rows, up_send.at[1, i], recv_sem.at[7, i], up)
            send(across, rows, down_send.at[1, i], recv_sem.at[5, i], down)
            to_sibling(1, 0, i)
            multiply(across, i)
            return [(1, 0, i)]
        far = 0 if name in ("Z", "F") else 1
        if name in ("Z", "P"):
            got(far, 3, i)
            if far == 0:
                send(at(0, 3), span(i, 0), up_send.at[2, i], recv_sem.at[2, i], up)
                if i == split:
                    send(at(0, 3), span(i, 1), split_send.at[1], split_recv.at[1], across)
            got(far, 1, i)
            if far == 0:
                send(at(0, 1), span(i, 1), down_send.at[2, i], recv_sem.at[8, i], down)
                if i == split:
                    send(at(0, 1), span(i, 1), split_send.at[0], split_recv.at[0], across)
            to_sibling(far, 3, i)
            to_sibling(far, 1, i)
            multiply(at(far, 3), i)
            multiply(at(far, 1), i)
            return [(far, 3, i), (far, 1, i)]
        got(far, 2, i)
        if far == 0:
            send(at(0, 2), span(i), x_send.at[GATHER_CHUNKS + i], recv_sem.at[6, i], across)
        to_sibling(far, 2, i)
        multiply(at(far, 2), i)
        return [(far, 2, i)]

    order = (
        ("O", 0), ("O", 1), ("O", 2), ("O", 3), ("Z", 0), ("Z", 1), ("Z", 2), ("Z", 3),
        ("X", 0), ("X", 1), ("X", 2), ("X", 3), ("F", 0), ("F", 1), ("F", 2), ("F", 3),
        ("P", 0), ("P", 1), ("G", 0), ("P", 2), ("G", 1), ("G", 2), ("P", 3), ("G", 3),
    )
    late = []
    for name, i in order:
        fresh = event(name, i)
        if name in ("Z", "X"):
            dec_old(i + (4 if name == "X" else 0))
        if name == "F":
            pack(2 * i)
            pack(2 * i + 1)
        for item in late:
            from_sibling(*item)
        late = fresh
    for item in late:
        from_sibling(*item)

    for i in range(GATHER_CHUNKS):
        rows = pl.ds(i * chunk, chunk)
        total = jnp.sum(power[rows, :], axis=-1, keepdims=True) / (width * 2 * RING * SIDES)
        factor = lax.rsqrt(total + EPSILON)
        new = pl.ds(prefix_rows + i * chunk, chunk)
        kv_out[core, new, :] = (acc_k[rows, :] * factor).astype(BF)
        ref = kv_out.at[core, new, :]
        sends.append(push(ref, ref, kv_send.at[1 + i], kv_recv.at[1 + i], sib))
        queries = (acc_q[rows, :] * (factor * LOG_SCALE)).astype(BF)
        for h in range(q_out.shape[0]):
            q_out[h, rows, :] = queries[:, h * HD : (h + 1) * HD]
    for part in range(PACK_PARTS):
        rows = pl.ds(part * block, block)
        made = jnp.dot(
            choice[rows, :],
            kv_out[core, pl.ds(prefix_rows, rows_all), :],
            preferred_element_type=F32,
        )
        pages[rows, :] = (made + tags[rows, :].astype(F32)).astype(BF)
    landed(kv_out.at[1 - core, pl.ds(0, prefix_rows), :], kv_recv.at[0], sib)
    for i in range(GATHER_CHUNKS):
        new = pl.ds(prefix_rows + i * chunk, chunk)
        landed(kv_out.at[1 - core, new, :], kv_recv.at[1 + i], sib)
    for copy in sends:
        copy.wait_send()


def gather_multiply(
    tokens,
    gain,
    prefix,
    query_weight,
    kv_weight,
    dec_q,
    dec_len,
    cache,
    owner,
    seq_of_page,
    live_len,
    groups,
):
    rows, width = tokens.shape
    shards = 2 * RING * SIDES
    kv_rows = prefix.shape[0] + rows
    vmem = pl.BlockSpec(memory_space=pltpu.VMEM)
    dma = pltpu.SemaphoreType.DMA
    n = GATHER_CHUNKS
    dec_rows = cache.shape[0] * 8
    page_rows = shards * groups * 16
    return pl.pallas_call(
        gather_kernel,
        out_shape=(
            jax.ShapeDtypeStruct((query_weight.shape[1] // HD, rows, HD), BF),
            jax.ShapeDtypeStruct((2, kv_rows, HD), BF),
            jax.ShapeDtypeStruct((KVH, dec_rows, HD), BF),
            jax.ShapeDtypeStruct((KVH, dec_rows, HD), F32),
            jax.ShapeDtypeStruct((KVH, dec_rows, HD), F32),
            jax.ShapeDtypeStruct((page_rows, HD), BF),
        ),
        in_specs=[vmem] * 4
        + [pl.BlockSpec(memory_space=pltpu.SMEM)] * 2
        + [pl.BlockSpec(memory_space=pltpu.HBM)] * 5,
        out_specs=(vmem,) * 6,
        scratch_shapes=[
            pltpu.VMEM((shards, rows + GAIN_ROWS, width), BF),
            pltpu.VMEM(cache.shape, BF),
            pltpu.VMEM((page_rows, rows), BF),
            pltpu.VMEM((page_rows, HD), BF),
            pltpu.VMEM(query_weight.shape, BF),
            pltpu.VMEM(kv_weight.shape, BF),
            pltpu.VMEM((rows, query_weight.shape[1]), F32),
            pltpu.VMEM((rows, HD), F32),
            pltpu.VMEM((rows, HD), F32),
            dma((5,)),
            dma((9, n)),
            dma((8, n)),
            dma((2 * n,)),
            dma((3, n)),
            dma((3, n)),
            dma((8, n)),
            dma((n + 1,)),
            dma((n + 1,)),
            dma((2,)),
            dma((2,)),
        ],
        compiler_params=pltpu.CompilerParams(
            collective_id=1, has_side_effects=True, vmem_limit_bytes=62 * MIB
        ),
        cost_estimate=pl.CostEstimate(
            flops=2 * rows * width * shards * (query_weight.shape[1] + HD),
            bytes_accessed=16 * MIB,
            transcendentals=0,
        ),
        name="gather_multiply",
    )(
        gain,
        dec_q,
        owner,
        seq_of_page,
        dec_len,
        live_len,
        tokens,
        prefix,
        query_weight,
        kv_weight,
        cache,
    )


SCATTER_CHUNKS = 8


def attend_kernel(
    q,
    kv,
    heads,
    old_sum,
    old_stat,
    pages,
    tok_hbm,
    wo_hbm,
    out,
    dec_out,
    wo,
    att,
    mine,
    lend,
    borrowed,
    mid,
    near,
    last,
    far_in,
    tok,
    first_stop,
    fresh,
    partial,
    shares,
    results,
    w_sem,
    lend_send,
    lend_recv,
    mid_send,
    mid_recv,
    near_send,
    near_recv,
    last_send,
    last_recv,
    far_send,
    far_recv,
    first_send,
    first_recv,
    fresh_send,
    fresh_recv,
    share_send,
    share_recv,
    done_send,
    done_recv,
):
    side, ring, core = here()
    rows_all, width = out.shape
    chunk = rows_all // SCATTER_CHUNKS
    half = chunk // 2
    old = kv.shape[1] - rows_all
    n = SCATTER_CHUNKS

    def at(far, step, other=0):
        return shard_at(side, ring, core, far, step, other)

    across, sib, up, down = at(1, 0), at(0, 0, 1), at(0, 1), at(0, 3)
    load = pltpu.make_async_copy(wo_hbm, wo, w_sem.at[0])
    load.start()
    load_tok = pltpu.make_async_copy(tok_hbm, tok, w_sem.at[1])
    load_tok.start()
    shard = lax.axis_index("tp")
    group = lax.axis_index("group")
    shards = 2 * RING * SIDES
    groups = lax.axis_size("group")
    dec_seqs = dec_out.shape[0]
    barrier = pltpu.get_barrier_semaphore()

    def greet_shard(d, carry):
        pl.semaphore_signal(
            barrier, inc=1, device_id={"tp": lax.rem(shard + d, shards)}, device_id_type=MESH
        )
        return carry

    def greet_group(d, carry):
        pl.semaphore_signal(
            barrier, inc=1, device_id={"group": lax.rem(group + d, groups)}, device_id_type=MESH
        )
        return carry

    lax.fori_loop(1, shards, greet_shard, 0)
    lax.fori_loop(1, groups, greet_group, 0)

    def copy_to(src, dst, send_sem, recv_sem, to):
        return pltpu.make_async_remote_copy(
            src_ref=src,
            dst_ref=dst,
            send_sem=send_sem,
            recv_sem=recv_sem,
            device_id=to,
            device_id_type=MESH,
        )

    def first_copy(d):
        to = lax.rem(shard + d, shards)
        return copy_to(
            pages.at[to], first_stop.at[shard], first_send.at[d], first_recv.at[d], {"tp": to}
        )

    def fresh_copy(d):
        to = lax.rem(group + d, groups)
        return copy_to(
            first_stop.at[:, to], fresh.at[group], fresh_send.at[d], fresh_recv.at[d], {"group": to}
        )

    def share_copy(d):
        to = lax.rem(shard + d, shards)
        return copy_to(
            partial.at[to], shares.at[shard], share_send.at[d], share_recv.at[d], {"tp": to}
        )

    def result_of(of):
        return results.at[:, pl.ds(pl.multiple_of(of * width, width), width)]

    def done_copy(d):
        to = lax.rem(shard + d, shards)
        return copy_to(
            result_of(shard), result_of(shard), done_send.at[d], done_recv.at[d], {"tp": to}
        )

    def each(count, act):
        def body(d, carry):
            act(d)
            return carry

        lax.fori_loop(1, count, body, 0)

    def source(d, count, of):
        return lax.rem(of + count - d, count)

    def dec_begin():
        first_stop[shard] = pages[shard]
        each(shards, lambda d: first_copy(d).start())

    def dec_forward():
        def take(d):
            frm = source(d, shards, shard)
            ref = first_stop.at[frm]
            copy_to(ref, ref, first_send.at[d], first_recv.at[d], {"tp": frm}).wait_recv()

        each(shards, take)
        fresh[group] = first_stop[:, pl.ds(group, 1)].reshape(shards, 16, HD)
        each(groups, lambda d: fresh_copy(d).start())

    def dec_arrive():
        def take(d):
            frm = source(d, groups, group)
            ref = fresh.at[frm]
            copy_to(ref, ref, fresh_send.at[d], fresh_recv.at[d], {"group": frm}).wait_recv()

        each(groups, take)

    contract = (((1,), (1,)), ((), ()))

    count = dec_seqs * 8
    seq_row = lax.rem(lax.broadcasted_iota(jnp.int32, (count, HD), 0), 8)

    def dec_settle(k):
        spots = fresh.shape[0] * 16
        mark = fresh[0, 0].astype(F32)
        for g in range(1, fresh.shape[0]):
            mark = mark + fresh[g, 0].astype(F32)
        mark = mark[12:13, :]
        held = mark == (seq_row + 1).astype(F32)
        key = fresh[:, pl.ds(2 * k, 1)].reshape(spots, HD)
        value = fresh[:, pl.ds(2 * k + 1, 1)].reshape(spots, HD)
        new = lax.dot_general(heads[k], key, contract, preferred_element_type=F32)
        new = jnp.where(held, new * LOG_SCALE, NEG_BIG)
        old_top = old_stat[k, :, pl.ds(0, 1)]
        old_total = old_stat[k, :, pl.ds(HD // 2, 1)]
        top = jnp.maximum(jnp.max(new, axis=-1, keepdims=True), old_top)
        new = jnp.where(held, jnp.exp2(new - top), 0.0)
        keep = jnp.exp2(old_top - top)
        total = jnp.sum(new, axis=-1, keepdims=True) + keep * old_total
        accum = jnp.dot(new.astype(BF), value, preferred_element_type=F32) + keep * old_sum[k]
        lane = lax.broadcasted_iota(jnp.int32, (8, HD), 1) // 16
        for half_of_heads in range(2):
            low = half_of_heads * 32
            stat = jnp.zeros((8, HD), F32)
            for h in range(4):
                rows = slice(low + h * 8, low + h * 8 + 8)
                stat = jnp.where(lane == h, top[rows], stat)
                stat = jnp.where(lane == 4 + h, total[rows], stat)
            partial[2 * k + half_of_heads, pl.ds(0, 32), :] = accum[low : low + 32]
            partial[2 * k + half_of_heads, pl.ds(32, 8), :] = stat

    def dec_share():
        shares[shard] = partial[shard]
        each(shards, lambda d: share_copy(d).start())

    def dec_combine():
        def take(d):
            frm = source(d, shards, shard)
            ref = shares.at[frm]
            copy_to(ref, ref, share_send.at[d], share_recv.at[d], {"tp": frm}).wait_recv()

        each(shards, take)
        stat = shares[:, pl.ds(32, 8), :]
        lane = lax.broadcasted_iota(jnp.int32, (shards, 8, HD), 2) // 16
        for h in range(4):
            top = jnp.max(jnp.where(lane == h, stat, NEG_BIG), axis=-1, keepdims=True)
            total = jnp.max(jnp.where(lane == 4 + h, stat, 0.0), axis=-1, keepdims=True)
            factor = jnp.exp2(top - jnp.max(top, axis=0, keepdims=True))
            whole = jnp.sum(factor * total, axis=0)
            accum = jnp.sum(factor * shares[:, pl.ds(h * 8, 8), :], axis=0)
            cols = pl.ds(pl.multiple_of(shard * width + h * HD, HD), HD)
            results[:, cols] = accum / whole
        each(shards, lambda d: done_copy(d).start())

    def dec_end():
        def take(d):
            frm = source(d, shards, shard)
            ref = result_of(frm)
            copy_to(ref, ref, done_send.at[d], done_recv.at[d], {"tp": frm}).wait_recv()

        each(shards, take)
        dec_out[...] = results[...].astype(BF)
        for copy in (first_copy, share_copy, done_copy):
            each(shards, lambda d, copy=copy: copy(d).wait_send())
        each(groups, lambda d: fresh_copy(d).wait_send())


    def rows_of(j):
        return pl.ds(pl.multiple_of(j * chunk, chunk), chunk)

    def half_of(j, k):
        return pl.ds(pl.multiple_of(j * chunk + k * half, half), half)

    def attend(j, plain, edge):
        rows = rows_of(j)
        count = width // HD
        query = q[:, rows, :].reshape(count * chunk, HD)
        row = lax.rem(lax.broadcasted_iota(jnp.int32, (count * chunk, edge), 0), chunk)
        column = lax.broadcasted_iota(jnp.int32, (count * chunk, edge), 1)
        seen = column + plain <= row + old + j * chunk
        first = lax.dot_general(
            query, kv[0, pl.ds(0, plain), :], contract, preferred_element_type=F32
        )
        second = lax.dot_general(
            query, kv[0, pl.ds(plain, edge), :], contract, preferred_element_type=F32
        )
        second = jnp.where(seen, second, NEG_BIG)
        top = jnp.maximum(
            jnp.max(first, axis=-1, keepdims=True), jnp.max(second, axis=-1, keepdims=True)
        )
        first = jnp.exp2(first - top)
        second = jnp.exp2(second - top)
        total = jnp.sum(first, axis=-1, keepdims=True) + jnp.sum(second, axis=-1, keepdims=True)
        value = jnp.dot(
            first.astype(BF), kv[1, pl.ds(0, plain), :], preferred_element_type=F32
        ) + jnp.dot(second.astype(BF), kv[1, pl.ds(plain, edge), :], preferred_element_type=F32)
        value = value / total
        for h in range(count):
            att[:, h * HD : (h + 1) * HD] = value[h * chunk : (h + 1) * chunk].astype(BF)

    def attention(j):
        for pair in range(n // 2):

            @pl.when(j // 2 == pair)
            def _(pair=pair):
                attend(j, old + 2 * pair * chunk, 2 * chunk)

    def term(far, step, other):
        slot = at(far, step, other)
        cols = pl.ds(pl.multiple_of(slot * width, width), width)
        return jnp.dot(att[...], wo[:, cols], preferred_element_type=F32)

    def add_into(dst, src):
        dst[...] = (dst[...].astype(F32) + src[...].astype(F32)).astype(BF)

    def lend_copy(kind, j):
        rows = rows_of(j)
        return pltpu.make_async_remote_copy(
            src_ref=lend.at[kind, rows, :],
            dst_ref=borrowed.at[kind, rows, :],
            send_sem=lend_send.at[kind, j],
            recv_sem=lend_recv.at[kind, j],
            device_id={"tp": sib},
            device_id_type=MESH,
        )

    def mid_copy(way, j):
        rows = half_of(j, way)
        return pltpu.make_async_remote_copy(
            src_ref=mine.at[2, rows, :],
            dst_ref=mid.at[rows, :],
            send_sem=mid_send.at[way, j],
            recv_sem=mid_recv.at[way, j],
            device_id={"tp": down if way else up},
            device_id_type=MESH,
        )

    def far_copy(j):
        rows = rows_of(j)
        return pltpu.make_async_remote_copy(
            src_ref=mine.at[6, rows, :],
            dst_ref=far_in.at[rows, :],
            send_sem=far_send.at[j],
            recv_sem=far_recv.at[j],
            device_id={"tp": across},
            device_id_type=MESH,
        )

    def near_copy(far, way, k, j):
        rows = half_of(j, k)
        return pltpu.make_async_remote_copy(
            src_ref=mine.at[far * 4 + (3 if way else 1), rows, :],
            dst_ref=near.at[far * 2 + way, rows, :],
            send_sem=near_send.at[far * 4 + way * 2 + k, j],
            recv_sem=near_recv.at[far * 4 + way * 2 + k, j],
            device_id={"tp": down if way else up},
            device_id_type=MESH,
        )

    def last_copy(j):
        rows = rows_of(j)
        return pltpu.make_async_remote_copy(
            src_ref=mine.at[4, rows, :],
            dst_ref=last.at[rows, :],
            send_sem=last_send.at[j],
            recv_sem=last_recv.at[j],
            device_id={"tp": across},
            device_id_type=MESH,
        )

    kinds = ((1, 2), (1, 1), (1, 3), (0, 2), (0, 1), (0, 3), (1, 0), (0, 0))
    ahead = 4

    def produce(j):
        rows = rows_of(j)

        def offer(far, step):
            kind = far * 4 + step
            lend[kind, rows, :] = term(far, step, 1).astype(BF)
            lend_copy(kind, j).start()

        for far, step in kinds[:ahead]:
            offer(far, step)
        for k, (far, step) in enumerate(kinds):
            if k + ahead < len(kinds):
                offer(*kinds[k + ahead])
            kind = far * 4 + step
            own = term(far, step, 0)
            lend_copy(kind, j).wait_recv()
            mine[kind, rows, :] = (own + borrowed[kind, rows, :].astype(F32)).astype(BF)
            if (far, step) == (1, 2):
                far_copy(j).start()
            if step == 1:
                near_copy(far, 0, 1, j).start()
                if far:
                    near_copy(far, 0, 0, j).start()
            if step == 3:
                near_copy(far, 1, 0, j).start()
                if far:
                    near_copy(far, 1, 1, j).start()

    def pass_on(j):
        far_copy(j).wait_recv()
        rows = rows_of(j)
        add_into(mine.at[2, rows, :], far_in.at[rows, :])
        mid_copy(0, j).start()
        mid_copy(1, j).start()

    def relay(j):
        for way in (0, 1):
            mid_copy(way, j).wait_recv()
            rows = half_of(j, way)
            add_into(mine.at[3 if way else 1, rows, :], mid.at[rows, :])
            near_copy(0, way, way, j).start()

    def near_wait(far, j):
        for way in (0, 1):
            for k in (0, 1):
                near_copy(far, way, k, j).wait_recv()

    def cross(j):
        near_wait(1, j)
        rows = rows_of(j)
        mine[4, rows, :] = (
            mine[4, rows, :].astype(F32) + near[2, rows, :].astype(F32) + near[3, rows, :].astype(F32)
        ).astype(BF)
        last_copy(j).start()

    def finish(j):
        near_wait(0, j)
        last_copy(j).wait_recv()
        rows = rows_of(j)
        out[rows, :] = (
            tok[rows, :].astype(F32)
            + (
                mine[0, rows, :].astype(F32)
                + near[0, rows, :].astype(F32)
                + near[1, rows, :].astype(F32)
                + last[rows, :].astype(F32)
            )
        ).astype(BF)

    pl.semaphore_wait(barrier, shards + groups - 2)
    dec_begin()
    attend(0, old, 2 * chunk)

    def turn(j, carry):
        @pl.when((j >= 1) & (j < n))
        def _():
            attention(j)

        @pl.when(j == 0)
        def _():
            load.wait()
            load_tok.wait()

        @pl.when((j >= 1) & (j < n + 1))
        def _():
            pass_on(j - 1)

        @pl.when(j < n)
        def _():
            produce(j)

        @pl.when((j >= 2) & (j < n + 2))
        def _():
            relay(j - 2)

        @pl.when((j >= 3) & (j < n + 3))
        def _():
            cross(j - 3)

        @pl.when(j >= 4)
        def _():
            finish(j - 4)

        @pl.when(j == 0)
        def _():
            dec_forward()

        @pl.when(j == 2)
        def _():
            dec_arrive()

        @pl.when((j >= 2) & (j < 4))
        def _():
            def settle(k, carry):
                dec_settle(k)
                return carry

            lax.fori_loop((j - 2) * 4, (j - 1) * 4, settle, 0)

        @pl.when(j == 3)
        def _():
            dec_share()

        @pl.when(j == 6)
        def _():
            dec_combine()

        return carry

    lax.fori_loop(0, n + 4, turn, 0)

    def drain(j, carry):
        for kind in range(8):
            lend_copy(kind, j).wait_send()
        for far in (0, 1):
            for way in (0, 1):
                for k in (0, 1):
                    near_copy(far, way, k, j).wait_send()
        last_copy(j).wait_send()
        far_copy(j).wait_send()
        mid_copy(0, j).wait_send()
        mid_copy(1, j).wait_send()
        return carry

    lax.fori_loop(0, n, drain, 0)
    dec_end()


def attend_scatter(
    tokens, queries, kv, heads, old_sum, old_stat, pages, out_weight
):
    rows, width = tokens.shape
    vmem = pl.BlockSpec(memory_space=pltpu.VMEM)
    dma = pltpu.SemaphoreType.DMA
    n = SCATTER_CHUNKS
    groups = pages.shape[1]
    seqs = heads.shape[1] // 8
    shards = 2 * RING * SIDES
    return pl.pallas_call(
        attend_kernel,
        out_shape=(
            jax.ShapeDtypeStruct((rows, width), BF),
            jax.ShapeDtypeStruct((seqs, HEADS * HD), BF),
        ),
        in_specs=[
            vmem,
            vmem,
            vmem,
            vmem,
            vmem,
            vmem,
            pl.BlockSpec(memory_space=pltpu.HBM),
            pl.BlockSpec(memory_space=pltpu.HBM),
        ],
        out_specs=(vmem, vmem),
        scratch_shapes=[
            pltpu.VMEM(out_weight.shape, BF),
            pltpu.VMEM((rows // n, width), BF),
            pltpu.VMEM((8, rows, width), BF),
            pltpu.VMEM((8, rows, width), BF),
            pltpu.VMEM((8, rows, width), BF),
            pltpu.VMEM((rows, width), BF),
            pltpu.VMEM((4, rows, width), BF),
            pltpu.VMEM((rows, width), BF),
            pltpu.VMEM((rows, width), BF),
            pltpu.VMEM((rows, width), BF),
            pltpu.VMEM((shards, groups, 16, HD), BF),
            pltpu.VMEM((groups, shards, 16, HD), BF),
            pltpu.VMEM((shards, 40, HD), F32),
            pltpu.VMEM((shards, 40, HD), F32),
            pltpu.VMEM((seqs, HEADS * HD), F32),
            dma((2,)),
            dma((8, n)),
            dma((8, n)),
            dma((2, n)),
            dma((2, n)),
            dma((8, n)),
            dma((8, n)),
            dma((n,)),
            dma((n,)),
            dma((n,)),
            dma((n,)),
            dma((shards,)),
            dma((shards,)),
            dma((groups,)),
            dma((groups,)),
            dma((shards,)),
            dma((shards,)),
            dma((shards,)),
            dma((shards,)),
        ],
        compiler_params=pltpu.CompilerParams(
            collective_id=2, has_side_effects=True, vmem_limit_bytes=62 * MIB
        ),
        cost_estimate=pl.CostEstimate(
            flops=2 * rows * width * out_weight.shape[1] * 2,
            bytes_accessed=12 * MIB,
            transcendentals=4 * rows * kv.shape[1],
        ),
        name="attend_scatter",
    )(queries, kv, heads, old_sum, old_stat, pages, tokens, out_weight)


def hand_on_kernel(hidden, dec, hidden_out, dec_out, sem):
    first = pltpu.make_async_copy(hidden, hidden_out, sem.at[0])
    second = pltpu.make_async_copy(dec, dec_out, sem.at[1])
    first.start()
    second.start()
    first.wait()
    second.wait()


def hand_on(hidden, dec):
    vmem = pl.BlockSpec(memory_space=pltpu.VMEM)
    hbm = pl.BlockSpec(memory_space=pltpu.HBM)
    return pl.pallas_call(
        hand_on_kernel,
        out_shape=(
            jax.ShapeDtypeStruct(hidden.shape, hidden.dtype),
            jax.ShapeDtypeStruct(dec.shape, dec.dtype),
        ),
        in_specs=[vmem, vmem],
        out_specs=(hbm, hbm),
        scratch_shapes=[pltpu.SemaphoreType.DMA((2,))],
        name="hand_on",
    )(hidden, dec)


def per_device(
    tokens,
    norm_gain,
    query_weight,
    kv_weight,
    out_weight,
    prefix_cache,
    prompt_len,
    page_owner,
    page_seq,
    dec_queries,
    dec_cache,
    dec_len,
):
    group_count = lax.axis_size("group")
    queries, kv_both, heads, old_sum, old_stat, pages = gather_multiply(
        tokens,
        norm_gain,
        prefix_cache,
        query_weight,
        kv_weight,
        dec_queries,
        dec_len,
        dec_cache,
        page_owner.reshape(1, -1),
        page_seq.reshape(1, -1),
        prompt_len,
        group_count,
    )
    pages = pages.reshape(-1, group_count, 16, HD)
    hidden_out, dec_out = attend_scatter(
        tokens, queries, kv_both, heads, old_sum, old_stat, pages, out_weight
    )
    return hand_on(hidden_out, dec_out)


def solution(mesh):
    return jax.shard_map(
        per_device,
        mesh=mesh,
        in_specs=(
            P("group", "tp"),
            P(None, "tp"),
            P(None, "tp"),
            P(None, "tp"),
            P("tp", None),
            P("group", "tp"),
            P("group"),
            P("group", None),
            P("group"),
            P("group", None),
            P("group", "tp", None),
            P("group"),
        ),
        out_specs=(P("group", "tp"), P("group", None)),
        check_vma=False,
    )
```

```python
import math

import jax
import jax.numpy as jnp
from jax import lax
from jax.experimental import pallas as pl
from jax.experimental.pallas import tpu as pltpu
from jax.sharding import PartitionSpec as P

HEADS = 64
KVH = 8
HD = 128
PAGE = 4


EPSILON = 1e-05
NEG_BIG = -1e30


MESH = pl.DeviceIdType.MESH
BF = jnp.bfloat16
F32 = jnp.float32
MIB = 1024 * 1024
SIDES = 2
RING = 4


def here():
    t = lax.axis_index("tp")
    return t // (RING * 2), lax.rem(t // 2, RING), lax.rem(t, 2)


def shard_at(side, ring, core, far, step, other):
    s = lax.rem(side + far, SIDES)
    r = lax.rem(ring + step, RING)
    c = lax.rem(core + other, 2)
    return (s * RING + r) * 2 + c


def push(src, dst, send_sem, recv_sem, to):
    copy = pltpu.make_async_remote_copy(
        src_ref=src,
        dst_ref=dst,
        send_sem=send_sem,
        recv_sem=recv_sem,
        device_id={"tp": to},
        device_id_type=MESH,
    )
    copy.start()
    return copy


def landed(ref, recv_sem, to):
    pltpu.make_async_remote_copy(
        src_ref=ref,
        dst_ref=ref,
        send_sem=recv_sem,
        recv_sem=recv_sem,
        device_id={"tp": to},
        device_id_type=MESH,
    ).wait_recv()


def greet(peers):
    barrier = pltpu.get_barrier_semaphore()
    for peer in peers:
        pl.semaphore_signal(barrier, inc=1, device_id={"tp": peer}, device_id_type=MESH)
    pl.semaphore_wait(barrier, len(peers))


GATHER_CHUNKS = 4
GAIN_ROWS = 16
SHARE_ROWS = 40
LOG_SCALE = math.log2(math.e) / math.sqrt(HD)


def write_share(share, accum, top, total, low):
    lane = lax.broadcasted_iota(jnp.int32, (8, HD), 1) // 16
    stat = jnp.zeros((8, HD), F32)
    for h in range(4):
        rows = slice(low + h * 8, low + h * 8 + 8)
        stat = jnp.where(lane == h, top[rows], stat)
        stat = jnp.where(lane == 4 + h, total[rows], stat)
    share[pl.ds(0, 32), :] = accum[low : low + 32]
    share[pl.ds(32, 8), :] = stat


def gather_kernel(
    gain,
    dec_q,
    dec_len,
    tok,
    prefix,
    qw_hbm,
    kw_hbm,
    cache_hbm,
    q_out,
    kv_out,
    old_share,
    xall,
    cache,
    qw,
    kw,
    acc_q,
    acc_k,
    power,
    w_sem,
    recv_sem,
    sib_sem,
    x_send,
    up_send,
    down_send,
    sib_send,
    kv_send,
    kv_recv,
    split_send,
    split_recv,
):
    side, ring, core = here()
    rows_all, width = tok.shape
    chunk = rows_all // GATHER_CHUNKS

    def at(far, step, other=0):
        return shard_at(side, ring, core, far, step, other)

    me, across, sib = at(0, 0), at(1, 0), at(0, 0, 1)
    up, down = at(0, 1), at(0, 3)

    load_q = pltpu.make_async_copy(qw_hbm, qw, w_sem.at[0])
    load_k = pltpu.make_async_copy(kw_hbm, kw, w_sem.at[1])
    prefix_rows = prefix.shape[0]
    load_x = pltpu.make_async_copy(tok, xall.at[me, pl.ds(GAIN_ROWS, rows_all), :], w_sem.at[2])
    load_x.start()
    load_p = pltpu.make_async_copy(prefix, kv_out.at[core, pl.ds(0, prefix_rows), :], w_sem.at[3])
    load_p.start()
    load_q.start()
    load_k.start()
    load_cache = pltpu.make_async_copy(cache_hbm, cache, w_sem.at[4])
    load_cache.start()
    xall[me, pl.ds(0, GAIN_ROWS), :] = jnp.broadcast_to(gain[...], (GAIN_ROWS, width))
    acc_q[...] = jnp.zeros_like(acc_q)
    acc_k[...] = jnp.zeros_like(acc_k)
    power[...] = jnp.zeros_like(power)
    greet((across, up, down, sib))
    load_x.wait()

    sends = []
    split = GATHER_CHUNKS - 1

    def span(i, half=None):
        low = 0 if i == 0 else GAIN_ROWS + i * chunk
        high = GAIN_ROWS + (i + 1) * chunk
        middle = high - chunk // 2
        if half == 0:
            high = middle
        if half == 1:
            low = middle
        return pl.ds(low, high - low)

    def send(slot, rows, send_sem, there_sem, to):
        ref = xall.at[slot, rows, :]
        sends.append(push(ref, ref, send_sem, there_sem, to))

    def to_sibling(far, step, i):
        kind = far * 4 + step
        send(at(far, step), span(i), sib_send.at[kind, i], sib_sem.at[kind, i], sib)

    def multiply(slot, i):
        rows = pl.ds(i * chunk, chunk)
        wide = xall[slot, pl.ds(GAIN_ROWS + i * chunk, chunk), :].astype(F32)
        weight = xall[slot, pl.ds(0, 1), :].astype(F32)
        square = wide * wide
        part = square[:, 0:HD]
        for k in range(1, width // HD):
            part = part + square[:, k * HD : (k + 1) * HD]
        power[rows, :] += part
        scaled = (wide * weight).astype(BF)
        depth = pl.ds(pl.multiple_of(slot * width, width), width)
        acc_q[rows, :] += jnp.dot(scaled, qw[depth, :], preferred_element_type=F32)
        acc_k[rows, :] += jnp.dot(scaled, kw[depth, :], preferred_element_type=F32)

    def from_sibling(far, step, i):
        kind = far * 4 + step
        slot = at(far, step, 1)
        landed(xall.at[slot, span(i), :], sib_sem.at[kind, i], sib)
        multiply(slot, i)

    def got(far, step, i):
        kind = far * 4 + step
        slot = at(far, step)
        if step == 2 and far == 0:
            landed(xall.at[slot, span(i, 0), :], recv_sem.at[kind, i], down)
            landed(xall.at[slot, span(i, 1), :], recv_sem.at[8, i], up)
        elif i == split and far == 1 and step in (1, 3):
            landed(xall.at[slot, span(i, 0), :], recv_sem.at[kind, i], up)
            landed(xall.at[slot, span(i, 1), :], split_recv.at[step // 2], across)
        else:
            landed(xall.at[slot, span(i), :], recv_sem.at[kind, i], up)

    for i in range(GATHER_CHUNKS):
        send(me, span(i), x_send.at[i], recv_sem.at[4, i], across)
        send(me, span(i), up_send.at[0, i], recv_sem.at[3, i], up)
        send(me, span(i), down_send.at[0, i], recv_sem.at[1, i], down)
        to_sibling(0, 0, i)
    load_p.wait()
    early = kv_out.at[core, pl.ds(0, prefix_rows), :]
    sends.append(push(early, early, kv_send.at[0], kv_recv.at[0], sib))
    load_q.wait()
    load_k.wait()
    load_cache.wait()
    dec_seqs, ctx = cache.shape[0], cache.shape[1]
    contract = (((1,), (1,)), ((), ()))

    def dec_old(k):
        count = dec_seqs * 8
        seq_row = lax.rem(lax.broadcasted_iota(jnp.int32, (count, ctx), 0), 8)
        position = lax.broadcasted_iota(jnp.int32, (count, ctx), 1) + me * ctx
        parts = [dec_q[:, pl.ds((k * 8 + h) * HD, HD)].astype(F32) for h in range(8)]
        query = jnp.concatenate(parts, axis=0).astype(BF)
        found = jnp.full((count, ctx), NEG_BIG, F32)
        for seq in range(dec_seqs):
            score = lax.dot_general(
                query,
                cache[seq, :, pl.ds(2 * k * HD, HD)],
                contract,
                preferred_element_type=F32,
            )
            valid = (position < dec_len[seq]) & (seq_row == seq)
            found = jnp.where(valid, score * LOG_SCALE, found)
        top = jnp.max(found, axis=-1, keepdims=True)
        expo = jnp.where(found > 0.5 * NEG_BIG, jnp.exp2(found - top), 0.0)
        accum = jnp.zeros((count, HD), F32)
        for seq in range(dec_seqs):
            own = jnp.where(seq_row == seq, expo, 0.0).astype(BF)
            accum = accum + jnp.dot(
                own, cache[seq, :, pl.ds((2 * k + 1) * HD, HD)], preferred_element_type=F32
            )
        total = jnp.sum(expo, axis=-1, keepdims=True)
        for part in range(2):
            write_share(old_share.at[2 * k + part], accum, top, total, part * 32)

    def event(name, i):
        if name == "O":
            multiply(me, i)
            return [(0, 0, i)]
        if name == "X":
            got(1, 0, i)
            rows = span(i, 0) if i == split else span(i)
            send(across, rows, up_send.at[1, i], recv_sem.at[7, i], up)
            send(across, rows, down_send.at[1, i], recv_sem.at[5, i], down)
            to_sibling(1, 0, i)
            multiply(across, i)
            return [(1, 0, i)]
        far = 0 if name in ("Z", "F") else 1
        if name in ("Z", "P"):
            got(far, 3, i)
            if far == 0:
                send(at(0, 3), span(i, 0), up_send.at[2, i], recv_sem.at[2, i], up)
                if i == split:
                    send(at(0, 3), span(i, 1), split_send.at[1], split_recv.at[1], across)
            got(far, 1, i)
            if far == 0:
                send(at(0, 1), span(i, 1), down_send.at[2, i], recv_sem.at[8, i], down)
                if i == split:
                    send(at(0, 1), span(i, 1), split_send.at[0], split_recv.at[0], across)
            to_sibling(far, 3, i)
            to_sibling(far, 1, i)
            multiply(at(far, 3), i)
            multiply(at(far, 1), i)
            return [(far, 3, i), (far, 1, i)]
        got(far, 2, i)
        if far == 0:
            send(at(0, 2), span(i), x_send.at[GATHER_CHUNKS + i], recv_sem.at[6, i], across)
        to_sibling(far, 2, i)
        multiply(at(far, 2), i)
        return [(far, 2, i)]

    order = (
        ("O", 0), ("O", 1), ("O", 2), ("O", 3), ("Z", 0), ("Z", 1), ("Z", 2), ("Z", 3),
        ("X", 0), ("X", 1), ("X", 2), ("X", 3), ("F", 0), ("F", 1), ("F", 2), ("F", 3),
        ("P", 0), ("P", 1), ("G", 0), ("P", 2), ("G", 1), ("G", 2), ("P", 3), ("G", 3),
    )
    late = []
    for name, i in order:
        fresh = event(name, i)
        if name in ("Z", "X"):
            dec_old(i + (4 if name == "X" else 0))
        for item in late:
            from_sibling(*item)
        late = fresh
    for item in late:
        from_sibling(*item)

    for i in range(GATHER_CHUNKS):
        rows = pl.ds(i * chunk, chunk)
        total = jnp.sum(power[rows, :], axis=-1, keepdims=True) / (width * 2 * RING * SIDES)
        factor = lax.rsqrt(total + EPSILON)
        new = pl.ds(prefix_rows + i * chunk, chunk)
        kv_out[core, new, :] = (acc_k[rows, :] * factor).astype(BF)
        ref = kv_out.at[core, new, :]
        sends.append(push(ref, ref, kv_send.at[1 + i], kv_recv.at[1 + i], sib))
        queries = (acc_q[rows, :] * (factor * LOG_SCALE)).astype(BF)
        for h in range(q_out.shape[0]):
            q_out[h, rows, :] = queries[:, h * HD : (h + 1) * HD]
    landed(kv_out.at[1 - core, pl.ds(0, prefix_rows), :], kv_recv.at[0], sib)
    for i in range(GATHER_CHUNKS):
        new = pl.ds(prefix_rows + i * chunk, chunk)
        landed(kv_out.at[1 - core, new, :], kv_recv.at[1 + i], sib)
    for copy in sends:
        copy.wait_send()


def gather_multiply(tokens, gain, prefix, query_weight, kv_weight, dec_q, dec_len, cache):
    rows, width = tokens.shape
    shards = 2 * RING * SIDES
    kv_rows = prefix.shape[0] + rows
    vmem = pl.BlockSpec(memory_space=pltpu.VMEM)
    dma = pltpu.SemaphoreType.DMA
    n = GATHER_CHUNKS
    return pl.pallas_call(
        gather_kernel,
        out_shape=(
            jax.ShapeDtypeStruct((query_weight.shape[1] // HD, rows, HD), BF),
            jax.ShapeDtypeStruct((2, kv_rows, HD), BF),
            jax.ShapeDtypeStruct((shards, SHARE_ROWS, HD), F32),
        ),
        in_specs=[vmem, vmem, pl.BlockSpec(memory_space=pltpu.SMEM)]
        + [pl.BlockSpec(memory_space=pltpu.HBM)] * 5,
        out_specs=(vmem,) * 3,
        scratch_shapes=[
            pltpu.VMEM((shards, rows + GAIN_ROWS, width), BF),
            pltpu.VMEM(cache.shape, BF),
            pltpu.VMEM(query_weight.shape, BF),
            pltpu.VMEM(kv_weight.shape, BF),
            pltpu.VMEM((rows, query_weight.shape[1]), F32),
            pltpu.VMEM((rows, HD), F32),
            pltpu.VMEM((rows, HD), F32),
            dma((5,)),
            dma((9, n)),
            dma((8, n)),
            dma((2 * n,)),
            dma((3, n)),
            dma((3, n)),
            dma((8, n)),
            dma((n + 1,)),
            dma((n + 1,)),
            dma((2,)),
            dma((2,)),
        ],
        compiler_params=pltpu.CompilerParams(
            collective_id=1, has_side_effects=True, vmem_limit_bytes=62 * MIB
        ),
        cost_estimate=pl.CostEstimate(
            flops=2 * rows * width * shards * (query_weight.shape[1] + HD),
            bytes_accessed=16 * MIB,
            transcendentals=0,
        ),
        name="gather_multiply",
    )(gain, dec_q, dec_len, tokens, prefix, query_weight, kv_weight, cache)


SCATTER_CHUNKS = 8


def attend_kernel(
    q,
    kv,
    dec_q,
    old_share,
    owner,
    seq_of_page,
    live_len,
    tok_hbm,
    wo_hbm,
    out,
    dec_out,
    wo,
    att,
    mine,
    lend,
    borrowed,
    mid,
    near,
    last,
    far_in,
    tok,
    asked,
    answers,
    shares,
    results,
    w_sem,
    lend_send,
    lend_recv,
    mid_send,
    mid_recv,
    near_send,
    near_recv,
    last_send,
    last_recv,
    far_send,
    far_recv,
    ask_send,
    ask_recv,
    answer_send,
    answer_recv,
    share_send,
    share_recv,
    done_send,
    done_recv,
):
    side, ring, core = here()
    rows_all, width = out.shape
    chunk = rows_all // SCATTER_CHUNKS
    half = chunk // 2
    old = kv.shape[1] - rows_all
    n = SCATTER_CHUNKS

    def at(far, step, other=0):
        return shard_at(side, ring, core, far, step, other)

    across, sib, up, down = at(1, 0), at(0, 0, 1), at(0, 1), at(0, 3)
    load = pltpu.make_async_copy(wo_hbm, wo, w_sem.at[0])
    load.start()
    load_tok = pltpu.make_async_copy(tok_hbm, tok, w_sem.at[1])
    load_tok.start()
    shard = lax.axis_index("tp")
    group = lax.axis_index("group")
    shards = 2 * RING * SIDES
    groups = lax.axis_size("group")
    dec_seqs = dec_out.shape[0]
    barrier = pltpu.get_barrier_semaphore()

    def greet_shard(d, carry):
        pl.semaphore_signal(
            barrier, inc=1, device_id={"tp": lax.rem(shard + d, shards)}, device_id_type=MESH
        )
        return carry

    def greet_group(d, carry):
        pl.semaphore_signal(
            barrier, inc=1, device_id={"group": lax.rem(group + d, groups)}, device_id_type=MESH
        )
        return carry

    lax.fori_loop(1, shards, greet_shard, 0)
    lax.fori_loop(1, groups, greet_group, 0)

    def copy_to(src, dst, send_sem, recv_sem, to):
        return pltpu.make_async_remote_copy(
            src_ref=src,
            dst_ref=dst,
            send_sem=send_sem,
            recv_sem=recv_sem,
            device_id=to,
            device_id_type=MESH,
        )

    contract = (((1,), (1,)), ((), ()))
    per = 4 * dec_seqs

    def ask_copy(d):
        to = lax.rem(group + d, groups)
        return copy_to(
            asked.at[group], asked.at[group], ask_send.at[d], ask_recv.at[d], {"group": to}
        )

    def answer_copy(d):
        to = lax.rem(group + d, groups)
        return copy_to(
            answers.at[to],
            shares.at[shards + group],
            answer_send.at[d],
            answer_recv.at[d],
            {"group": to},
        )

    def share_copy(d):
        to = lax.rem(shard + d, shards)
        return copy_to(
            old_share.at[to], shares.at[shard], share_send.at[d], share_recv.at[d], {"tp": to}
        )

    def done_copy(d):
        to = lax.rem(shard + d, shards)
        return copy_to(
            results.at[shard], results.at[shard], done_send.at[d], done_recv.at[d], {"tp": to}
        )

    def each(count, act):
        def body(d, carry):
            act(d)
            return carry

        lax.fori_loop(1, count, body, 0)

    def arrive(count, of, axis, place, send_sem, recv_sem):
        def take(d):
            frm = lax.rem(of + count - d, count)
            ref = place(frm)
            copy_to(ref, ref, send_sem.at[d], recv_sem.at[d], {axis: frm}).wait_recv()

        each(count, take)

    def dec_begin():
        parts = []
        for h in range(4):
            cols = pl.ds(pl.multiple_of(shard * width + h * HD, HD), HD)
            parts.append(dec_q[:, cols].astype(F32))
        asked[group] = jnp.concatenate(parts, axis=0).astype(BF)
        each(groups, lambda d: ask_copy(d).start())
        shares[shard] = old_share[shard]
        each(shards, lambda d: share_copy(d).start())

    def dec_answer():
        arrive(groups, group, "group", lambda frm: asked.at[frm], ask_send, ask_recv)
        count = owner.shape[1]
        old_rows = kv.shape[1] - rows_all
        both = jnp.concatenate(
            [
                jnp.broadcast_to(owner[...], (8, count)),
                jnp.broadcast_to(seq_of_page[...], (8, count)),
            ],
            axis=0,
        ).astype(F32)
        page = lax.broadcasted_iota(jnp.int32, (count, rows_all), 0)
        page_of = lax.broadcasted_iota(jnp.int32, (count, rows_all), 1) // PAGE
        spread = jnp.where(page == page_of, 1.0, 0.0).astype(BF)
        by_token = jnp.dot(both.astype(BF), spread, preferred_element_type=F32).astype(jnp.int32)
        token = lax.broadcasted_iota(jnp.int32, (1, rows_all), 1)
        code = by_token[0:1, :] // shards * dec_seqs + by_token[8:9, :]
        code = jnp.where(token < live_len[0], code, -1)
        row = lax.broadcasted_iota(jnp.int32, (groups * per, rows_all), 0)
        held = code == row // per * dec_seqs + lax.rem(row, dec_seqs)
        query = asked[...].reshape(groups * per, HD)
        score = lax.dot_general(
            query, kv[0, pl.ds(old_rows, rows_all), :], contract, preferred_element_type=F32
        )
        score = jnp.where(held, score * LOG_SCALE, NEG_BIG)
        top = jnp.max(score, axis=-1, keepdims=True)
        expo = jnp.where(held, jnp.exp2(score - top), 0.0)
        total = jnp.sum(expo, axis=-1, keepdims=True)
        accum = jnp.dot(
            expo.astype(BF), kv[1, pl.ds(old_rows, rows_all), :], preferred_element_type=F32
        )
        for g in range(answers.shape[0]):
            write_share(answers.at[g], accum, top, total, g * per)
        shares[shards + group] = answers[group]
        each(groups, lambda d: answer_copy(d).start())

    def dec_combine():
        arrive(shards, shard, "tp", lambda frm: shares.at[frm], share_send, share_recv)
        arrive(
            groups, group, "group", lambda frm: shares.at[shards + frm], answer_send, answer_recv
        )
        stat = shares[:, pl.ds(32, 8), :]
        lane = lax.broadcasted_iota(jnp.int32, stat.shape, 2) // 16
        parts = []
        for h in range(4):
            top = jnp.max(jnp.where(lane == h, stat, NEG_BIG), axis=-1, keepdims=True)
            total = jnp.max(jnp.where(lane == 4 + h, stat, 0.0), axis=-1, keepdims=True)
            factor = jnp.exp2(top - jnp.max(top, axis=0, keepdims=True))
            whole = jnp.sum(factor * total, axis=0)
            accum = jnp.sum(factor * shares[:, pl.ds(h * 8, 8), :], axis=0)
            parts.append(accum / whole)
        results[shard] = jnp.concatenate(parts, axis=0).astype(BF)
        each(shards, lambda d: done_copy(d).start())

    def dec_end():
        arrive(shards, shard, "tp", lambda frm: results.at[frm], done_send, done_recv)
        for t in range(results.shape[0]):
            block = results[t].astype(F32)
            for h in range(4):
                dec_out[:, (t * 4 + h) * HD : (t * 4 + h + 1) * HD] = block[
                    h * 8 : h * 8 + 8
                ].astype(BF)
        for copy in (share_copy, done_copy):
            each(shards, lambda d, copy=copy: copy(d).wait_send())
        for copy in (ask_copy, answer_copy):
            each(groups, lambda d, copy=copy: copy(d).wait_send())

    def rows_of(j):
        return pl.ds(pl.multiple_of(j * chunk, chunk), chunk)

    def half_of(j, k):
        return pl.ds(pl.multiple_of(j * chunk + k * half, half), half)

    def attend(j, plain, edge):
        rows = rows_of(j)
        count = width // HD
        query = q[:, rows, :].reshape(count * chunk, HD)
        row = lax.rem(lax.broadcasted_iota(jnp.int32, (count * chunk, edge), 0), chunk)
        column = lax.broadcasted_iota(jnp.int32, (count * chunk, edge), 1)
        seen = column + plain <= row + old + j * chunk
        first = lax.dot_general(
            query, kv[0, pl.ds(0, plain), :], contract, preferred_element_type=F32
        )
        second = lax.dot_general(
            query, kv[0, pl.ds(plain, edge), :], contract, preferred_element_type=F32
        )
        second = jnp.where(seen, second, NEG_BIG)
        top = jnp.maximum(
            jnp.max(first, axis=-1, keepdims=True), jnp.max(second, axis=-1, keepdims=True)
        )
        first = jnp.exp2(first - top)
        second = jnp.exp2(second - top)
        total = jnp.sum(first, axis=-1, keepdims=True) + jnp.sum(second, axis=-1, keepdims=True)
        value = jnp.dot(
            first.astype(BF), kv[1, pl.ds(0, plain), :], preferred_element_type=F32
        ) + jnp.dot(second.astype(BF), kv[1, pl.ds(plain, edge), :], preferred_element_type=F32)
        value = value / total
        for h in range(count):
            att[:, h * HD : (h + 1) * HD] = value[h * chunk : (h + 1) * chunk].astype(BF)

    def attention(j):
        for pair in range(n // 2):

            @pl.when(j // 2 == pair)
            def _(pair=pair):
                attend(j, old + 2 * pair * chunk, 2 * chunk)

    def term(far, step, other):
        slot = at(far, step, other)
        cols = pl.ds(pl.multiple_of(slot * width, width), width)
        return jnp.dot(att[...], wo[:, cols], preferred_element_type=F32)

    def add_into(dst, src):
        dst[...] = (dst[...].astype(F32) + src[...].astype(F32)).astype(BF)

    def lend_copy(kind, j):
        rows = rows_of(j)
        return pltpu.make_async_remote_copy(
            src_ref=lend.at[kind, rows, :],
            dst_ref=borrowed.at[kind, rows, :],
            send_sem=lend_send.at[kind, j],
            recv_sem=lend_recv.at[kind, j],
            device_id={"tp": sib},
            device_id_type=MESH,
        )

    def mid_copy(way, j):
        rows = half_of(j, way)
        return pltpu.make_async_remote_copy(
            src_ref=mine.at[2, rows, :],
            dst_ref=mid.at[rows, :],
            send_sem=mid_send.at[way, j],
            recv_sem=mid_recv.at[way, j],
            device_id={"tp": down if way else up},
            device_id_type=MESH,
        )

    def far_copy(j):
        rows = rows_of(j)
        return pltpu.make_async_remote_copy(
            src_ref=mine.at[6, rows, :],
            dst_ref=far_in.at[rows, :],
            send_sem=far_send.at[j],
            recv_sem=far_recv.at[j],
            device_id={"tp": across},
            device_id_type=MESH,
        )

    def near_copy(far, way, k, j):
        rows = half_of(j, k)
        return pltpu.make_async_remote_copy(
            src_ref=mine.at[far * 4 + (3 if way else 1), rows, :],
            dst_ref=near.at[far * 2 + way, rows, :],
            send_sem=near_send.at[far * 4 + way * 2 + k, j],
            recv_sem=near_recv.at[far * 4 + way * 2 + k, j],
            device_id={"tp": down if way else up},
            device_id_type=MESH,
        )

    def last_copy(j):
        rows = rows_of(j)
        return pltpu.make_async_remote_copy(
            src_ref=mine.at[4, rows, :],
            dst_ref=last.at[rows, :],
            send_sem=last_send.at[j],
            recv_sem=last_recv.at[j],
            device_id={"tp": across},
            device_id_type=MESH,
        )

    kinds = ((1, 2), (1, 1), (1, 3), (0, 2), (0, 1), (0, 3), (1, 0), (0, 0))
    ahead = 4

    def produce(j):
        rows = rows_of(j)

        def offer(far, step):
            kind = far * 4 + step
            lend[kind, rows, :] = term(far, step, 1).astype(BF)
            lend_copy(kind, j).start()

        for far, step in kinds[:ahead]:
            offer(far, step)
        for k, (far, step) in enumerate(kinds):
            if k + ahead < len(kinds):
                offer(*kinds[k + ahead])
            kind = far * 4 + step
            own = term(far, step, 0)
            lend_copy(kind, j).wait_recv()
            mine[kind, rows, :] = (own + borrowed[kind, rows, :].astype(F32)).astype(BF)
            if (far, step) == (1, 2):
                far_copy(j).start()
            if step == 1:
                near_copy(far, 0, 1, j).start()
                if far:
                    near_copy(far, 0, 0, j).start()
            if step == 3:
                near_copy(far, 1, 0, j).start()
                if far:
                    near_copy(far, 1, 1, j).start()

    def pass_on(j):
        far_copy(j).wait_recv()
        rows = rows_of(j)
        add_into(mine.at[2, rows, :], far_in.at[rows, :])
        mid_copy(0, j).start()
        mid_copy(1, j).start()

    def relay(j):
        for way in (0, 1):
            mid_copy(way, j).wait_recv()
            rows = half_of(j, way)
            add_into(mine.at[3 if way else 1, rows, :], mid.at[rows, :])
            near_copy(0, way, way, j).start()

    def near_wait(far, j):
        for way in (0, 1):
            for k in (0, 1):
                near_copy(far, way, k, j).wait_recv()

    def cross(j):
        near_wait(1, j)
        rows = rows_of(j)
        mine[4, rows, :] = (
            mine[4, rows, :].astype(F32) + near[2, rows, :].astype(F32) + near[3, rows, :].astype(F32)
        ).astype(BF)
        last_copy(j).start()

    def finish(j):
        near_wait(0, j)
        last_copy(j).wait_recv()
        rows = rows_of(j)
        out[rows, :] = (
            tok[rows, :].astype(F32)
            + (
                mine[0, rows, :].astype(F32)
                + near[0, rows, :].astype(F32)
                + near[1, rows, :].astype(F32)
                + last[rows, :].astype(F32)
            )
        ).astype(BF)

    pl.semaphore_wait(barrier, shards + groups - 2)
    dec_begin()
    attend(0, old, 2 * chunk)

    def turn(j, carry):
        @pl.when((j >= 1) & (j < n))
        def _():
            attention(j)

        @pl.when(j == 0)
        def _():
            load.wait()
            load_tok.wait()

        @pl.when((j >= 1) & (j < n + 1))
        def _():
            pass_on(j - 1)

        @pl.when(j < n)
        def _():
            produce(j)

        @pl.when((j >= 2) & (j < n + 2))
        def _():
            relay(j - 2)

        @pl.when((j >= 3) & (j < n + 3))
        def _():
            cross(j - 3)

        @pl.when(j >= 4)
        def _():
            finish(j - 4)

        @pl.when(j == 1)
        def _():
            dec_answer()

        @pl.when(j == 4)
        def _():
            dec_combine()

        @pl.when(j == 8)
        def _():
            dec_end()

        return carry

    lax.fori_loop(0, n + 4, turn, 0)

    def drain(j, carry):
        for kind in range(8):
            lend_copy(kind, j).wait_send()
        for far in (0, 1):
            for way in (0, 1):
                for k in (0, 1):
                    near_copy(far, way, k, j).wait_send()
        last_copy(j).wait_send()
        far_copy(j).wait_send()
        mid_copy(0, j).wait_send()
        mid_copy(1, j).wait_send()
        return carry

    lax.fori_loop(0, n, drain, 0)


def attend_scatter(
    tokens, queries, kv, dec_q, old_share, owner, seq_of_page, live_len, out_weight, groups
):
    rows, width = tokens.shape
    vmem = pl.BlockSpec(memory_space=pltpu.VMEM)
    dma = pltpu.SemaphoreType.DMA
    n = SCATTER_CHUNKS
    seqs = dec_q.shape[0]
    shards = 2 * RING * SIDES
    return pl.pallas_call(
        attend_kernel,
        out_shape=(
            jax.ShapeDtypeStruct((rows, width), BF),
            jax.ShapeDtypeStruct((seqs, HEADS * HD), BF),
        ),
        in_specs=[
            vmem,
            vmem,
            vmem,
            vmem,
            vmem,
            vmem,
            pl.BlockSpec(memory_space=pltpu.SMEM),
            pl.BlockSpec(memory_space=pltpu.HBM),
            pl.BlockSpec(memory_space=pltpu.HBM),
        ],
        out_specs=(vmem, vmem),
        scratch_shapes=[
            pltpu.VMEM(out_weight.shape, BF),
            pltpu.VMEM((rows // n, width), BF),
            pltpu.VMEM((8, rows, width), BF),
            pltpu.VMEM((8, rows, width), BF),
            pltpu.VMEM((8, rows, width), BF),
            pltpu.VMEM((rows, width), BF),
            pltpu.VMEM((4, rows, width), BF),
            pltpu.VMEM((rows, width), BF),
            pltpu.VMEM((rows, width), BF),
            pltpu.VMEM((rows, width), BF),
            pltpu.VMEM((groups, 4 * seqs, HD), BF),
            pltpu.VMEM((groups, SHARE_ROWS, HD), F32),
            pltpu.VMEM((shards + groups, SHARE_ROWS, HD), F32),
            pltpu.VMEM((shards, 4 * seqs, HD), BF),
            dma((2,)),
            dma((8, n)),
            dma((8, n)),
            dma((2, n)),
            dma((2, n)),
            dma((8, n)),
            dma((8, n)),
            dma((n,)),
            dma((n,)),
            dma((n,)),
            dma((n,)),
            dma((groups,)),
            dma((groups,)),
            dma((groups,)),
            dma((groups,)),
            dma((shards,)),
            dma((shards,)),
            dma((shards,)),
            dma((shards,)),
        ],
        compiler_params=pltpu.CompilerParams(
            collective_id=2, has_side_effects=True, vmem_limit_bytes=62 * MIB
        ),
        cost_estimate=pl.CostEstimate(
            flops=2 * rows * width * out_weight.shape[1] * 2,
            bytes_accessed=12 * MIB,
            transcendentals=4 * rows * kv.shape[1],
        ),
        name="attend_scatter",
    )(queries, kv, dec_q, old_share, owner, seq_of_page, live_len, tokens, out_weight)


def hand_on_kernel(hidden, dec, hidden_out, dec_out, sem):
    first = pltpu.make_async_copy(hidden, hidden_out, sem.at[0])
    second = pltpu.make_async_copy(dec, dec_out, sem.at[1])
    first.start()
    second.start()
    first.wait()
    second.wait()


def hand_on(hidden, dec):
    vmem = pl.BlockSpec(memory_space=pltpu.VMEM)
    hbm = pl.BlockSpec(memory_space=pltpu.HBM)
    return pl.pallas_call(
        hand_on_kernel,
        out_shape=(
            jax.ShapeDtypeStruct(hidden.shape, hidden.dtype),
            jax.ShapeDtypeStruct(dec.shape, dec.dtype),
        ),
        in_specs=[vmem, vmem],
        out_specs=(hbm, hbm),
        scratch_shapes=[pltpu.SemaphoreType.DMA((2,))],
        name="hand_on",
    )(hidden, dec)


def per_device(
    tokens,
    norm_gain,
    query_weight,
    kv_weight,
    out_weight,
    prefix_cache,
    prompt_len,
    page_owner,
    page_seq,
    dec_queries,
    dec_cache,
    dec_len,
):
    queries, kv_both, old_share = gather_multiply(
        tokens, norm_gain, prefix_cache, query_weight, kv_weight, dec_queries, dec_len, dec_cache
    )
    hidden_out, dec_out = attend_scatter(
        tokens,
        queries,
        kv_both,
        dec_queries,
        old_share,
        page_owner.reshape(1, -1),
        page_seq.reshape(1, -1),
        prompt_len,
        out_weight,
        lax.axis_size("group"),
    )
    return hand_on(hidden_out, dec_out)


def solution(mesh):
    return jax.shard_map(
        per_device,
        mesh=mesh,
        in_specs=(
            P("group", "tp"),
            P(None, "tp"),
            P(None, "tp"),
            P(None, "tp"),
            P("tp", None),
            P("group", "tp"),
            P("group"),
            P("group", None),
            P("group"),
            P("group", None),
            P("group", "tp", None),
            P("group"),
        ),
        out_specs=(P("group", "tp"), P("group", None)),
        check_vma=False,
    )
```

```python
import math

import jax
import jax.numpy as jnp
from jax import lax
from jax.experimental import pallas as pl
from jax.experimental.pallas import tpu as pltpu
from jax.sharding import PartitionSpec as P

HEADS = 64
KVH = 8
HD = 128
PAGE = 4


EPSILON = 1e-05
NEG_BIG = -1e30


MESH = pl.DeviceIdType.MESH
BF = jnp.bfloat16
F32 = jnp.float32
MIB = 1024 * 1024
SIDES = 2
RING = 4


def here():
    t = lax.axis_index("tp")
    return t // (RING * 2), lax.rem(t // 2, RING), lax.rem(t, 2)


def shard_at(side, ring, core, far, step, other):
    s = lax.rem(side + far, SIDES)
    r = lax.rem(ring + step, RING)
    c = lax.rem(core + other, 2)
    return (s * RING + r) * 2 + c


def push(src, dst, send_sem, recv_sem, to):
    copy = pltpu.make_async_remote_copy(
        src_ref=src,
        dst_ref=dst,
        send_sem=send_sem,
        recv_sem=recv_sem,
        device_id={"tp": to},
        device_id_type=MESH,
    )
    copy.start()
    return copy


def landed(ref, recv_sem, to):
    pltpu.make_async_remote_copy(
        src_ref=ref,
        dst_ref=ref,
        send_sem=recv_sem,
        recv_sem=recv_sem,
        device_id={"tp": to},
        device_id_type=MESH,
    ).wait_recv()


def greet(peers):
    barrier = pltpu.get_barrier_semaphore()
    for peer in peers:
        pl.semaphore_signal(barrier, inc=1, device_id={"tp": peer}, device_id_type=MESH)
    pl.semaphore_wait(barrier, len(peers))


GATHER_CHUNKS = 4
GAIN_ROWS = 16
SHARE_ROWS = 40
LOG_SCALE = math.log2(math.e) / math.sqrt(HD)


def write_share(share, accum, top, total, low):
    lane = lax.broadcasted_iota(jnp.int32, (8, HD), 1) // 16
    stat = jnp.zeros((8, HD), F32)
    for h in range(4):
        rows = slice(low + h * 8, low + h * 8 + 8)
        stat = jnp.where(lane == h, top[rows], stat)
        stat = jnp.where(lane == 4 + h, total[rows], stat)
    share[pl.ds(0, 32), :] = accum[low : low + 32]
    share[pl.ds(32, 8), :] = stat


def gather_kernel(
    gain,
    dec_q,
    dec_len,
    tok,
    prefix,
    qw_hbm,
    kw_hbm,
    cache_hbm,
    q_out,
    kv_out,
    old_share,
    xall,
    cache,
    qw,
    kw,
    acc_q,
    acc_k,
    power,
    w_sem,
    recv_sem,
    sib_sem,
    x_send,
    up_send,
    down_send,
    sib_send,
    kv_send,
    kv_recv,
    split_send,
    split_recv,
):
    side, ring, core = here()
    rows_all, width = tok.shape
    chunk = rows_all // GATHER_CHUNKS

    def at(far, step, other=0):
        return shard_at(side, ring, core, far, step, other)

    me, across, sib = at(0, 0), at(1, 0), at(0, 0, 1)
    up, down = at(0, 1), at(0, 3)

    load_q = pltpu.make_async_copy(qw_hbm, qw, w_sem.at[0])
    load_k = pltpu.make_async_copy(kw_hbm, kw, w_sem.at[1])
    prefix_rows = prefix.shape[0]
    load_x = pltpu.make_async_copy(tok, xall.at[me, pl.ds(GAIN_ROWS, rows_all), :], w_sem.at[2])
    load_x.start()
    load_p = pltpu.make_async_copy(prefix, kv_out.at[core, pl.ds(0, prefix_rows), :], w_sem.at[3])
    load_p.start()
    load_q.start()
    load_k.start()
    load_cache = pltpu.make_async_copy(cache_hbm, cache, w_sem.at[4])
    load_cache.start()
    xall[me, pl.ds(0, GAIN_ROWS), :] = jnp.broadcast_to(gain[...], (GAIN_ROWS, width))
    acc_q[...] = jnp.zeros_like(acc_q)
    acc_k[...] = jnp.zeros_like(acc_k)
    power[...] = jnp.zeros_like(power)
    greet((across, up, down, sib))
    load_x.wait()

    sends = []
    split = GATHER_CHUNKS - 1

    def span(i, half=None):
        low = 0 if i == 0 else GAIN_ROWS + i * chunk
        high = GAIN_ROWS + (i + 1) * chunk
        middle = high - chunk // 2
        if half == 0:
            high = middle
        if half == 1:
            low = middle
        return pl.ds(low, high - low)

    def send(slot, rows, send_sem, there_sem, to):
        ref = xall.at[slot, rows, :]
        sends.append(push(ref, ref, send_sem, there_sem, to))

    def to_sibling(far, step, i):
        kind = far * 4 + step
        send(at(far, step), span(i), sib_send.at[kind, i], sib_sem.at[kind, i], sib)

    def multiply(slot, i):
        rows = pl.ds(i * chunk, chunk)
        wide = xall[slot, pl.ds(GAIN_ROWS + i * chunk, chunk), :].astype(F32)
        weight = xall[slot, pl.ds(0, 1), :].astype(F32)
        square = wide * wide
        part = square[:, 0:HD]
        for k in range(1, width // HD):
            part = part + square[:, k * HD : (k + 1) * HD]
        power[rows, :] += part
        scaled = (wide * weight).astype(BF)
        depth = pl.ds(pl.multiple_of(slot * width, width), width)
        acc_q[rows, :] += jnp.dot(scaled, qw[depth, :], preferred_element_type=F32)
        acc_k[rows, :] += jnp.dot(scaled, kw[depth, :], preferred_element_type=F32)

    def from_sibling(far, step, i):
        kind = far * 4 + step
        slot = at(far, step, 1)
        landed(xall.at[slot, span(i), :], sib_sem.at[kind, i], sib)
        multiply(slot, i)

    def got(far, step, i):
        kind = far * 4 + step
        slot = at(far, step)
        if step == 2 and far == 0:
            landed(xall.at[slot, span(i, 0), :], recv_sem.at[kind, i], down)
            landed(xall.at[slot, span(i, 1), :], recv_sem.at[8, i], up)
        elif i == split and far == 1 and step in (1, 3):
            landed(xall.at[slot, span(i, 0), :], recv_sem.at[kind, i], up)
            landed(xall.at[slot, span(i, 1), :], split_recv.at[step // 2], across)
        else:
            landed(xall.at[slot, span(i), :], recv_sem.at[kind, i], up)

    for i in range(GATHER_CHUNKS):
        send(me, span(i), x_send.at[i], recv_sem.at[4, i], across)
        send(me, span(i), up_send.at[0, i], recv_sem.at[3, i], up)
        send(me, span(i), down_send.at[0, i], recv_sem.at[1, i], down)
        to_sibling(0, 0, i)
    load_p.wait()
    early = kv_out.at[core, pl.ds(0, prefix_rows), :]
    sends.append(push(early, early, kv_send.at[0], kv_recv.at[0], sib))
    load_q.wait()
    load_k.wait()
    load_cache.wait()
    dec_seqs, ctx = cache.shape[0], cache.shape[1]
    contract = (((1,), (1,)), ((), ()))

    def dec_old(k):
        count = dec_seqs * 8
        seq_row = lax.rem(lax.broadcasted_iota(jnp.int32, (count, ctx), 0), 8)
        position = lax.broadcasted_iota(jnp.int32, (count, ctx), 1) + me * ctx
        parts = [dec_q[:, pl.ds((k * 8 + h) * HD, HD)].astype(F32) for h in range(8)]
        query = jnp.concatenate(parts, axis=0).astype(BF)
        found = jnp.full((count, ctx), NEG_BIG, F32)
        for seq in range(dec_seqs):
            score = lax.dot_general(
                query,
                cache[seq, :, pl.ds(2 * k * HD, HD)],
                contract,
                preferred_element_type=F32,
            )
            valid = (position < dec_len[seq]) & (seq_row == seq)
            found = jnp.where(valid, score * LOG_SCALE, found)
        top = jnp.max(found, axis=-1, keepdims=True)
        expo = jnp.where(found > 0.5 * NEG_BIG, jnp.exp2(found - top), 0.0)
        accum = jnp.zeros((count, HD), F32)
        for seq in range(dec_seqs):
            own = jnp.where(seq_row == seq, expo, 0.0).astype(BF)
            accum = accum + jnp.dot(
                own, cache[seq, :, pl.ds((2 * k + 1) * HD, HD)], preferred_element_type=F32
            )
        total = jnp.sum(expo, axis=-1, keepdims=True)
        for part in range(2):
            write_share(old_share.at[2 * k + part], accum, top, total, part * 32)

    def event(name, i):
        if name == "O":
            multiply(me, i)
            return [(0, 0, i)]
        if name == "X":
            got(1, 0, i)
            rows = span(i, 0) if i == split else span(i)
            send(across, rows, up_send.at[1, i], recv_sem.at[7, i], up)
            send(across, rows, down_send.at[1, i], recv_sem.at[5, i], down)
            to_sibling(1, 0, i)
            multiply(across, i)
            return [(1, 0, i)]
        far = 0 if name in ("Z", "F") else 1
        if name in ("Z", "P"):
            got(far, 3, i)
            if far == 0:
                send(at(0, 3), span(i, 0), up_send.at[2, i], recv_sem.at[2, i], up)
                if i == split:
                    send(at(0, 3), span(i, 1), split_send.at[1], split_recv.at[1], across)
            got(far, 1, i)
            if far == 0:
                send(at(0, 1), span(i, 1), down_send.at[2, i], recv_sem.at[8, i], down)
                if i == split:
                    send(at(0, 1), span(i, 1), split_send.at[0], split_recv.at[0], across)
            to_sibling(far, 3, i)
            to_sibling(far, 1, i)
            multiply(at(far, 3), i)
            multiply(at(far, 1), i)
            return [(far, 3, i), (far, 1, i)]
        got(far, 2, i)
        if far == 0:
            send(at(0, 2), span(i), x_send.at[GATHER_CHUNKS + i], recv_sem.at[6, i], across)
        to_sibling(far, 2, i)
        multiply(at(far, 2), i)
        return [(far, 2, i)]

    order = (
        ("O", 0), ("O", 1), ("O", 2), ("O", 3), ("Z", 0), ("Z", 1), ("Z", 2), ("Z", 3),
        ("X", 0), ("X", 1), ("X", 2), ("X", 3), ("F", 0), ("F", 1), ("F", 2), ("F", 3),
        ("P", 0), ("P", 1), ("G", 0), ("P", 2), ("G", 1), ("G", 2), ("P", 3), ("G", 3),
    )
    def settle(i):
        rows = pl.ds(i * chunk, chunk)
        total = jnp.sum(power[rows, :], axis=-1, keepdims=True) / (width * 2 * RING * SIDES)
        factor = lax.rsqrt(total + EPSILON)
        new = pl.ds(prefix_rows + i * chunk, chunk)
        kv_out[core, new, :] = (acc_k[rows, :] * factor).astype(BF)
        ref = kv_out.at[core, new, :]
        sends.append(push(ref, ref, kv_send.at[1 + i], kv_recv.at[1 + i], sib))
        queries = (acc_q[rows, :] * (factor * LOG_SCALE)).astype(BF)
        for h in range(q_out.shape[0]):
            q_out[h, rows, :] = queries[:, h * HD : (h + 1) * HD]

    late = []
    for name, i in order:
        fresh = event(name, i)
        if name in ("Z", "X"):
            dec_old(i + (4 if name == "X" else 0))
        for item in late:
            from_sibling(*item)
        for far, step, k in late:
            if (far, step) == (1, 2):
                settle(k)
        late = fresh
    for item in late:
        from_sibling(*item)
    settle(GATHER_CHUNKS - 1)
    landed(kv_out.at[1 - core, pl.ds(0, prefix_rows), :], kv_recv.at[0], sib)
    for i in range(GATHER_CHUNKS):
        new = pl.ds(prefix_rows + i * chunk, chunk)
        landed(kv_out.at[1 - core, new, :], kv_recv.at[1 + i], sib)
    for copy in sends:
        copy.wait_send()


def gather_multiply(tokens, gain, prefix, query_weight, kv_weight, dec_q, dec_len, cache):
    rows, width = tokens.shape
    shards = 2 * RING * SIDES
    kv_rows = prefix.shape[0] + rows
    vmem = pl.BlockSpec(memory_space=pltpu.VMEM)
    dma = pltpu.SemaphoreType.DMA
    n = GATHER_CHUNKS
    return pl.pallas_call(
        gather_kernel,
        out_shape=(
            jax.ShapeDtypeStruct((query_weight.shape[1] // HD, rows, HD), BF),
            jax.ShapeDtypeStruct((2, kv_rows, HD), BF),
            jax.ShapeDtypeStruct((shards, SHARE_ROWS, HD), F32),
        ),
        in_specs=[vmem, vmem, pl.BlockSpec(memory_space=pltpu.SMEM)]
        + [pl.BlockSpec(memory_space=pltpu.HBM)] * 5,
        out_specs=(vmem,) * 3,
        scratch_shapes=[
            pltpu.VMEM((shards, rows + GAIN_ROWS, width), BF),
            pltpu.VMEM(cache.shape, BF),
            pltpu.VMEM(query_weight.shape, BF),
            pltpu.VMEM(kv_weight.shape, BF),
            pltpu.VMEM((rows, query_weight.shape[1]), F32),
            pltpu.VMEM((rows, HD), F32),
            pltpu.VMEM((rows, HD), F32),
            dma((5,)),
            dma((9, n)),
            dma((8, n)),
            dma((2 * n,)),
            dma((3, n)),
            dma((3, n)),
            dma((8, n)),
            dma((n + 1,)),
            dma((n + 1,)),
            dma((2,)),
            dma((2,)),
        ],
        compiler_params=pltpu.CompilerParams(
            collective_id=1, has_side_effects=True, vmem_limit_bytes=62 * MIB
        ),
        cost_estimate=pl.CostEstimate(
            flops=2 * rows * width * shards * (query_weight.shape[1] + HD),
            bytes_accessed=16 * MIB,
            transcendentals=0,
        ),
        name="gather_multiply",
    )(gain, dec_q, dec_len, tokens, prefix, query_weight, kv_weight, cache)


SCATTER_CHUNKS = 8


def attend_kernel(
    q,
    kv,
    dec_q,
    old_share,
    owner,
    seq_of_page,
    live_len,
    tok_hbm,
    wo_hbm,
    out,
    dec_out,
    wo,
    att,
    mine,
    lend,
    borrowed,
    mid,
    near,
    last,
    far_in,
    tok,
    asked,
    answers,
    shares,
    results,
    w_sem,
    lend_send,
    lend_recv,
    mid_send,
    mid_recv,
    near_send,
    near_recv,
    last_send,
    last_recv,
    far_send,
    far_recv,
    ask_send,
    ask_recv,
    answer_send,
    answer_recv,
    share_send,
    share_recv,
    done_send,
    done_recv,
):
    side, ring, core = here()
    rows_all, width = out.shape
    chunk = rows_all // SCATTER_CHUNKS
    half = chunk // 2
    old = kv.shape[1] - rows_all
    n = SCATTER_CHUNKS

    def at(far, step, other=0):
        return shard_at(side, ring, core, far, step, other)

    across, sib, up, down = at(1, 0), at(0, 0, 1), at(0, 1), at(0, 3)
    load = pltpu.make_async_copy(wo_hbm, wo, w_sem.at[0])
    load.start()
    load_tok = pltpu.make_async_copy(tok_hbm, tok, w_sem.at[1])
    load_tok.start()
    shard = lax.axis_index("tp")
    group = lax.axis_index("group")
    shards = 2 * RING * SIDES
    groups = lax.axis_size("group")
    dec_seqs = dec_out.shape[0]
    barrier = pltpu.get_barrier_semaphore()

    def greet_shard(d, carry):
        pl.semaphore_signal(
            barrier, inc=1, device_id={"tp": lax.rem(shard + d, shards)}, device_id_type=MESH
        )
        return carry

    def greet_group(d, carry):
        pl.semaphore_signal(
            barrier, inc=1, device_id={"group": lax.rem(group + d, groups)}, device_id_type=MESH
        )
        return carry

    lax.fori_loop(1, shards, greet_shard, 0)
    lax.fori_loop(1, groups, greet_group, 0)

    def copy_to(src, dst, send_sem, recv_sem, to):
        return pltpu.make_async_remote_copy(
            src_ref=src,
            dst_ref=dst,
            send_sem=send_sem,
            recv_sem=recv_sem,
            device_id=to,
            device_id_type=MESH,
        )

    contract = (((1,), (1,)), ((), ()))
    per = 4 * dec_seqs

    def ask_copy(d):
        to = lax.rem(group + d, groups)
        return copy_to(
            asked.at[group], asked.at[group], ask_send.at[d], ask_recv.at[d], {"group": to}
        )

    def answer_copy(d):
        to = lax.rem(group + d, groups)
        return copy_to(
            answers.at[to],
            shares.at[shards + group],
            answer_send.at[d],
            answer_recv.at[d],
            {"group": to},
        )

    def share_copy(d):
        to = lax.rem(shard + d, shards)
        return copy_to(
            old_share.at[to], shares.at[shard], share_send.at[d], share_recv.at[d], {"tp": to}
        )

    def done_copy(d):
        to = lax.rem(shard + d, shards)
        return copy_to(
            results.at[shard], results.at[shard], done_send.at[d], done_recv.at[d], {"tp": to}
        )

    def each(count, act):
        def body(d, carry):
            act(d)
            return carry

        lax.fori_loop(1, count, body, 0)

    def arrive(count, of, axis, place, send_sem, recv_sem):
        def take(d):
            frm = lax.rem(of + count - d, count)
            ref = place(frm)
            copy_to(ref, ref, send_sem.at[d], recv_sem.at[d], {axis: frm}).wait_recv()

        each(count, take)

    def dec_begin():
        parts = []
        for h in range(4):
            cols = pl.ds(pl.multiple_of(shard * width + h * HD, HD), HD)
            parts.append(dec_q[:, cols].astype(F32))
        asked[group] = jnp.concatenate(parts, axis=0).astype(BF)
        each(groups, lambda d: ask_copy(d).start())
        shares[shard] = old_share[shard]
        each(shards, lambda d: share_copy(d).start())

    def dec_answer():
        arrive(groups, group, "group", lambda frm: asked.at[frm], ask_send, ask_recv)
        count = owner.shape[1]
        old_rows = kv.shape[1] - rows_all
        both = jnp.concatenate(
            [
                jnp.broadcast_to(owner[...], (8, count)),
                jnp.broadcast_to(seq_of_page[...], (8, count)),
            ],
            axis=0,
        ).astype(F32)
        page = lax.broadcasted_iota(jnp.int32, (count, rows_all), 0)
        page_of = lax.broadcasted_iota(jnp.int32, (count, rows_all), 1) // PAGE
        spread = jnp.where(page == page_of, 1.0, 0.0).astype(BF)
        by_token = jnp.dot(both.astype(BF), spread, preferred_element_type=F32).astype(jnp.int32)
        token = lax.broadcasted_iota(jnp.int32, (1, rows_all), 1)
        code = by_token[0:1, :] // shards * dec_seqs + by_token[8:9, :]
        code = jnp.where(token < live_len[0], code, -1)
        row = lax.broadcasted_iota(jnp.int32, (groups * per, rows_all), 0)
        held = code == row // per * dec_seqs + lax.rem(row, dec_seqs)
        query = asked[...].reshape(groups * per, HD)
        score = lax.dot_general(
            query, kv[0, pl.ds(old_rows, rows_all), :], contract, preferred_element_type=F32
        )
        score = jnp.where(held, score * LOG_SCALE, NEG_BIG)
        top = jnp.max(score, axis=-1, keepdims=True)
        expo = jnp.where(held, jnp.exp2(score - top), 0.0)
        total = jnp.sum(expo, axis=-1, keepdims=True)
        accum = jnp.dot(
            expo.astype(BF), kv[1, pl.ds(old_rows, rows_all), :], preferred_element_type=F32
        )
        for g in range(answers.shape[0]):
            write_share(answers.at[g], accum, top, total, g * per)
        shares[shards + group] = answers[group]
        each(groups, lambda d: answer_copy(d).start())

    def dec_combine():
        arrive(shards, shard, "tp", lambda frm: shares.at[frm], share_send, share_recv)
        arrive(
            groups, group, "group", lambda frm: shares.at[shards + frm], answer_send, answer_recv
        )
        stat = shares[:, pl.ds(32, 8), :]
        lane = lax.broadcasted_iota(jnp.int32, stat.shape, 2) // 16
        parts = []
        for h in range(4):
            top = jnp.max(jnp.where(lane == h, stat, NEG_BIG), axis=-1, keepdims=True)
            total = jnp.max(jnp.where(lane == 4 + h, stat, 0.0), axis=-1, keepdims=True)
            factor = jnp.exp2(top - jnp.max(top, axis=0, keepdims=True))
            whole = jnp.sum(factor * total, axis=0)
            accum = jnp.sum(factor * shares[:, pl.ds(h * 8, 8), :], axis=0)
            parts.append(accum / whole)
        results[shard] = jnp.concatenate(parts, axis=0).astype(BF)
        each(shards, lambda d: done_copy(d).start())

    def dec_end():
        arrive(shards, shard, "tp", lambda frm: results.at[frm], done_send, done_recv)
        for t in range(results.shape[0]):
            block = results[t].astype(F32)
            for h in range(4):
                dec_out[:, (t * 4 + h) * HD : (t * 4 + h + 1) * HD] = block[
                    h * 8 : h * 8 + 8
                ].astype(BF)
        for copy in (share_copy, done_copy):
            each(shards, lambda d, copy=copy: copy(d).wait_send())
        for copy in (ask_copy, answer_copy):
            each(groups, lambda d, copy=copy: copy(d).wait_send())

    def rows_of(j):
        return pl.ds(pl.multiple_of(j * chunk, chunk), chunk)

    def half_of(j, k):
        return pl.ds(pl.multiple_of(j * chunk + k * half, half), half)

    def attend(j, plain, edge):
        rows = rows_of(j)
        count = width // HD
        query = q[:, rows, :].reshape(count * chunk, HD)
        row = lax.rem(lax.broadcasted_iota(jnp.int32, (count * chunk, edge), 0), chunk)
        column = lax.broadcasted_iota(jnp.int32, (count * chunk, edge), 1)
        seen = column + plain <= row + old + j * chunk
        first = lax.dot_general(
            query, kv[0, pl.ds(0, plain), :], contract, preferred_element_type=F32
        )
        second = lax.dot_general(
            query, kv[0, pl.ds(plain, edge), :], contract, preferred_element_type=F32
        )
        second = jnp.where(seen, second, NEG_BIG)
        top = jnp.maximum(
            jnp.max(first, axis=-1, keepdims=True), jnp.max(second, axis=-1, keepdims=True)
        )
        first = jnp.exp2(first - top)
        second = jnp.exp2(second - top)
        total = jnp.sum(first, axis=-1, keepdims=True) + jnp.sum(second, axis=-1, keepdims=True)
        value = jnp.dot(
            first.astype(BF), kv[1, pl.ds(0, plain), :], preferred_element_type=F32
        ) + jnp.dot(second.astype(BF), kv[1, pl.ds(plain, edge), :], preferred_element_type=F32)
        value = value / total
        for h in range(count):
            att[:, h * HD : (h + 1) * HD] = value[h * chunk : (h + 1) * chunk].astype(BF)

    def attention(j):
        for pair in range(n // 2):

            @pl.when(j // 2 == pair)
            def _(pair=pair):
                attend(j, old + 2 * pair * chunk, 2 * chunk)

    def term(far, step, other):
        slot = at(far, step, other)
        cols = pl.ds(pl.multiple_of(slot * width, width), width)
        return jnp.dot(att[...], wo[:, cols], preferred_element_type=F32)

    def add_into(dst, src):
        dst[...] = (dst[...].astype(F32) + src[...].astype(F32)).astype(BF)

    def lend_copy(kind, j):
        rows = rows_of(j)
        return pltpu.make_async_remote_copy(
            src_ref=lend.at[kind, rows, :],
            dst_ref=borrowed.at[kind, rows, :],
            send_sem=lend_send.at[kind, j],
            recv_sem=lend_recv.at[kind, j],
            device_id={"tp": sib},
            device_id_type=MESH,
        )

    def mid_copy(way, j):
        rows = half_of(j, way)
        return pltpu.make_async_remote_copy(
            src_ref=mine.at[2, rows, :],
            dst_ref=mid.at[rows, :],
            send_sem=mid_send.at[way, j],
            recv_sem=mid_recv.at[way, j],
            device_id={"tp": down if way else up},
            device_id_type=MESH,
        )

    def far_copy(j):
        rows = rows_of(j)
        return pltpu.make_async_remote_copy(
            src_ref=mine.at[6, rows, :],
            dst_ref=far_in.at[rows, :],
            send_sem=far_send.at[j],
            recv_sem=far_recv.at[j],
            device_id={"tp": across},
            device_id_type=MESH,
        )

    def near_copy(far, way, k, j):
        rows = half_of(j, k)
        return pltpu.make_async_remote_copy(
            src_ref=mine.at[far * 4 + (3 if way else 1), rows, :],
            dst_ref=near.at[far * 2 + way, rows, :],
            send_sem=near_send.at[far * 4 + way * 2 + k, j],
            recv_sem=near_recv.at[far * 4 + way * 2 + k, j],
            device_id={"tp": down if way else up},
            device_id_type=MESH,
        )

    def last_copy(j):
        rows = rows_of(j)
        return pltpu.make_async_remote_copy(
            src_ref=mine.at[4, rows, :],
            dst_ref=last.at[rows, :],
            send_sem=last_send.at[j],
            recv_sem=last_recv.at[j],
            device_id={"tp": across},
            device_id_type=MESH,
        )

    kinds = ((1, 2), (1, 1), (1, 3), (0, 2), (0, 1), (0, 3), (1, 0), (0, 0))
    ahead = 4

    def produce(j):
        rows = rows_of(j)

        def offer(far, step):
            kind = far * 4 + step
            lend[kind, rows, :] = term(far, step, 1).astype(BF)
            lend_copy(kind, j).start()

        for far, step in kinds[:ahead]:
            offer(far, step)
        for k, (far, step) in enumerate(kinds):
            if k + ahead < len(kinds):
                offer(*kinds[k + ahead])
            kind = far * 4 + step
            own = term(far, step, 0)
            lend_copy(kind, j).wait_recv()
            mine[kind, rows, :] = (own + borrowed[kind, rows, :].astype(F32)).astype(BF)
            if (far, step) == (1, 2):
                far_copy(j).start()
            if step == 1:
                near_copy(far, 0, 1, j).start()
                if far:
                    near_copy(far, 0, 0, j).start()
            if step == 3:
                near_copy(far, 1, 0, j).start()
                if far:
                    near_copy(far, 1, 1, j).start()

    def pass_on(j):
        far_copy(j).wait_recv()
        rows = rows_of(j)
        add_into(mine.at[2, rows, :], far_in.at[rows, :])
        mid_copy(0, j).start()
        mid_copy(1, j).start()

    def relay(j):
        for way in (0, 1):
            mid_copy(way, j).wait_recv()
            rows = half_of(j, way)
            add_into(mine.at[3 if way else 1, rows, :], mid.at[rows, :])
            near_copy(0, way, way, j).start()

    def near_wait(far, j):
        for way in (0, 1):
            for k in (0, 1):
                near_copy(far, way, k, j).wait_recv()

    def cross(j):
        near_wait(1, j)
        rows = rows_of(j)
        mine[4, rows, :] = (
            mine[4, rows, :].astype(F32) + near[2, rows, :].astype(F32) + near[3, rows, :].astype(F32)
        ).astype(BF)
        last_copy(j).start()

    def finish(j):
        near_wait(0, j)
        last_copy(j).wait_recv()
        rows = rows_of(j)
        out[rows, :] = (
            tok[rows, :].astype(F32)
            + (
                mine[0, rows, :].astype(F32)
                + near[0, rows, :].astype(F32)
                + near[1, rows, :].astype(F32)
                + last[rows, :].astype(F32)
            )
        ).astype(BF)

    attend(0, old, 2 * chunk)
    pl.semaphore_wait(barrier, shards + groups - 2)

    def turn(j, carry):
        @pl.when((j >= 1) & (j < n))
        def _():
            attention(j)

        @pl.when(j == 0)
        def _():
            load.wait()
            load_tok.wait()

        @pl.when((j >= 1) & (j < n + 1))
        def _():
            pass_on(j - 1)

        @pl.when(j < n)
        def _():
            produce(j)

        @pl.when((j >= 2) & (j < n + 2))
        def _():
            relay(j - 2)

        @pl.when((j >= 3) & (j < n + 3))
        def _():
            cross(j - 3)

        @pl.when(j >= 4)
        def _():
            finish(j - 4)

        @pl.when(j == 0)
        def _():
            dec_begin()

        @pl.when(j == 2)
        def _():
            dec_answer()

        @pl.when(j == 5)
        def _():
            dec_combine()

        @pl.when(j == 8)
        def _():
            dec_end()

        return carry

    lax.fori_loop(0, n + 4, turn, 0)

    def drain(j, carry):
        for kind in range(8):
            lend_copy(kind, j).wait_send()
        for far in (0, 1):
            for way in (0, 1):
                for k in (0, 1):
                    near_copy(far, way, k, j).wait_send()
        last_copy(j).wait_send()
        far_copy(j).wait_send()
        mid_copy(0, j).wait_send()
        mid_copy(1, j).wait_send()
        return carry

    lax.fori_loop(0, n, drain, 0)


def attend_scatter(
    tokens, queries, kv, dec_q, old_share, owner, seq_of_page, live_len, out_weight, groups
):
    rows, width = tokens.shape
    vmem = pl.BlockSpec(memory_space=pltpu.VMEM)
    dma = pltpu.SemaphoreType.DMA
    n = SCATTER_CHUNKS
    seqs = dec_q.shape[0]
    shards = 2 * RING * SIDES
    return pl.pallas_call(
        attend_kernel,
        out_shape=(
            jax.ShapeDtypeStruct((rows, width), BF),
            jax.ShapeDtypeStruct((seqs, HEADS * HD), BF),
        ),
        in_specs=[
            vmem,
            vmem,
            vmem,
            vmem,
            vmem,
            vmem,
            pl.BlockSpec(memory_space=pltpu.SMEM),
            pl.BlockSpec(memory_space=pltpu.HBM),
            pl.BlockSpec(memory_space=pltpu.HBM),
        ],
        out_specs=(vmem, vmem),
        scratch_shapes=[
            pltpu.VMEM(out_weight.shape, BF),
            pltpu.VMEM((rows // n, width), BF),
            pltpu.VMEM((8, rows, width), BF),
            pltpu.VMEM((8, rows, width), BF),
            pltpu.VMEM((8, rows, width), BF),
            pltpu.VMEM((rows, width), BF),
            pltpu.VMEM((4, rows, width), BF),
            pltpu.VMEM((rows, width), BF),
            pltpu.VMEM((rows, width), BF),
            pltpu.VMEM((rows, width), BF),
            pltpu.VMEM((groups, 4 * seqs, HD), BF),
            pltpu.VMEM((groups, SHARE_ROWS, HD), F32),
            pltpu.VMEM((shards + groups, SHARE_ROWS, HD), F32),
            pltpu.VMEM((shards, 4 * seqs, HD), BF),
            dma((2,)),
            dma((8, n)),
            dma((8, n)),
            dma((2, n)),
            dma((2, n)),
            dma((8, n)),
            dma((8, n)),
            dma((n,)),
            dma((n,)),
            dma((n,)),
            dma((n,)),
            dma((groups,)),
            dma((groups,)),
            dma((groups,)),
            dma((groups,)),
            dma((shards,)),
            dma((shards,)),
            dma((shards,)),
            dma((shards,)),
        ],
        compiler_params=pltpu.CompilerParams(
            collective_id=2, has_side_effects=True, vmem_limit_bytes=62 * MIB
        ),
        cost_estimate=pl.CostEstimate(
            flops=2 * rows * width * out_weight.shape[1] * 2,
            bytes_accessed=12 * MIB,
            transcendentals=4 * rows * kv.shape[1],
        ),
        name="attend_scatter",
    )(queries, kv, dec_q, old_share, owner, seq_of_page, live_len, tokens, out_weight)


def hand_on_kernel(hidden, dec, hidden_out, dec_out, sem):
    first = pltpu.make_async_copy(hidden, hidden_out, sem.at[0])
    second = pltpu.make_async_copy(dec, dec_out, sem.at[1])
    first.start()
    second.start()
    first.wait()
    second.wait()


def hand_on(hidden, dec):
    vmem = pl.BlockSpec(memory_space=pltpu.VMEM)
    hbm = pl.BlockSpec(memory_space=pltpu.HBM)
    return pl.pallas_call(
        hand_on_kernel,
        out_shape=(
            jax.ShapeDtypeStruct(hidden.shape, hidden.dtype),
            jax.ShapeDtypeStruct(dec.shape, dec.dtype),
        ),
        in_specs=[vmem, vmem],
        out_specs=(hbm, hbm),
        scratch_shapes=[pltpu.SemaphoreType.DMA((2,))],
        name="hand_on",
    )(hidden, dec)


def per_device(
    tokens,
    norm_gain,
    query_weight,
    kv_weight,
    out_weight,
    prefix_cache,
    prompt_len,
    page_owner,
    page_seq,
    dec_queries,
    dec_cache,
    dec_len,
):
    queries, kv_both, old_share = gather_multiply(
        tokens, norm_gain, prefix_cache, query_weight, kv_weight, dec_queries, dec_len, dec_cache
    )
    hidden_out, dec_out = attend_scatter(
        tokens,
        queries,
        kv_both,
        dec_queries,
        old_share,
        page_owner.reshape(1, -1),
        page_seq.reshape(1, -1),
        prompt_len,
        out_weight,
        lax.axis_size("group"),
    )
    return hand_on(hidden_out, dec_out)


def solution(mesh):
    return jax.shard_map(
        per_device,
        mesh=mesh,
        in_specs=(
            P("group", "tp"),
            P(None, "tp"),
            P(None, "tp"),
            P(None, "tp"),
            P("tp", None),
            P("group", "tp"),
            P("group"),
            P("group", None),
            P("group"),
            P("group", None),
            P("group", "tp", None),
            P("group"),
        ),
        out_specs=(P("group", "tp"), P("group", None)),
        check_vma=False,
    )
```

```python
import math

import jax
import jax.numpy as jnp
from jax import lax
from jax.experimental import pallas as pl
from jax.experimental.pallas import tpu as pltpu
from jax.sharding import PartitionSpec as P

HEADS = 64
KVH = 8
HD = 128
PAGE = 4


EPSILON = 1e-05
NEG_BIG = -1e30


MESH = pl.DeviceIdType.MESH
BF = jnp.bfloat16
F32 = jnp.float32
MIB = 1024 * 1024
SIDES = 2
RING = 4


def here():
    t = lax.axis_index("tp")
    return t // (RING * 2), lax.rem(t // 2, RING), lax.rem(t, 2)


def shard_at(side, ring, core, far, step, other):
    s = lax.rem(side + far, SIDES)
    r = lax.rem(ring + step, RING)
    c = lax.rem(core + other, 2)
    return (s * RING + r) * 2 + c


def push(src, dst, send_sem, recv_sem, to):
    copy = pltpu.make_async_remote_copy(
        src_ref=src,
        dst_ref=dst,
        send_sem=send_sem,
        recv_sem=recv_sem,
        device_id={"tp": to},
        device_id_type=MESH,
    )
    copy.start()
    return copy


def landed(ref, recv_sem, to):
    pltpu.make_async_remote_copy(
        src_ref=ref,
        dst_ref=ref,
        send_sem=recv_sem,
        recv_sem=recv_sem,
        device_id={"tp": to},
        device_id_type=MESH,
    ).wait_recv()


def greet(peers):
    barrier = pltpu.get_barrier_semaphore()
    for peer in peers:
        pl.semaphore_signal(barrier, inc=1, device_id={"tp": peer}, device_id_type=MESH)
    pl.semaphore_wait(barrier, len(peers))


GATHER_CHUNKS = 4
GAIN_ROWS = 16
SHARE_ROWS = 40
LOG_SCALE = math.log2(math.e) / math.sqrt(HD)


def write_share(share, accum, top, total, low):
    lane = lax.broadcasted_iota(jnp.int32, (8, HD), 1) // 16
    stat = jnp.zeros((8, HD), F32)
    for h in range(4):
        rows = slice(low + h * 8, low + h * 8 + 8)
        stat = jnp.where(lane == h, top[rows], stat)
        stat = jnp.where(lane == 4 + h, total[rows], stat)
    share[pl.ds(0, 32), :] = accum[low : low + 32]
    share[pl.ds(32, 8), :] = stat


def gather_kernel(
    gain,
    dec_q,
    dec_len,
    tok,
    prefix,
    qw_hbm,
    kw_hbm,
    cache_hbm,
    q_out,
    kv_out,
    old_share,
    xall,
    cache,
    qw,
    kw,
    acc_q,
    acc_k,
    power,
    w_sem,
    recv_sem,
    sib_sem,
    x_send,
    up_send,
    down_send,
    sib_send,
    kv_send,
    kv_recv,
    split_send,
    split_recv,
):
    side, ring, core = here()
    rows_all, width = tok.shape
    chunk = rows_all // GATHER_CHUNKS

    def at(far, step, other=0):
        return shard_at(side, ring, core, far, step, other)

    me, across, sib = at(0, 0), at(1, 0), at(0, 0, 1)
    up, down = at(0, 1), at(0, 3)

    load_q = pltpu.make_async_copy(qw_hbm, qw, w_sem.at[0])
    load_k = pltpu.make_async_copy(kw_hbm, kw, w_sem.at[1])
    prefix_rows = prefix.shape[0]
    load_x = pltpu.make_async_copy(tok, xall.at[me, pl.ds(GAIN_ROWS, rows_all), :], w_sem.at[2])
    load_x.start()
    load_p = pltpu.make_async_copy(prefix, kv_out.at[core, pl.ds(0, prefix_rows), :], w_sem.at[3])
    load_p.start()
    load_q.start()
    load_k.start()
    load_cache = pltpu.make_async_copy(cache_hbm, cache, w_sem.at[4])
    load_cache.start()
    xall[me, pl.ds(0, GAIN_ROWS), :] = jnp.broadcast_to(gain[...], (GAIN_ROWS, width))
    acc_q[...] = jnp.zeros_like(acc_q)
    acc_k[...] = jnp.zeros_like(acc_k)
    power[...] = jnp.zeros_like(power)
    greet((across, up, down, sib))
    load_x.wait()

    sends = []
    split = GATHER_CHUNKS - 1

    def span(i, half=None):
        low = 0 if i == 0 else GAIN_ROWS + i * chunk
        high = GAIN_ROWS + (i + 1) * chunk
        middle = high - chunk // 2
        if half == 0:
            high = middle
        if half == 1:
            low = middle
        return pl.ds(low, high - low)

    def send(slot, rows, send_sem, there_sem, to):
        ref = xall.at[slot, rows, :]
        sends.append(push(ref, ref, send_sem, there_sem, to))

    def to_sibling(far, step, i):
        kind = far * 4 + step
        send(at(far, step), span(i), sib_send.at[kind, i], sib_sem.at[kind, i], sib)

    def multiply(slot, i):
        rows = pl.ds(i * chunk, chunk)
        wide = xall[slot, pl.ds(GAIN_ROWS + i * chunk, chunk), :].astype(F32)
        weight = xall[slot, pl.ds(0, 1), :].astype(F32)
        square = wide * wide
        part = square[:, 0:HD]
        for k in range(1, width // HD):
            part = part + square[:, k * HD : (k + 1) * HD]
        power[rows, :] += part
        scaled = (wide * weight).astype(BF)
        depth = pl.ds(pl.multiple_of(slot * width, width), width)
        acc_q[rows, :] += jnp.dot(scaled, qw[depth, :], preferred_element_type=F32)
        acc_k[rows, :] += jnp.dot(scaled, kw[depth, :], preferred_element_type=F32)

    def from_sibling(far, step, i):
        kind = far * 4 + step
        slot = at(far, step, 1)
        landed(xall.at[slot, span(i), :], sib_sem.at[kind, i], sib)
        multiply(slot, i)

    def got(far, step, i):
        kind = far * 4 + step
        slot = at(far, step)
        if step == 2 and far == 0:
            landed(xall.at[slot, span(i, 0), :], recv_sem.at[kind, i], down)
            landed(xall.at[slot, span(i, 1), :], recv_sem.at[8, i], up)
        elif i == split and far == 1 and step in (1, 3):
            landed(xall.at[slot, span(i, 0), :], recv_sem.at[kind, i], up)
            landed(xall.at[slot, span(i, 1), :], split_recv.at[step // 2], across)
        else:
            landed(xall.at[slot, span(i), :], recv_sem.at[kind, i], up)

    for i in range(GATHER_CHUNKS):
        send(me, span(i), x_send.at[i], recv_sem.at[4, i], across)
        send(me, span(i), up_send.at[0, i], recv_sem.at[3, i], up)
        send(me, span(i), down_send.at[0, i], recv_sem.at[1, i], down)
        to_sibling(0, 0, i)
    load_p.wait()
    early = kv_out.at[core, pl.ds(0, prefix_rows), :]
    sends.append(push(early, early, kv_send.at[0], kv_recv.at[0], sib))
    load_q.wait()
    load_k.wait()
    load_cache.wait()
    dec_seqs, ctx = cache.shape[0], cache.shape[1]
    contract = (((1,), (1,)), ((), ()))

    def dec_old(k):
        count = dec_seqs * 8
        seq_row = lax.rem(lax.broadcasted_iota(jnp.int32, (count, ctx), 0), 8)
        position = lax.broadcasted_iota(jnp.int32, (count, ctx), 1) + me * ctx
        parts = [dec_q[:, pl.ds((k * 8 + h) * HD, HD)].astype(F32) for h in range(8)]
        query = jnp.concatenate(parts, axis=0).astype(BF)
        found = jnp.full((count, ctx), NEG_BIG, F32)
        for seq in range(dec_seqs):
            score = lax.dot_general(
                query,
                cache[seq, :, pl.ds(2 * k * HD, HD)],
                contract,
                preferred_element_type=F32,
            )
            valid = (position < dec_len[seq]) & (seq_row == seq)
            found = jnp.where(valid, score * LOG_SCALE, found)
        top = jnp.max(found, axis=-1, keepdims=True)
        expo = jnp.where(found > 0.5 * NEG_BIG, jnp.exp2(found - top), 0.0)
        accum = jnp.zeros((count, HD), F32)
        for seq in range(dec_seqs):
            own = jnp.where(seq_row == seq, expo, 0.0).astype(BF)
            accum = accum + jnp.dot(
                own, cache[seq, :, pl.ds((2 * k + 1) * HD, HD)], preferred_element_type=F32
            )
        total = jnp.sum(expo, axis=-1, keepdims=True)
        for part in range(2):
            write_share(old_share.at[2 * k + part], accum, top, total, part * 32)

    def event(name, i):
        if name == "O":
            multiply(me, i)
            return [(0, 0, i)]
        if name == "X":
            got(1, 0, i)
            rows = span(i, 0) if i == split else span(i)
            send(across, rows, up_send.at[1, i], recv_sem.at[7, i], up)
            send(across, rows, down_send.at[1, i], recv_sem.at[5, i], down)
            to_sibling(1, 0, i)
            multiply(across, i)
            return [(1, 0, i)]
        far = 0 if name in ("Z", "F") else 1
        if name in ("Z", "P"):
            got(far, 3, i)
            if far == 0:
                send(at(0, 3), span(i, 0), up_send.at[2, i], recv_sem.at[2, i], up)
                if i == split:
                    send(at(0, 3), span(i, 1), split_send.at[1], split_recv.at[1], across)
            got(far, 1, i)
            if far == 0:
                send(at(0, 1), span(i, 1), down_send.at[2, i], recv_sem.at[8, i], down)
                if i == split:
                    send(at(0, 1), span(i, 1), split_send.at[0], split_recv.at[0], across)
            to_sibling(far, 3, i)
            to_sibling(far, 1, i)
            multiply(at(far, 3), i)
            multiply(at(far, 1), i)
            return [(far, 3, i), (far, 1, i)]
        got(far, 2, i)
        if far == 0:
            send(at(0, 2), span(i), x_send.at[GATHER_CHUNKS + i], recv_sem.at[6, i], across)
        to_sibling(far, 2, i)
        multiply(at(far, 2), i)
        return [(far, 2, i)]

    order = (
        ("O", 0), ("O", 1), ("O", 2), ("O", 3), ("Z", 0), ("Z", 1), ("Z", 2), ("Z", 3),
        ("X", 0), ("X", 1), ("X", 2), ("X", 3), ("F", 0), ("F", 1), ("F", 2), ("F", 3),
        ("P", 0), ("P", 1), ("G", 0), ("P", 2), ("G", 1), ("G", 2), ("P", 3), ("G", 3),
    )
    def settle(i):
        rows = pl.ds(i * chunk, chunk)
        total = jnp.sum(power[rows, :], axis=-1, keepdims=True) / (width * 2 * RING * SIDES)
        factor = lax.rsqrt(total + EPSILON)
        new = pl.ds(prefix_rows + i * chunk, chunk)
        kv_out[core, new, :] = (acc_k[rows, :] * factor).astype(BF)
        ref = kv_out.at[core, new, :]
        sends.append(push(ref, ref, kv_send.at[1 + i], kv_recv.at[1 + i], sib))
        queries = (acc_q[rows, :] * (factor * LOG_SCALE)).astype(BF)
        for h in range(q_out.shape[0]):
            q_out[h, rows, :] = queries[:, h * HD : (h + 1) * HD]

    late = []
    for name, i in order:
        fresh = event(name, i)
        if name in ("Z", "X"):
            dec_old(i + (4 if name == "X" else 0))
        for item in late:
            from_sibling(*item)
        for far, step, k in late:
            if (far, step) == (1, 2):
                settle(k)
        late = fresh
    for item in late:
        from_sibling(*item)
    settle(GATHER_CHUNKS - 1)
    landed(kv_out.at[1 - core, pl.ds(0, prefix_rows), :], kv_recv.at[0], sib)
    for i in range(GATHER_CHUNKS):
        new = pl.ds(prefix_rows + i * chunk, chunk)
        landed(kv_out.at[1 - core, new, :], kv_recv.at[1 + i], sib)
    for copy in sends:
        copy.wait_send()


def gather_multiply(tokens, gain, prefix, query_weight, kv_weight, dec_q, dec_len, cache):
    rows, width = tokens.shape
    shards = 2 * RING * SIDES
    kv_rows = prefix.shape[0] + rows
    vmem = pl.BlockSpec(memory_space=pltpu.VMEM)
    dma = pltpu.SemaphoreType.DMA
    n = GATHER_CHUNKS
    return pl.pallas_call(
        gather_kernel,
        out_shape=(
            jax.ShapeDtypeStruct((query_weight.shape[1] // HD, rows, HD), BF),
            jax.ShapeDtypeStruct((2, kv_rows, HD), BF),
            jax.ShapeDtypeStruct((shards, SHARE_ROWS, HD), F32),
        ),
        in_specs=[vmem, vmem, pl.BlockSpec(memory_space=pltpu.SMEM)]
        + [pl.BlockSpec(memory_space=pltpu.HBM)] * 5,
        out_specs=(vmem,) * 3,
        scratch_shapes=[
            pltpu.VMEM((shards, rows + GAIN_ROWS, width), BF),
            pltpu.VMEM(cache.shape, BF),
            pltpu.VMEM(query_weight.shape, BF),
            pltpu.VMEM(kv_weight.shape, BF),
            pltpu.VMEM((rows, query_weight.shape[1]), F32),
            pltpu.VMEM((rows, HD), F32),
            pltpu.VMEM((rows, HD), F32),
            dma((5,)),
            dma((9, n)),
            dma((8, n)),
            dma((2 * n,)),
            dma((3, n)),
            dma((3, n)),
            dma((8, n)),
            dma((n + 1,)),
            dma((n + 1,)),
            dma((2,)),
            dma((2,)),
        ],
        compiler_params=pltpu.CompilerParams(
            collective_id=1, has_side_effects=True, vmem_limit_bytes=62 * MIB
        ),
        cost_estimate=pl.CostEstimate(
            flops=2 * rows * width * shards * (query_weight.shape[1] + HD),
            bytes_accessed=16 * MIB,
            transcendentals=0,
        ),
        name="gather_multiply",
    )(gain, dec_q, dec_len, tokens, prefix, query_weight, kv_weight, cache)


SCATTER_CHUNKS = 8
SIDE_CHUNK = 1


def attend_kernel(
    q,
    kv,
    dec_q,
    old_share,
    owner,
    seq_of_page,
    live_len,
    tok_hbm,
    wo_hbm,
    out,
    dec_out,
    wo,
    att,
    mine,
    lend,
    borrowed,
    mid,
    near,
    last,
    far_in,
    side_in,
    tok,
    asked,
    answers,
    shares,
    results,
    w_sem,
    lend_send,
    lend_recv,
    mid_send,
    mid_recv,
    near_send,
    near_recv,
    last_send,
    last_recv,
    far_send,
    far_recv,
    side_send,
    side_recv,
    ask_send,
    ask_recv,
    answer_send,
    answer_recv,
    share_send,
    share_recv,
    done_send,
    done_recv,
):
    side, ring, core = here()
    rows_all, width = out.shape
    chunk = rows_all // SCATTER_CHUNKS
    half = chunk // 2
    old = kv.shape[1] - rows_all
    n = SCATTER_CHUNKS

    def at(far, step, other=0):
        return shard_at(side, ring, core, far, step, other)

    across, sib, up, down = at(1, 0), at(0, 0, 1), at(0, 1), at(0, 3)
    load = pltpu.make_async_copy(wo_hbm, wo, w_sem.at[0])
    load.start()
    load_tok = pltpu.make_async_copy(tok_hbm, tok, w_sem.at[1])
    load_tok.start()
    shard = lax.axis_index("tp")
    group = lax.axis_index("group")
    shards = 2 * RING * SIDES
    groups = lax.axis_size("group")
    dec_seqs = dec_out.shape[0]
    barrier = pltpu.get_barrier_semaphore()

    def greet_shard(d, carry):
        pl.semaphore_signal(
            barrier, inc=1, device_id={"tp": lax.rem(shard + d, shards)}, device_id_type=MESH
        )
        return carry

    def greet_group(d, carry):
        pl.semaphore_signal(
            barrier, inc=1, device_id={"group": lax.rem(group + d, groups)}, device_id_type=MESH
        )
        return carry

    lax.fori_loop(1, shards, greet_shard, 0)
    lax.fori_loop(1, groups, greet_group, 0)

    def copy_to(src, dst, send_sem, recv_sem, to):
        return pltpu.make_async_remote_copy(
            src_ref=src,
            dst_ref=dst,
            send_sem=send_sem,
            recv_sem=recv_sem,
            device_id=to,
            device_id_type=MESH,
        )

    contract = (((1,), (1,)), ((), ()))
    per = 4 * dec_seqs

    def ask_copy(d):
        to = lax.rem(group + d, groups)
        return copy_to(
            asked.at[group], asked.at[group], ask_send.at[d], ask_recv.at[d], {"group": to}
        )

    def answer_copy(d):
        to = lax.rem(group + d, groups)
        return copy_to(
            answers.at[to],
            shares.at[shards + group],
            answer_send.at[d],
            answer_recv.at[d],
            {"group": to},
        )

    def share_copy(d):
        to = lax.rem(shard + d, shards)
        return copy_to(
            old_share.at[to], shares.at[shard], share_send.at[d], share_recv.at[d], {"tp": to}
        )

    def done_copy(d):
        to = lax.rem(shard + d, shards)
        return copy_to(
            results.at[shard], results.at[shard], done_send.at[d], done_recv.at[d], {"tp": to}
        )

    def each(count, act):
        def body(d, carry):
            act(d)
            return carry

        lax.fori_loop(1, count, body, 0)

    def arrive(count, of, axis, place, send_sem, recv_sem):
        def take(d):
            frm = lax.rem(of + count - d, count)
            ref = place(frm)
            copy_to(ref, ref, send_sem.at[d], recv_sem.at[d], {axis: frm}).wait_recv()

        each(count, take)

    def dec_begin():
        parts = []
        for h in range(4):
            cols = pl.ds(pl.multiple_of(shard * width + h * HD, HD), HD)
            parts.append(dec_q[:, cols].astype(F32))
        asked[group] = jnp.concatenate(parts, axis=0).astype(BF)
        each(groups, lambda d: ask_copy(d).start())
        shares[shard] = old_share[shard]
        each(shards, lambda d: share_copy(d).start())

    def dec_answer():
        arrive(groups, group, "group", lambda frm: asked.at[frm], ask_send, ask_recv)
        count = owner.shape[1]
        old_rows = kv.shape[1] - rows_all
        both = jnp.concatenate(
            [
                jnp.broadcast_to(owner[...], (8, count)),
                jnp.broadcast_to(seq_of_page[...], (8, count)),
            ],
            axis=0,
        ).astype(F32)
        page = lax.broadcasted_iota(jnp.int32, (count, rows_all), 0)
        page_of = lax.broadcasted_iota(jnp.int32, (count, rows_all), 1) // PAGE
        spread = jnp.where(page == page_of, 1.0, 0.0).astype(BF)
        by_token = jnp.dot(both.astype(BF), spread, preferred_element_type=F32).astype(jnp.int32)
        token = lax.broadcasted_iota(jnp.int32, (1, rows_all), 1)
        code = by_token[0:1, :] // shards * dec_seqs + by_token[8:9, :]
        code = jnp.where(token < live_len[0], code, -1)
        row = lax.broadcasted_iota(jnp.int32, (groups * per, rows_all), 0)
        held = code == row // per * dec_seqs + lax.rem(row, dec_seqs)
        query = asked[...].reshape(groups * per, HD)
        score = lax.dot_general(
            query, kv[0, pl.ds(old_rows, rows_all), :], contract, preferred_element_type=F32
        )
        score = jnp.where(held, score * LOG_SCALE, NEG_BIG)
        top = jnp.max(score, axis=-1, keepdims=True)
        expo = jnp.where(held, jnp.exp2(score - top), 0.0)
        total = jnp.sum(expo, axis=-1, keepdims=True)
        accum = jnp.dot(
            expo.astype(BF), kv[1, pl.ds(old_rows, rows_all), :], preferred_element_type=F32
        )
        for g in range(answers.shape[0]):
            write_share(answers.at[g], accum, top, total, g * per)
        shares[shards + group] = answers[group]
        each(groups, lambda d: answer_copy(d).start())

    def dec_combine():
        arrive(shards, shard, "tp", lambda frm: shares.at[frm], share_send, share_recv)
        arrive(
            groups, group, "group", lambda frm: shares.at[shards + frm], answer_send, answer_recv
        )
        stat = shares[:, pl.ds(32, 8), :]
        lane = lax.broadcasted_iota(jnp.int32, stat.shape, 2) // 16
        parts = []
        for h in range(4):
            top = jnp.max(jnp.where(lane == h, stat, NEG_BIG), axis=-1, keepdims=True)
            total = jnp.max(jnp.where(lane == 4 + h, stat, 0.0), axis=-1, keepdims=True)
            factor = jnp.exp2(top - jnp.max(top, axis=0, keepdims=True))
            whole = jnp.sum(factor * total, axis=0)
            accum = jnp.sum(factor * shares[:, pl.ds(h * 8, 8), :], axis=0)
            parts.append(accum / whole)
        results[shard] = jnp.concatenate(parts, axis=0).astype(BF)
        each(shards, lambda d: done_copy(d).start())

    def dec_end():
        arrive(shards, shard, "tp", lambda frm: results.at[frm], done_send, done_recv)
        for t in range(results.shape[0]):
            block = results[t].astype(F32)
            for h in range(4):
                dec_out[:, (t * 4 + h) * HD : (t * 4 + h + 1) * HD] = block[
                    h * 8 : h * 8 + 8
                ].astype(BF)
        for copy in (share_copy, done_copy):
            each(shards, lambda d, copy=copy: copy(d).wait_send())
        for copy in (ask_copy, answer_copy):
            each(groups, lambda d, copy=copy: copy(d).wait_send())

    def rows_of(j):
        return pl.ds(pl.multiple_of(j * chunk, chunk), chunk)

    def half_of(j, k):
        return pl.ds(pl.multiple_of(j * chunk + k * half, half), half)

    def attend(j, plain, edge):
        rows = rows_of(j)
        count = width // HD
        query = q[:, rows, :].reshape(count * chunk, HD)
        row = lax.rem(lax.broadcasted_iota(jnp.int32, (count * chunk, edge), 0), chunk)
        column = lax.broadcasted_iota(jnp.int32, (count * chunk, edge), 1)
        seen = column + plain <= row + old + j * chunk
        first = lax.dot_general(
            query, kv[0, pl.ds(0, plain), :], contract, preferred_element_type=F32
        )
        second = lax.dot_general(
            query, kv[0, pl.ds(plain, edge), :], contract, preferred_element_type=F32
        )
        second = jnp.where(seen, second, NEG_BIG)
        top = jnp.maximum(
            jnp.max(first, axis=-1, keepdims=True), jnp.max(second, axis=-1, keepdims=True)
        )
        first = jnp.exp2(first - top)
        second = jnp.exp2(second - top)
        total = jnp.sum(first, axis=-1, keepdims=True) + jnp.sum(second, axis=-1, keepdims=True)
        value = jnp.dot(
            first.astype(BF), kv[1, pl.ds(0, plain), :], preferred_element_type=F32
        ) + jnp.dot(second.astype(BF), kv[1, pl.ds(plain, edge), :], preferred_element_type=F32)
        value = value / total
        for h in range(count):
            att[:, h * HD : (h + 1) * HD] = value[h * chunk : (h + 1) * chunk].astype(BF)

    def attention(j):
        for pair in range(n // 2):

            @pl.when(j // 2 == pair)
            def _(pair=pair):
                attend(j, old + 2 * pair * chunk, 2 * chunk)

    def term(far, step, other):
        slot = at(far, step, other)
        cols = pl.ds(pl.multiple_of(slot * width, width), width)
        return jnp.dot(att[...], wo[:, cols], preferred_element_type=F32)

    def add_into(dst, src):
        dst[...] = (dst[...].astype(F32) + src[...].astype(F32)).astype(BF)

    def lend_copy(kind, j):
        rows = rows_of(j)
        return pltpu.make_async_remote_copy(
            src_ref=lend.at[kind, rows, :],
            dst_ref=borrowed.at[kind, rows, :],
            send_sem=lend_send.at[kind, j],
            recv_sem=lend_recv.at[kind, j],
            device_id={"tp": sib},
            device_id_type=MESH,
        )

    def mid_copy(way, j):
        rows = half_of(j, way)
        return pltpu.make_async_remote_copy(
            src_ref=mine.at[2, rows, :],
            dst_ref=mid.at[rows, :],
            send_sem=mid_send.at[way, j],
            recv_sem=mid_recv.at[way, j],
            device_id={"tp": down if way else up},
            device_id_type=MESH,
        )

    def far_copy(j):
        rows = rows_of(j)
        return pltpu.make_async_remote_copy(
            src_ref=mine.at[6, rows, :],
            dst_ref=far_in.at[rows, :],
            send_sem=far_send.at[j],
            recv_sem=far_recv.at[j],
            device_id={"tp": across},
            device_id_type=MESH,
        )

    def near_copy(far, way, k, j):
        rows = half_of(j, k)
        return pltpu.make_async_remote_copy(
            src_ref=mine.at[far * 4 + (3 if way else 1), rows, :],
            dst_ref=near.at[far * 2 + way, rows, :],
            send_sem=near_send.at[far * 4 + way * 2 + k, j],
            recv_sem=near_recv.at[far * 4 + way * 2 + k, j],
            device_id={"tp": down if way else up},
            device_id_type=MESH,
        )

    def last_copy(j):
        rows = rows_of(j)
        return pltpu.make_async_remote_copy(
            src_ref=mine.at[4, rows, :],
            dst_ref=last.at[rows, :],
            send_sem=last_send.at[j],
            recv_sem=last_recv.at[j],
            device_id={"tp": across},
            device_id_type=MESH,
        )

    kinds = ((1, 2), (1, 1), (1, 3), (0, 2), (0, 1), (0, 3), (1, 0), (0, 0))
    ahead = 4

    def produce(j):
        rows = rows_of(j)

        def offer(far, step):
            kind = far * 4 + step
            lend[kind, rows, :] = term(far, step, 1).astype(BF)
            lend_copy(kind, j).start()

        for far, step in kinds[:ahead]:
            offer(far, step)
        for k, (far, step) in enumerate(kinds):
            if k + ahead < len(kinds):
                offer(*kinds[k + ahead])
            kind = far * 4 + step
            own = term(far, step, 0)
            lend_copy(kind, j).wait_recv()
            mine[kind, rows, :] = (own + borrowed[kind, rows, :].astype(F32)).astype(BF)
            if (far, step) == (1, 2):
                far_copy(j).start()
            if step in (1, 3):

                @pl.when(j != SIDE_CHUNK)
                def _(far=far, way=step // 2):
                    near_copy(far, way, 1 - way, j).start()
                    if far:
                        near_copy(far, way, way, j).start()

                if far:

                    @pl.when(j == SIDE_CHUNK)
                    def _(way=step // 2):
                        side_copy(way).start()


    def side_copy(way):
        rows = pl.ds(SIDE_CHUNK * chunk, chunk)
        return pltpu.make_async_remote_copy(
            src_ref=mine.at[7 if way else 5, rows, :],
            dst_ref=side_in.at[way],
            send_sem=side_send.at[way],
            recv_sem=side_recv.at[way],
            device_id={"tp": across},
            device_id_type=MESH,
        )

    def pass_on(j):
        @pl.when(j == SIDE_CHUNK)
        def _():
            for way in (0, 1):
                side_copy(way).wait_recv()
                add_into(mine.at[3 if way else 1, rows_of(j), :], side_in.at[way])
                near_copy(0, way, 1 - way, j).start()

        far_copy(j).wait_recv()
        rows = rows_of(j)
        add_into(mine.at[2, rows, :], far_in.at[rows, :])
        mid_copy(0, j).start()
        mid_copy(1, j).start()

    def relay(j):
        for way in (0, 1):
            mid_copy(way, j).wait_recv()
            rows = half_of(j, way)
            add_into(mine.at[3 if way else 1, rows, :], mid.at[rows, :])
            near_copy(0, way, way, j).start()

    def near_wait(far, j):
        for way in (0, 1):
            for k in (0, 1):
                near_copy(far, way, k, j).wait_recv()

    def cross(j):
        rows = rows_of(j)

        @pl.when(j != SIDE_CHUNK)
        def _():
            near_wait(1, j)
            mine[4, rows, :] = (
                mine[4, rows, :].astype(F32)
                + near[2, rows, :].astype(F32)
                + near[3, rows, :].astype(F32)
            ).astype(BF)

        last_copy(j).start()

    def finish(j):
        near_wait(0, j)
        last_copy(j).wait_recv()
        rows = rows_of(j)
        out[rows, :] = (
            tok[rows, :].astype(F32)
            + (
                mine[0, rows, :].astype(F32)
                + near[0, rows, :].astype(F32)
                + near[1, rows, :].astype(F32)
                + last[rows, :].astype(F32)
            )
        ).astype(BF)

    attend(0, old, 2 * chunk)
    pl.semaphore_wait(barrier, shards + groups - 2)

    def turn(j, carry):
        @pl.when((j >= 1) & (j < n))
        def _():
            attention(j)

        @pl.when(j == 0)
        def _():
            load.wait()
            load_tok.wait()

        @pl.when((j >= 1) & (j < n + 1))
        def _():
            pass_on(j - 1)

        @pl.when(j < n)
        def _():
            produce(j)

        @pl.when((j >= 2) & (j < n + 2))
        def _():
            relay(j - 2)

        @pl.when((j >= 3) & (j < n + 3))
        def _():
            cross(j - 3)

        @pl.when(j >= 4)
        def _():
            finish(j - 4)

        @pl.when(j == 0)
        def _():
            dec_begin()

        @pl.when(j == 2)
        def _():
            dec_answer()

        @pl.when(j == 5)
        def _():
            dec_combine()

        @pl.when(j == 8)
        def _():
            dec_end()

        return carry

    lax.fori_loop(0, n + 4, turn, 0)

    def drain(j, carry):
        for kind in range(8):
            lend_copy(kind, j).wait_send()
        for way in (0, 1):
            for k in (0, 1):
                near_copy(0, way, k, j).wait_send()

        @pl.when(j != SIDE_CHUNK)
        def _():
            for way in (0, 1):
                for k in (0, 1):
                    near_copy(1, way, k, j).wait_send()

        last_copy(j).wait_send()
        far_copy(j).wait_send()
        mid_copy(0, j).wait_send()
        mid_copy(1, j).wait_send()
        return carry

    lax.fori_loop(0, n, drain, 0)
    side_copy(0).wait_send()
    side_copy(1).wait_send()


def attend_scatter(
    tokens, queries, kv, dec_q, old_share, owner, seq_of_page, live_len, out_weight, groups
):
    rows, width = tokens.shape
    vmem = pl.BlockSpec(memory_space=pltpu.VMEM)
    dma = pltpu.SemaphoreType.DMA
    n = SCATTER_CHUNKS
    seqs = dec_q.shape[0]
    shards = 2 * RING * SIDES
    return pl.pallas_call(
        attend_kernel,
        out_shape=(
            jax.ShapeDtypeStruct((rows, width), BF),
            jax.ShapeDtypeStruct((seqs, HEADS * HD), BF),
        ),
        in_specs=[
            vmem,
            vmem,
            vmem,
            vmem,
            vmem,
            vmem,
            pl.BlockSpec(memory_space=pltpu.SMEM),
            pl.BlockSpec(memory_space=pltpu.HBM),
            pl.BlockSpec(memory_space=pltpu.HBM),
        ],
        out_specs=(vmem, vmem),
        scratch_shapes=[
            pltpu.VMEM(out_weight.shape, BF),
            pltpu.VMEM((rows // n, width), BF),
            pltpu.VMEM((8, rows, width), BF),
            pltpu.VMEM((8, rows, width), BF),
            pltpu.VMEM((8, rows, width), BF),
            pltpu.VMEM((rows, width), BF),
            pltpu.VMEM((4, rows, width), BF),
            pltpu.VMEM((rows, width), BF),
            pltpu.VMEM((rows, width), BF),
            pltpu.VMEM((2, rows // n, width), BF),
            pltpu.VMEM((rows, width), BF),
            pltpu.VMEM((groups, 4 * seqs, HD), BF),
            pltpu.VMEM((groups, SHARE_ROWS, HD), F32),
            pltpu.VMEM((shards + groups, SHARE_ROWS, HD), F32),
            pltpu.VMEM((shards, 4 * seqs, HD), BF),
            dma((2,)),
            dma((8, n)),
            dma((8, n)),
            dma((2, n)),
            dma((2, n)),
            dma((8, n)),
            dma((8, n)),
            dma((n,)),
            dma((n,)),
            dma((n,)),
            dma((n,)),
            dma((2,)),
            dma((2,)),
            dma((groups,)),
            dma((groups,)),
            dma((groups,)),
            dma((groups,)),
            dma((shards,)),
            dma((shards,)),
            dma((shards,)),
            dma((shards,)),
        ],
        compiler_params=pltpu.CompilerParams(
            collective_id=2, has_side_effects=True, vmem_limit_bytes=62 * MIB
        ),
        cost_estimate=pl.CostEstimate(
            flops=2 * rows * width * out_weight.shape[1] * 2,
            bytes_accessed=12 * MIB,
            transcendentals=4 * rows * kv.shape[1],
        ),
        name="attend_scatter",
    )(queries, kv, dec_q, old_share, owner, seq_of_page, live_len, tokens, out_weight)


def hand_on_kernel(hidden, dec, hidden_out, dec_out, buffer, dec_buffer, sem_in, sem_out):
    part = hidden.shape[0] // 4
    moves = [(dec, dec_buffer, dec_out)]
    for k in range(4):
        rows = pl.ds(k * part, part)
        moves.append((hidden.at[rows], buffer.at[rows], hidden_out.at[rows]))
    loads = [pltpu.make_async_copy(a, b, sem_in.at[k]) for k, (a, b, _) in enumerate(moves)]
    stores = [pltpu.make_async_copy(b, c, sem_out.at[k]) for k, (_, b, c) in enumerate(moves)]
    for load in loads:
        load.start()
    for load, store in zip(loads, stores):
        load.wait()
        store.start()
    for store in stores:
        store.wait()


def hand_on(hidden, dec):
    hbm = pl.BlockSpec(memory_space=pltpu.HBM)
    return pl.pallas_call(
        hand_on_kernel,
        out_shape=(
            jax.ShapeDtypeStruct(hidden.shape, hidden.dtype),
            jax.ShapeDtypeStruct(dec.shape, dec.dtype),
        ),
        in_specs=[hbm, hbm],
        out_specs=(hbm, hbm),
        scratch_shapes=[
            pltpu.VMEM(hidden.shape, hidden.dtype),
            pltpu.VMEM(dec.shape, dec.dtype),
            pltpu.SemaphoreType.DMA((5,)),
            pltpu.SemaphoreType.DMA((5,)),
        ],
        name="hand_on",
    )(hidden, dec)


def per_device(
    tokens,
    norm_gain,
    query_weight,
    kv_weight,
    out_weight,
    prefix_cache,
    prompt_len,
    page_owner,
    page_seq,
    dec_queries,
    dec_cache,
    dec_len,
):
    queries, kv_both, old_share = gather_multiply(
        tokens, norm_gain, prefix_cache, query_weight, kv_weight, dec_queries, dec_len, dec_cache
    )
    hidden_out, dec_out = attend_scatter(
        tokens,
        queries,
        kv_both,
        dec_queries,
        old_share,
        page_owner.reshape(1, -1),
        page_seq.reshape(1, -1),
        prompt_len,
        out_weight,
        lax.axis_size("group"),
    )
    return hand_on(hidden_out, dec_out)


def solution(mesh):
    return jax.shard_map(
        per_device,
        mesh=mesh,
        in_specs=(
            P("group", "tp"),
            P(None, "tp"),
            P(None, "tp"),
            P(None, "tp"),
            P("tp", None),
            P("group", "tp"),
            P("group"),
            P("group", None),
            P("group"),
            P("group", None),
            P("group", "tp", None),
            P("group"),
        ),
        out_specs=(P("group", "tp"), P("group", None)),
        check_vma=False,
    )
```

```python
import math

import jax
import jax.numpy as jnp
from jax import lax
from jax.experimental import pallas as pl
from jax.experimental.pallas import tpu as pltpu
from jax.sharding import PartitionSpec as P

HEADS = 64
KVH = 8
HD = 128
PAGE = 4


EPSILON = 1e-05
NEG_BIG = -1e30


MESH = pl.DeviceIdType.MESH
BF = jnp.bfloat16
F32 = jnp.float32
MIB = 1024 * 1024
SIDES = 2
RING = 4


def here():
    t = lax.axis_index("tp")
    return t // (RING * 2), lax.rem(t // 2, RING), lax.rem(t, 2)


def shard_at(side, ring, core, far, step, other):
    s = lax.rem(side + far, SIDES)
    r = lax.rem(ring + step, RING)
    c = lax.rem(core + other, 2)
    return (s * RING + r) * 2 + c


def push(src, dst, send_sem, recv_sem, to):
    copy = pltpu.make_async_remote_copy(
        src_ref=src,
        dst_ref=dst,
        send_sem=send_sem,
        recv_sem=recv_sem,
        device_id={"tp": to},
        device_id_type=MESH,
    )
    copy.start()
    return copy


def landed(ref, recv_sem, to):
    pltpu.make_async_remote_copy(
        src_ref=ref,
        dst_ref=ref,
        send_sem=recv_sem,
        recv_sem=recv_sem,
        device_id={"tp": to},
        device_id_type=MESH,
    ).wait_recv()


def greet(peers):
    barrier = pltpu.get_barrier_semaphore()
    for peer in peers:
        pl.semaphore_signal(barrier, inc=1, device_id={"tp": peer}, device_id_type=MESH)
    pl.semaphore_wait(barrier, len(peers))


GATHER_CHUNKS = 4
GAIN_ROWS = 16
SHARE_ROWS = 40
LOG_SCALE = math.log2(math.e) / math.sqrt(HD)


def write_share(share, accum, top, total, low):
    lane = lax.broadcasted_iota(jnp.int32, (8, HD), 1) // 16
    stat = jnp.zeros((8, HD), F32)
    for h in range(4):
        rows = slice(low + h * 8, low + h * 8 + 8)
        stat = jnp.where(lane == h, top[rows], stat)
        stat = jnp.where(lane == 4 + h, total[rows], stat)
    share[pl.ds(0, 32), :] = accum[low : low + 32]
    share[pl.ds(32, 8), :] = stat


def gather_kernel(
    gain,
    dec_q,
    dec_len,
    tok,
    prefix,
    qw_hbm,
    kw_hbm,
    cache_hbm,
    q_out,
    kv_out,
    old_share,
    xall,
    cache,
    qw,
    kw,
    acc_q,
    acc_k,
    power,
    w_sem,
    recv_sem,
    sib_sem,
    x_send,
    up_send,
    down_send,
    sib_send,
    kv_send,
    kv_recv,
    split_send,
    split_recv,
):
    side, ring, core = here()
    rows_all, width = tok.shape
    chunk = rows_all // GATHER_CHUNKS

    def at(far, step, other=0):
        return shard_at(side, ring, core, far, step, other)

    me, across, sib = at(0, 0), at(1, 0), at(0, 0, 1)
    up, down = at(0, 1), at(0, 3)

    load_q = pltpu.make_async_copy(qw_hbm, qw, w_sem.at[0])
    load_k = pltpu.make_async_copy(kw_hbm, kw, w_sem.at[1])
    prefix_rows = prefix.shape[0]
    load_x = pltpu.make_async_copy(tok, xall.at[me, pl.ds(GAIN_ROWS, rows_all), :], w_sem.at[2])
    load_x.start()
    load_p = pltpu.make_async_copy(prefix, kv_out.at[core, pl.ds(0, prefix_rows), :], w_sem.at[3])
    load_p.start()
    load_q.start()
    load_k.start()
    load_cache = pltpu.make_async_copy(cache_hbm, cache, w_sem.at[4])
    load_cache.start()
    xall[me, pl.ds(0, GAIN_ROWS), :] = jnp.broadcast_to(gain[...], (GAIN_ROWS, width))
    acc_q[...] = jnp.zeros_like(acc_q)
    acc_k[...] = jnp.zeros_like(acc_k)
    power[...] = jnp.zeros_like(power)
    greet((across, up, down, sib))
    load_x.wait()

    sends = []
    split = GATHER_CHUNKS - 1

    def span(i, half=None):
        low = 0 if i == 0 else GAIN_ROWS + i * chunk
        high = GAIN_ROWS + (i + 1) * chunk
        middle = high - chunk // 2
        if half == 0:
            high = middle
        if half == 1:
            low = middle
        return pl.ds(low, high - low)

    def send(slot, rows, send_sem, there_sem, to):
        ref = xall.at[slot, rows, :]
        sends.append(push(ref, ref, send_sem, there_sem, to))

    def to_sibling(far, step, i):
        kind = far * 4 + step
        send(at(far, step), span(i), sib_send.at[kind, i], sib_sem.at[kind, i], sib)

    def multiply(slot, i):
        rows = pl.ds(i * chunk, chunk)
        wide = xall[slot, pl.ds(GAIN_ROWS + i * chunk, chunk), :].astype(F32)
        weight = xall[slot, pl.ds(0, 1), :].astype(F32)
        square = wide * wide
        part = square[:, 0:HD]
        for k in range(1, width // HD):
            part = part + square[:, k * HD : (k + 1) * HD]
        power[rows, :] += part
        scaled = (wide * weight).astype(BF)
        depth = pl.ds(pl.multiple_of(slot * width, width), width)
        acc_q[rows, :] += jnp.dot(scaled, qw[depth, :], preferred_element_type=F32)
        acc_k[rows, :] += jnp.dot(scaled, kw[depth, :], preferred_element_type=F32)

    def from_sibling(far, step, i):
        kind = far * 4 + step
        slot = at(far, step, 1)
        landed(xall.at[slot, span(i), :], sib_sem.at[kind, i], sib)
        multiply(slot, i)

    def got(far, step, i):
        kind = far * 4 + step
        slot = at(far, step)
        if step == 2 and far == 0:
            landed(xall.at[slot, span(i, 0), :], recv_sem.at[kind, i], down)
            landed(xall.at[slot, span(i, 1), :], recv_sem.at[8, i], up)
        elif i == split and far == 1 and step in (1, 3):
            landed(xall.at[slot, span(i, 0), :], recv_sem.at[kind, i], up)
            landed(xall.at[slot, span(i, 1), :], split_recv.at[step // 2], across)
        else:
            landed(xall.at[slot, span(i), :], recv_sem.at[kind, i], up)

    for i in range(GATHER_CHUNKS):
        send(me, span(i), x_send.at[i], recv_sem.at[4, i], across)
        send(me, span(i), up_send.at[0, i], recv_sem.at[3, i], up)
        send(me, span(i), down_send.at[0, i], recv_sem.at[1, i], down)
        to_sibling(0, 0, i)
    load_p.wait()
    early = kv_out.at[core, pl.ds(0, prefix_rows), :]
    sends.append(push(early, early, kv_send.at[0], kv_recv.at[0], sib))
    load_q.wait()
    load_k.wait()
    load_cache.wait()
    dec_seqs, ctx = cache.shape[0], cache.shape[1]
    contract = (((1,), (1,)), ((), ()))

    def dec_old(k):
        count = dec_seqs * 8
        seq_row = lax.rem(lax.broadcasted_iota(jnp.int32, (count, ctx), 0), 8)
        position = lax.broadcasted_iota(jnp.int32, (count, ctx), 1) + me * ctx
        parts = [dec_q[:, pl.ds((k * 8 + h) * HD, HD)].astype(F32) for h in range(8)]
        query = jnp.concatenate(parts, axis=0).astype(BF)
        found = jnp.full((count, ctx), NEG_BIG, F32)
        for seq in range(dec_seqs):
            score = lax.dot_general(
                query,
                cache[seq, :, pl.ds(2 * k * HD, HD)],
                contract,
                preferred_element_type=F32,
            )
            valid = (position < dec_len[seq]) & (seq_row == seq)
            found = jnp.where(valid, score * LOG_SCALE, found)
        top = jnp.max(found, axis=-1, keepdims=True)
        expo = jnp.where(found > 0.5 * NEG_BIG, jnp.exp2(found - top), 0.0)
        accum = jnp.zeros((count, HD), F32)
        for seq in range(dec_seqs):
            own = jnp.where(seq_row == seq, expo, 0.0).astype(BF)
            accum = accum + jnp.dot(
                own, cache[seq, :, pl.ds((2 * k + 1) * HD, HD)], preferred_element_type=F32
            )
        total = jnp.sum(expo, axis=-1, keepdims=True)
        for part in range(2):
            write_share(old_share.at[2 * k + part], accum, top, total, part * 32)

    def event(name, i):
        if name == "O":
            multiply(me, i)
            return [(0, 0, i)]
        if name == "X":
            got(1, 0, i)
            rows = span(i, 0) if i == split else span(i)
            send(across, rows, up_send.at[1, i], recv_sem.at[7, i], up)
            send(across, rows, down_send.at[1, i], recv_sem.at[5, i], down)
            to_sibling(1, 0, i)
            multiply(across, i)
            return [(1, 0, i)]
        far = 0 if name in ("Z", "F") else 1
        if name in ("Z", "P"):
            got(far, 3, i)
            if far == 0:
                send(at(0, 3), span(i, 0), up_send.at[2, i], recv_sem.at[2, i], up)
                if i == split:
                    send(at(0, 3), span(i, 1), split_send.at[1], split_recv.at[1], across)
            got(far, 1, i)
            if far == 0:
                send(at(0, 1), span(i, 1), down_send.at[2, i], recv_sem.at[8, i], down)
                if i == split:
                    send(at(0, 1), span(i, 1), split_send.at[0], split_recv.at[0], across)
            to_sibling(far, 3, i)
            to_sibling(far, 1, i)
            multiply(at(far, 3), i)
            multiply(at(far, 1), i)
            return [(far, 3, i), (far, 1, i)]
        got(far, 2, i)
        if far == 0:
            send(at(0, 2), span(i), x_send.at[GATHER_CHUNKS + i], recv_sem.at[6, i], across)
        to_sibling(far, 2, i)
        multiply(at(far, 2), i)
        return [(far, 2, i)]

    order = (
        ("O", 0), ("O", 1), ("O", 2), ("O", 3), ("Z", 0), ("Z", 1), ("Z", 2), ("Z", 3),
        ("X", 0), ("X", 1), ("X", 2), ("X", 3), ("F", 0), ("F", 1), ("F", 2), ("F", 3),
        ("P", 0), ("P", 1), ("G", 0), ("P", 2), ("G", 1), ("G", 2), ("P", 3), ("G", 3),
    )
    def settle(i):
        rows = pl.ds(i * chunk, chunk)
        total = jnp.sum(power[rows, :], axis=-1, keepdims=True) / (width * 2 * RING * SIDES)
        factor = lax.rsqrt(total + EPSILON)
        new = pl.ds(prefix_rows + i * chunk, chunk)
        kv_out[core, new, :] = (acc_k[rows, :] * factor).astype(BF)
        ref = kv_out.at[core, new, :]
        sends.append(push(ref, ref, kv_send.at[1 + i], kv_recv.at[1 + i], sib))
        queries = (acc_q[rows, :] * (factor * LOG_SCALE)).astype(BF)
        for h in range(q_out.shape[0]):
            q_out[h, rows, :] = queries[:, h * HD : (h + 1) * HD]

    late = []
    for name, i in order:
        fresh = event(name, i)
        if name in ("Z", "X"):
            dec_old(i + (4 if name == "X" else 0))
        for item in late:
            from_sibling(*item)
        for far, step, k in late:
            if (far, step) == (1, 2):
                settle(k)
        late = fresh
    for item in late:
        from_sibling(*item)
    settle(GATHER_CHUNKS - 1)
    landed(kv_out.at[1 - core, pl.ds(0, prefix_rows), :], kv_recv.at[0], sib)
    for i in range(GATHER_CHUNKS):
        new = pl.ds(prefix_rows + i * chunk, chunk)
        landed(kv_out.at[1 - core, new, :], kv_recv.at[1 + i], sib)
    for copy in sends:
        copy.wait_send()


def gather_multiply(tokens, gain, prefix, query_weight, kv_weight, dec_q, dec_len, cache):
    rows, width = tokens.shape
    shards = 2 * RING * SIDES
    kv_rows = prefix.shape[0] + rows
    vmem = pl.BlockSpec(memory_space=pltpu.VMEM)
    dma = pltpu.SemaphoreType.DMA
    n = GATHER_CHUNKS
    return pl.pallas_call(
        gather_kernel,
        out_shape=(
            jax.ShapeDtypeStruct((query_weight.shape[1] // HD, rows, HD), BF),
            jax.ShapeDtypeStruct((2, kv_rows, HD), BF),
            jax.ShapeDtypeStruct((shards, SHARE_ROWS, HD), F32),
        ),
        in_specs=[vmem, vmem, pl.BlockSpec(memory_space=pltpu.SMEM)]
        + [pl.BlockSpec(memory_space=pltpu.HBM)] * 5,
        out_specs=(vmem,) * 3,
        scratch_shapes=[
            pltpu.VMEM((shards, rows + GAIN_ROWS, width), BF),
            pltpu.VMEM(cache.shape, BF),
            pltpu.VMEM(query_weight.shape, BF),
            pltpu.VMEM(kv_weight.shape, BF),
            pltpu.VMEM((rows, query_weight.shape[1]), F32),
            pltpu.VMEM((rows, HD), F32),
            pltpu.VMEM((rows, HD), F32),
            dma((5,)),
            dma((9, n)),
            dma((8, n)),
            dma((2 * n,)),
            dma((3, n)),
            dma((3, n)),
            dma((8, n)),
            dma((n + 1,)),
            dma((n + 1,)),
            dma((2,)),
            dma((2,)),
        ],
        compiler_params=pltpu.CompilerParams(
            collective_id=1, has_side_effects=True, vmem_limit_bytes=62 * MIB
        ),
        cost_estimate=pl.CostEstimate(
            flops=2 * rows * width * shards * (query_weight.shape[1] + HD),
            bytes_accessed=16 * MIB,
            transcendentals=0,
        ),
        name="gather_multiply",
    )(gain, dec_q, dec_len, tokens, prefix, query_weight, kv_weight, cache)


SCATTER_CHUNKS = 8


def attend_kernel(
    q,
    kv,
    dec_q,
    old_share,
    owner,
    seq_of_page,
    live_len,
    tok_hbm,
    wo_hbm,
    out,
    dec_out,
    wo,
    att,
    mine,
    lend,
    borrowed,
    mid,
    near,
    last,
    far_in,
    tok,
    asked,
    answers,
    shares,
    results,
    w_sem,
    lend_send,
    lend_recv,
    mid_send,
    mid_recv,
    near_send,
    near_recv,
    last_send,
    last_recv,
    far_send,
    far_recv,
    ask_send,
    ask_recv,
    answer_send,
    answer_recv,
    share_send,
    share_recv,
    done_send,
    done_recv,
):
    side, ring, core = here()
    rows_all, width = out.shape
    chunk = rows_all // SCATTER_CHUNKS
    half = chunk // 2
    old = kv.shape[1] - rows_all
    n = SCATTER_CHUNKS

    def at(far, step, other=0):
        return shard_at(side, ring, core, far, step, other)

    across, sib, up, down = at(1, 0), at(0, 0, 1), at(0, 1), at(0, 3)
    load = pltpu.make_async_copy(wo_hbm, wo, w_sem.at[0])
    load.start()
    load_tok = pltpu.make_async_copy(tok_hbm, tok, w_sem.at[1])
    load_tok.start()
    shard = lax.axis_index("tp")
    group = lax.axis_index("group")
    shards = 2 * RING * SIDES
    groups = lax.axis_size("group")
    dec_seqs = dec_out.shape[0]
    barrier = pltpu.get_barrier_semaphore()

    def greet_shard(d, carry):
        pl.semaphore_signal(
            barrier, inc=1, device_id={"tp": lax.rem(shard + d, shards)}, device_id_type=MESH
        )
        return carry

    def greet_group(d, carry):
        pl.semaphore_signal(
            barrier, inc=1, device_id={"group": lax.rem(group + d, groups)}, device_id_type=MESH
        )
        return carry

    lax.fori_loop(1, shards, greet_shard, 0)
    lax.fori_loop(1, groups, greet_group, 0)

    def copy_to(src, dst, send_sem, recv_sem, to):
        return pltpu.make_async_remote_copy(
            src_ref=src,
            dst_ref=dst,
            send_sem=send_sem,
            recv_sem=recv_sem,
            device_id=to,
            device_id_type=MESH,
        )

    contract = (((1,), (1,)), ((), ()))
    per = 4 * dec_seqs

    def ask_copy(d):
        to = lax.rem(group + d, groups)
        return copy_to(
            asked.at[group], asked.at[group], ask_send.at[d], ask_recv.at[d], {"group": to}
        )

    def answer_copy(d):
        to = lax.rem(group + d, groups)
        return copy_to(
            answers.at[to],
            shares.at[shards + group],
            answer_send.at[d],
            answer_recv.at[d],
            {"group": to},
        )

    def share_copy(d):
        to = lax.rem(shard + d, shards)
        return copy_to(
            old_share.at[to], shares.at[shard], share_send.at[d], share_recv.at[d], {"tp": to}
        )

    def done_copy(d):
        to = lax.rem(shard + d, shards)
        return copy_to(
            results.at[shard], results.at[shard], done_send.at[d], done_recv.at[d], {"tp": to}
        )

    def each(count, act):
        def body(d, carry):
            act(d)
            return carry

        lax.fori_loop(1, count, body, 0)

    def arrive(count, of, axis, place, send_sem, recv_sem):
        def take(d):
            frm = lax.rem(of + count - d, count)
            ref = place(frm)
            copy_to(ref, ref, send_sem.at[d], recv_sem.at[d], {axis: frm}).wait_recv()

        each(count, take)

    def dec_begin():
        parts = []
        for h in range(4):
            cols = pl.ds(pl.multiple_of(shard * width + h * HD, HD), HD)
            parts.append(dec_q[:, cols].astype(F32))
        asked[group] = jnp.concatenate(parts, axis=0).astype(BF)
        each(groups, lambda d: ask_copy(d).start())
        shares[shard] = old_share[shard]
        each(shards, lambda d: share_copy(d).start())

    def dec_answer():
        arrive(groups, group, "group", lambda frm: asked.at[frm], ask_send, ask_recv)
        count = owner.shape[1]
        old_rows = kv.shape[1] - rows_all
        both = jnp.concatenate(
            [
                jnp.broadcast_to(owner[...], (8, count)),
                jnp.broadcast_to(seq_of_page[...], (8, count)),
            ],
            axis=0,
        ).astype(F32)
        page = lax.broadcasted_iota(jnp.int32, (count, rows_all), 0)
        page_of = lax.broadcasted_iota(jnp.int32, (count, rows_all), 1) // PAGE
        spread = jnp.where(page == page_of, 1.0, 0.0).astype(BF)
        by_token = jnp.dot(both.astype(BF), spread, preferred_element_type=F32).astype(jnp.int32)
        token = lax.broadcasted_iota(jnp.int32, (1, rows_all), 1)
        code = by_token[0:1, :] // shards * dec_seqs + by_token[8:9, :]
        code = jnp.where(token < live_len[0], code, -1)
        row = lax.broadcasted_iota(jnp.int32, (groups * per, rows_all), 0)
        held = code == row // per * dec_seqs + lax.rem(row, dec_seqs)
        query = asked[...].reshape(groups * per, HD)
        score = lax.dot_general(
            query, kv[0, pl.ds(old_rows, rows_all), :], contract, preferred_element_type=F32
        )
        score = jnp.where(held, score * LOG_SCALE, NEG_BIG)
        top = jnp.max(score, axis=-1, keepdims=True)
        expo = jnp.where(held, jnp.exp2(score - top), 0.0)
        total = jnp.sum(expo, axis=-1, keepdims=True)
        accum = jnp.dot(
            expo.astype(BF), kv[1, pl.ds(old_rows, rows_all), :], preferred_element_type=F32
        )
        for g in range(answers.shape[0]):
            write_share(answers.at[g], accum, top, total, g * per)
        shares[shards + group] = answers[group]
        each(groups, lambda d: answer_copy(d).start())

    def dec_combine():
        arrive(shards, shard, "tp", lambda frm: shares.at[frm], share_send, share_recv)
        arrive(
            groups, group, "group", lambda frm: shares.at[shards + frm], answer_send, answer_recv
        )
        stat = shares[:, pl.ds(32, 8), :]
        lane = lax.broadcasted_iota(jnp.int32, stat.shape, 2) // 16
        parts = []
        for h in range(4):
            top = jnp.max(jnp.where(lane == h, stat, NEG_BIG), axis=-1, keepdims=True)
            total = jnp.max(jnp.where(lane == 4 + h, stat, 0.0), axis=-1, keepdims=True)
            factor = jnp.exp2(top - jnp.max(top, axis=0, keepdims=True))
            whole = jnp.sum(factor * total, axis=0)
            accum = jnp.sum(factor * shares[:, pl.ds(h * 8, 8), :], axis=0)
            parts.append(accum / whole)
        results[shard] = jnp.concatenate(parts, axis=0).astype(BF)
        each(shards, lambda d: done_copy(d).start())

    def dec_end():
        arrive(shards, shard, "tp", lambda frm: results.at[frm], done_send, done_recv)
        for t in range(results.shape[0]):
            block = results[t].astype(F32)
            for h in range(4):
                dec_out[:, (t * 4 + h) * HD : (t * 4 + h + 1) * HD] = block[
                    h * 8 : h * 8 + 8
                ].astype(BF)
        for copy in (share_copy, done_copy):
            each(shards, lambda d, copy=copy: copy(d).wait_send())
        for copy in (ask_copy, answer_copy):
            each(groups, lambda d, copy=copy: copy(d).wait_send())

    def rows_of(j):
        return pl.ds(pl.multiple_of(j * chunk, chunk), chunk)

    def half_of(j, k):
        return pl.ds(pl.multiple_of(j * chunk + k * half, half), half)

    def attend(j, plain, edge):
        rows = rows_of(j)
        count = width // HD
        query = q[:, rows, :].reshape(count * chunk, HD)
        row = lax.rem(lax.broadcasted_iota(jnp.int32, (count * chunk, edge), 0), chunk)
        column = lax.broadcasted_iota(jnp.int32, (count * chunk, edge), 1)
        seen = column + plain <= row + old + j * chunk
        first = lax.dot_general(
            query, kv[0, pl.ds(0, plain), :], contract, preferred_element_type=F32
        )
        second = lax.dot_general(
            query, kv[0, pl.ds(plain, edge), :], contract, preferred_element_type=F32
        )
        second = jnp.where(seen, second, NEG_BIG)
        top = jnp.maximum(
            jnp.max(first, axis=-1, keepdims=True), jnp.max(second, axis=-1, keepdims=True)
        )
        first = jnp.exp2(first - top)
        second = jnp.exp2(second - top)
        total = jnp.sum(first, axis=-1, keepdims=True) + jnp.sum(second, axis=-1, keepdims=True)
        value = jnp.dot(
            first.astype(BF), kv[1, pl.ds(0, plain), :], preferred_element_type=F32
        ) + jnp.dot(second.astype(BF), kv[1, pl.ds(plain, edge), :], preferred_element_type=F32)
        value = value / total
        for h in range(count):
            att[:, h * HD : (h + 1) * HD] = value[h * chunk : (h + 1) * chunk].astype(BF)

    def attention(j):
        for pair in range(n // 2):

            @pl.when(j // 2 == pair)
            def _(pair=pair):
                attend(j, old + 2 * pair * chunk, 2 * chunk)

    def term(far, step, other):
        slot = at(far, step, other)
        cols = pl.ds(pl.multiple_of(slot * width, width), width)
        return jnp.dot(att[...], wo[:, cols], preferred_element_type=F32)

    def add_into(dst, src):
        dst[...] = (dst[...].astype(F32) + src[...].astype(F32)).astype(BF)

    def lend_copy(kind, j):
        rows = rows_of(j)
        return pltpu.make_async_remote_copy(
            src_ref=lend.at[kind, rows, :],
            dst_ref=borrowed.at[kind, rows, :],
            send_sem=lend_send.at[kind, j],
            recv_sem=lend_recv.at[kind, j],
            device_id={"tp": sib},
            device_id_type=MESH,
        )

    def mid_copy(way, j):
        rows = half_of(j, way)
        return pltpu.make_async_remote_copy(
            src_ref=mine.at[2, rows, :],
            dst_ref=mid.at[rows, :],
            send_sem=mid_send.at[way, j],
            recv_sem=mid_recv.at[way, j],
            device_id={"tp": down if way else up},
            device_id_type=MESH,
        )

    def far_copy(j):
        rows = rows_of(j)
        return pltpu.make_async_remote_copy(
            src_ref=mine.at[6, rows, :],
            dst_ref=far_in.at[rows, :],
            send_sem=far_send.at[j],
            recv_sem=far_recv.at[j],
            device_id={"tp": across},
            device_id_type=MESH,
        )

    def near_copy(far, way, k, j):
        rows = half_of(j, k)
        return pltpu.make_async_remote_copy(
            src_ref=mine.at[far * 4 + (3 if way else 1), rows, :],
            dst_ref=near.at[far * 2 + way, rows, :],
            send_sem=near_send.at[far * 4 + way * 2 + k, j],
            recv_sem=near_recv.at[far * 4 + way * 2 + k, j],
            device_id={"tp": down if way else up},
            device_id_type=MESH,
        )

    def last_copy(j):
        rows = rows_of(j)
        return pltpu.make_async_remote_copy(
            src_ref=mine.at[4, rows, :],
            dst_ref=last.at[rows, :],
            send_sem=last_send.at[j],
            recv_sem=last_recv.at[j],
            device_id={"tp": across},
            device_id_type=MESH,
        )

    kinds = ((1, 2), (1, 1), (1, 3), (0, 2), (0, 1), (0, 3), (1, 0), (0, 0))
    ahead = 4

    def produce(j):
        rows = rows_of(j)

        def offer(far, step):
            kind = far * 4 + step
            lend[kind, rows, :] = term(far, step, 1).astype(BF)
            lend_copy(kind, j).start()

        for far, step in kinds[:ahead]:
            offer(far, step)
        for k, (far, step) in enumerate(kinds):
            if k + ahead < len(kinds):
                offer(*kinds[k + ahead])
            kind = far * 4 + step
            own = term(far, step, 0)
            lend_copy(kind, j).wait_recv()
            mine[kind, rows, :] = (own + borrowed[kind, rows, :].astype(F32)).astype(BF)
            if (far, step) == (1, 2):
                far_copy(j).start()
            if step == 1:
                near_copy(far, 0, 1, j).start()
                if far:
                    near_copy(far, 0, 0, j).start()
            if step == 3:
                near_copy(far, 1, 0, j).start()
                if far:
                    near_copy(far, 1, 1, j).start()

    def pass_on(j):
        far_copy(j).wait_recv()
        rows = rows_of(j)
        add_into(mine.at[2, rows, :], far_in.at[rows, :])
        mid_copy(0, j).start()
        mid_copy(1, j).start()

    def relay(j):
        for way in (0, 1):
            mid_copy(way, j).wait_recv()
            rows = half_of(j, way)
            add_into(mine.at[3 if way else 1, rows, :], mid.at[rows, :])
            near_copy(0, way, way, j).start()

    def near_wait(far, j):
        for way in (0, 1):
            for k in (0, 1):
                near_copy(far, way, k, j).wait_recv()

    def cross(j):
        near_wait(1, j)
        rows = rows_of(j)
        mine[4, rows, :] = (
            mine[4, rows, :].astype(F32) + near[2, rows, :].astype(F32) + near[3, rows, :].astype(F32)
        ).astype(BF)
        last_copy(j).start()

    def finish(j):
        near_wait(0, j)
        last_copy(j).wait_recv()
        rows = rows_of(j)
        out[rows, :] = (
            tok[rows, :].astype(F32)
            + (
                mine[0, rows, :].astype(F32)
                + near[0, rows, :].astype(F32)
                + near[1, rows, :].astype(F32)
                + last[rows, :].astype(F32)
            )
        ).astype(BF)

    attend(0, old, 2 * chunk)
    pl.semaphore_wait(barrier, shards + groups - 2)

    def turn(j, carry):
        @pl.when((j >= 1) & (j < n))
        def _():
            attention(j)

        @pl.when(j == 0)
        def _():
            load.wait()
            load_tok.wait()

        @pl.when(j < n)
        def _():
            produce(j)

        @pl.when((j >= 1) & (j < n + 1))
        def _():
            pass_on(j - 1)

        @pl.when((j >= 3) & (j < n + 3))
        def _():
            relay(j - 3)

        @pl.when((j >= 4) & (j < n + 4))
        def _():
            cross(j - 4)

        @pl.when(j >= 5)
        def _():
            finish(j - 5)

        @pl.when(j == 0)
        def _():
            dec_begin()

        @pl.when(j == 2)
        def _():
            dec_answer()

        @pl.when(j == 5)
        def _():
            dec_combine()

        @pl.when(j == 8)
        def _():
            dec_end()

        return carry

    lax.fori_loop(0, n + 5, turn, 0)

    def drain(j, carry):
        for kind in range(8):
            lend_copy(kind, j).wait_send()
        for far in (0, 1):
            for way in (0, 1):
                for k in (0, 1):
                    near_copy(far, way, k, j).wait_send()
        last_copy(j).wait_send()
        far_copy(j).wait_send()
        mid_copy(0, j).wait_send()
        mid_copy(1, j).wait_send()
        return carry

    lax.fori_loop(0, n, drain, 0)


def attend_scatter(
    tokens, queries, kv, dec_q, old_share, owner, seq_of_page, live_len, out_weight, groups
):
    rows, width = tokens.shape
    vmem = pl.BlockSpec(memory_space=pltpu.VMEM)
    dma = pltpu.SemaphoreType.DMA
    n = SCATTER_CHUNKS
    seqs = dec_q.shape[0]
    shards = 2 * RING * SIDES
    return pl.pallas_call(
        attend_kernel,
        out_shape=(
            jax.ShapeDtypeStruct((rows, width), BF),
            jax.ShapeDtypeStruct((seqs, HEADS * HD), BF),
        ),
        in_specs=[
            vmem,
            vmem,
            vmem,
            vmem,
            vmem,
            vmem,
            pl.BlockSpec(memory_space=pltpu.SMEM),
            pl.BlockSpec(memory_space=pltpu.HBM),
            pl.BlockSpec(memory_space=pltpu.HBM),
        ],
        out_specs=(vmem, vmem),
        scratch_shapes=[
            pltpu.VMEM(out_weight.shape, BF),
            pltpu.VMEM((rows // n, width), BF),
            pltpu.VMEM((8, rows, width), BF),
            pltpu.VMEM((8, rows, width), BF),
            pltpu.VMEM((8, rows, width), BF),
            pltpu.VMEM((rows, width), BF),
            pltpu.VMEM((4, rows, width), BF),
            pltpu.VMEM((rows, width), BF),
            pltpu.VMEM((rows, width), BF),
            pltpu.VMEM((rows, width), BF),
            pltpu.VMEM((groups, 4 * seqs, HD), BF),
            pltpu.VMEM((groups, SHARE_ROWS, HD), F32),
            pltpu.VMEM((shards + groups, SHARE_ROWS, HD), F32),
            pltpu.VMEM((shards, 4 * seqs, HD), BF),
            dma((2,)),
            dma((8, n)),
            dma((8, n)),
            dma((2, n)),
            dma((2, n)),
            dma((8, n)),
            dma((8, n)),
            dma((n,)),
            dma((n,)),
            dma((n,)),
            dma((n,)),
            dma((groups,)),
            dma((groups,)),
            dma((groups,)),
            dma((groups,)),
            dma((shards,)),
            dma((shards,)),
            dma((shards,)),
            dma((shards,)),
        ],
        compiler_params=pltpu.CompilerParams(
            collective_id=2, has_side_effects=True, vmem_limit_bytes=62 * MIB
        ),
        cost_estimate=pl.CostEstimate(
            flops=2 * rows * width * out_weight.shape[1] * 2,
            bytes_accessed=12 * MIB,
            transcendentals=4 * rows * kv.shape[1],
        ),
        name="attend_scatter",
    )(queries, kv, dec_q, old_share, owner, seq_of_page, live_len, tokens, out_weight)


def hand_on_kernel(hidden, dec, hidden_out, dec_out, buffer, dec_buffer, sem_in, sem_out):
    part = hidden.shape[0] // 4
    moves = [(dec, dec_buffer, dec_out)]
    for k in range(4):
        rows = pl.ds(k * part, part)
        moves.append((hidden.at[rows], buffer.at[rows], hidden_out.at[rows]))
    loads = [pltpu.make_async_copy(a, b, sem_in.at[k]) for k, (a, b, _) in enumerate(moves)]
    stores = [pltpu.make_async_copy(b, c, sem_out.at[k]) for k, (_, b, c) in enumerate(moves)]
    for load in loads:
        load.start()
    for load, store in zip(loads, stores):
        load.wait()
        store.start()
    for store in stores:
        store.wait()


def hand_on(hidden, dec):
    hbm = pl.BlockSpec(memory_space=pltpu.HBM)
    return pl.pallas_call(
        hand_on_kernel,
        out_shape=(
            jax.ShapeDtypeStruct(hidden.shape, hidden.dtype),
            jax.ShapeDtypeStruct(dec.shape, dec.dtype),
        ),
        in_specs=[hbm, hbm],
        out_specs=(hbm, hbm),
        scratch_shapes=[
            pltpu.VMEM(hidden.shape, hidden.dtype),
            pltpu.VMEM(dec.shape, dec.dtype),
            pltpu.SemaphoreType.DMA((5,)),
            pltpu.SemaphoreType.DMA((5,)),
        ],
        name="hand_on",
    )(hidden, dec)


def per_device(
    tokens,
    norm_gain,
    query_weight,
    kv_weight,
    out_weight,
    prefix_cache,
    prompt_len,
    page_owner,
    page_seq,
    dec_queries,
    dec_cache,
    dec_len,
):
    queries, kv_both, old_share = gather_multiply(
        tokens, norm_gain, prefix_cache, query_weight, kv_weight, dec_queries, dec_len, dec_cache
    )
    hidden_out, dec_out = attend_scatter(
        tokens,
        queries,
        kv_both,
        dec_queries,
        old_share,
        page_owner.reshape(1, -1),
        page_seq.reshape(1, -1),
        prompt_len,
        out_weight,
        lax.axis_size("group"),
    )
    return hand_on(hidden_out, dec_out)


def solution(mesh):
    return jax.shard_map(
        per_device,
        mesh=mesh,
        in_specs=(
            P("group", "tp"),
            P(None, "tp"),
            P(None, "tp"),
            P(None, "tp"),
            P("tp", None),
            P("group", "tp"),
            P("group"),
            P("group", None),
            P("group"),
            P("group", None),
            P("group", "tp", None),
            P("group"),
        ),
        out_specs=(P("group", "tp"), P("group", None)),
        check_vma=False,
    )
```
